32 devices in a mesh: ctx: 8 (over z, y), kvh: 4 (over x, core).
Axes of the slice: x: 2, y: 2, z: 4, core: 2. Of those that a mesh axis runs over, the one named last changes fastest.
Arguments:
- queries: bfloat16 [64, 64, 4, 1024], P('ctx', None, 'kvh'), may hold values from -92 to 92
- resp_keys: bfloat16 [64, 64, 4, 128], P('ctx', None, 'kvh'), may hold values from -6 to 6
- resp_values: bfloat16 [64, 64, 4, 128], P('ctx', None, 'kvh'), may hold values from -6 to 6
- prefix_keys: bfloat16 [32768, 4, 128], P('ctx', 'kvh'), may hold values from -6 to 6
- prefix_values: bfloat16 [32768, 4, 128], P('ctx', 'kvh'), may hold values from -6 to 6
- prefix_len: int32 [4], replicated, may hold values from 2048 to 8192, as said below
- prompt_of: int32 [64], replicated, may hold values from 0 to 3, as said below
- out_weight: bfloat16 [4096, 8192], P('kvh', 'ctx'), may hold values from -0.09375 to 0.09375
Outputs:
- attended: bfloat16 [64, 64, 4, 1024], P('ctx', None, 'kvh')
- projected: bfloat16 [4096, 8192], P('ctx', 'kvh')
The draws below stay inside these ranges and needn't reach their ends.
Inputs may be any that keep to these rules, and one draw needn't show every extreme that they name: `prefix_len`: every prompt's length lies in the range and one prompt has exactly 8192. `prompt_of`: every prompt is named by 16 responses; the 8 responses of one index of ctx name each prompt at most 2 times, and some prompt exactly 2 times on every index.
All inputs are finite; a program needn't handle non-finite values.
Results may differ from the reference program's by a relative error of at most 0.038.
Values may be sent and summed in bfloat16 or wider, within the bound.
No kernel may reach another device: no remote copies, remote signals or barrier semaphores. Data moves between devices by JAX's collectives and lax.ppermute only.
A program may use at most 192 MiB of HBM per device.

```python
import math
import jax
import jax.numpy as jnp
from jax import lax

D = 8192
HQ = 8
HD = 128
P_SIZE = 4
RLEN = 64
LMAX = 8192
KVH = 4
R = 64
RESP_DEV = 8
SLOTS_DEV = 4096


def draw_resp_keys(key, part):
    key = jax.random.fold_in(key, 3)
    drawn = jax.random.normal(key, (R, RLEN, KVH, HD), jnp.float32) * 1.5
    return jnp.clip(drawn, -6.0, 6.0).astype(jnp.bfloat16)


def draw_queries(key, part):
    key = jax.random.fold_in(key, 4)
    drawn = jax.random.normal(key, (R, RLEN, KVH, HQ * HD), jnp.float32)
    return jnp.clip(drawn, -5.0, 5.0).astype(jnp.bfloat16)


def draw_prefix_len(key, part):
    key = jax.random.fold_in(key, 7)
    first_key, second_key = jax.random.split(key)
    lengths = jax.random.randint(first_key, (P_SIZE,), LMAX // 4, LMAX + 1)
    longest = jax.random.randint(second_key, (), 0, P_SIZE)
    return jnp.where(jnp.arange(P_SIZE) == longest, LMAX, lengths).astype(jnp.int32)


def draw_prompt_of(key, part):
    key = jax.random.fold_in(key, 5)
    first_key, second_key = jax.random.split(key)
    relabel = jax.random.permutation(first_key, P_SIZE)
    device_count = R // RESP_DEV

    def one_row(row_key):
        return jax.random.permutation(row_key, RESP_DEV)
    within = jax.vmap(one_row)(jax.random.split(second_key, device_count))
    devices = jnp.arange(device_count)[:, None]
    slot_prompt = (devices * RESP_DEV + within) % P_SIZE
    return relabel[slot_prompt].reshape(R).astype(jnp.int32)


def steps_of(own_key, dims, cuts, least, largest):
    level = 1.0
    for axis_at, blocks in cuts:
        draws = jax.random.uniform(jax.random.fold_in(jax.random.fold_in(own_key, 6), axis_at), (blocks,), jnp.float32, least / len(cuts), largest / len(cuts))
        level = level * jnp.repeat(jnp.exp(draws), dims[axis_at] // blocks).reshape((-1,) + (1,) * (len(dims) - 1 - axis_at))
    return level


def noise(key, shape, width, limit, pieces=(), held_as=jnp.bfloat16):
    values = width * jax.random.normal(key, shape, jnp.float32)
    if pieces:
        values = values * steps_of(key, shape, pieces, -0.22, 0.18)
    return jnp.clip(values, -limit, limit).astype(held_as)


def setup_inputs(seed: int = 0) -> dict:
    splits = jax.random.split(jax.random.key(seed), 9)
    return {
        "queries": draw_queries(jax.random.fold_in(splits[8], 71), 0),
        "resp_keys": draw_resp_keys(jax.random.fold_in(splits[8], 71), 0),
        "resp_values": noise(splits[2], (R, RLEN, KVH, HD), 1.0, 6.0, ((0, 8), (2, 4))),
        "prefix_keys": noise(splits[3], (P_SIZE * LMAX, KVH, HD), 1.0, 6.0, ((0, 8), (1, 4))),
        "prefix_values": noise(splits[4], (P_SIZE * LMAX, KVH, HD), 1.0, 6.0, ((0, 8), (1, 4))),
        "prefix_len": draw_prefix_len(jax.random.fold_in(splits[8], 71), 0),
        "prompt_of": draw_prompt_of(jax.random.fold_in(splits[8], 71), 0),
        "out_weight": noise(splits[7], (KVH * HQ * HD, D), (KVH * HQ * HD) ** -0.5, 0.09375, ((0, 4), (1, 8))),
    }


MASKED = -1e+30

def partial_block(query_rows, keys, values, live):
    scores = jnp.einsum('thd,sd->ths', query_rows.astype(jnp.float32), keys.astype(jnp.float32)) * (1.0 / math.sqrt(HD))
    scores = jnp.where(live, scores, MASKED)
    peak = lax.optimization_barrier(jnp.max(scores, axis=-1))
    weights = jnp.where(live, jnp.exp(scores - peak[..., None]), 0.0)
    totals = lax.optimization_barrier(jnp.sum(weights, axis=-1))
    rounded = lax.optimization_barrier(weights.astype(jnp.bfloat16)).astype(jnp.float32)
    mixed = jnp.einsum('ths,sd->thd', rounded, values.astype(jnp.float32))
    return (mixed, peak, totals)

def one_response(response, queries, resp_keys, resp_values, prefix_keys, prefix_values, prefix_len, prompt_of):
    prompt = prompt_of[response]
    start = (prompt * LMAX).astype(jnp.int32)
    near_keys = lax.dynamic_slice_in_dim(prefix_keys, start, LMAX, 0)
    near_values = lax.dynamic_slice_in_dim(prefix_values, start, LMAX, 0)
    holders = LMAX // SLOTS_DEV
    positions = jnp.arange(LMAX, dtype=jnp.int32).reshape(holders, SLOTS_DEV)
    live_slots = positions < prefix_len[prompt]
    causal = jnp.arange(RLEN)[:, None] >= jnp.arange(RLEN)[None, :]

    def per_head(query_group, own_keys, own_values, group_keys, group_values):
        query_rows = query_group.reshape(RLEN, HQ, HD)
        own_mixed, own_peak, own_totals = partial_block(query_rows, own_keys, own_values, causal[:, None, :])

        def per_block(block_keys, block_values, block_live):
            mixed, peak, totals = partial_block(query_rows, block_keys, block_values, block_live[None, None, :])
            mixed = lax.optimization_barrier(mixed.astype(jnp.bfloat16)).astype(jnp.float32)
            return (mixed, peak, totals)
        far_mixed, far_peak, far_totals = jax.vmap(per_block)(group_keys.reshape(holders, SLOTS_DEV, HD), group_values.reshape(holders, SLOTS_DEV, HD), live_slots)
        highest = jnp.maximum(own_peak, lax.optimization_barrier(jnp.max(far_peak, axis=0)))
        own_scale = jnp.exp(own_peak - highest)
        far_scale = jnp.exp(far_peak - highest[None])
        numerator = own_scale[..., None] * own_mixed + lax.optimization_barrier(jnp.sum(far_scale[..., None] * far_mixed, axis=0))
        denominator = own_scale * own_totals + lax.optimization_barrier(jnp.sum(far_scale * far_totals, axis=0))
        return (numerator / denominator[..., None]).astype(jnp.bfloat16).reshape(RLEN, HQ * HD)
    return jax.vmap(per_head, in_axes=(1, 1, 1, 1, 1), out_axes=1)(queries[response], resp_keys[response], resp_values[response], near_keys, near_values)

def reference(queries, resp_keys, resp_values, prefix_keys, prefix_values, prefix_len, prompt_of, out_weight):

    def step_fn(response):
        return one_response(response, queries, resp_keys, resp_values, prefix_keys, prefix_values, prefix_len, prompt_of)
    attended = lax.map(step_fn, jnp.arange(R, dtype=jnp.int32))
    flat_rows = attended.reshape(R * RLEN, KVH * HQ * HD)
    projected = jnp.dot(flat_rows, out_weight, preferred_element_type=jnp.float32).astype(jnp.bfloat16)
    return (attended, projected)
```

```python
import functools
import math

import jax
import jax.numpy as jnp
from jax import lax
from jax.experimental import pallas as pl
from jax.experimental.pallas import tpu as pltpu
from jax.sharding import PartitionSpec as P

MASKED = -1e30
LOG2E = math.log2(math.e)
LANES = 128
PART_ROWS = 16
MAX_TILE = 1024
MAX_BLOCK = 512


def nt_dot(a, b):
    return lax.dot_general(a, b, (((1,), (1,)), ((), ())), preferred_element_type=jnp.float32)


def after(x, *others):
    return lax.optimization_barrier((x, *others))[0]


def pack_kernel(capacity, holders, slots, prompt_ref, len_ref, q_ref, *refs):
    *chunk_refs, meta_ref = refs
    responses, tokens, _ = q_ref.shape
    position = lax.axis_index("ctx")
    mine, holder = position // holders, position % holders
    named = [prompt_ref[position * responses + r] for r in range(responses)]
    ranks = []
    for r in range(responses):
        rank = jnp.int32(0)
        for before in range(r):
            rank += (named[before] == named[r]).astype(jnp.int32)
        ranks.append(rank)
    places = len(chunk_refs) * capacity
    for i, chunk_ref in enumerate(chunk_refs):
        for slot in range(capacity):
            chosen, present = jnp.int32(0), jnp.int32(0)
            for r in range(responses):
                hit = ((named[r] == mine ^ i) & (ranks[r] == slot)).astype(jnp.int32)
                chosen += hit * r
                present += hit
            meta_ref[i * capacity + slot] = chosen
            meta_ref[places + i * capacity + slot] = present
            rows = slice(slot * tokens, (slot + 1) * tokens)
            chunk_ref[rows, :] = q_ref[chosen]

            @pl.when(present == 0)
            def _(chunk_ref=chunk_ref, rows=rows):
                chunk_ref[rows, :] = jnp.zeros_like(chunk_ref[rows, :])

    length = len_ref[mine]
    for j in range(holders):
        place = (holder + j) % holders
        meta_ref[2 * places + j] = jnp.clip(length - place * slots, 0, slots)
        meta_ref[2 * places + holders + j] = place


def pack(prompt_of, prefix_len, q, capacity, holders, slots):
    _, tokens, width = q.shape
    prompts = prefix_len.shape[0]
    smem = pl.BlockSpec(memory_space=pltpu.SMEM)
    vmem = pl.BlockSpec(memory_space=pltpu.VMEM)
    *chunks, meta = pl.pallas_call(
        functools.partial(pack_kernel, capacity, holders, slots),
        out_shape=[jax.ShapeDtypeStruct((capacity * tokens, width), q.dtype)] * prompts
        + [jax.ShapeDtypeStruct((2 * (prompts * capacity + holders),), jnp.int32)],
        in_specs=[smem, smem, vmem],
        out_specs=[vmem] * prompts + [smem],
        cost_estimate=pl.CostEstimate(flops=0, bytes_accessed=4 * q.size, transcendentals=0),
        name="pack",
    )(prompt_of, prefix_len, q)
    return chunks, meta


def attend_kernel(count, first, last, shard, places, meta_ref, *refs):
    q_refs, (k_ref, v_ref, *refs) = refs[:count], refs[count:]
    if not first:
        prev_o_ref, prev_lse_ref, *refs = refs
    if last:
        out_refs, refs = refs[:count], refs[count:]
    else:
        o_ref, lse_ref, *refs = refs
    qext, kext, vext, score_a, score_b = refs
    tokens = q_refs[0].shape[0]
    slots, hd = k_ref.shape
    heads = q_refs[0].shape[1] // hd
    scale = LOG2E / math.sqrt(hd)
    tiles, row_block, key_tile = score_a.shape
    per_chunk = heads * tokens // row_block
    live = meta_ref[2 * places + shard]

    @pl.when(live == slots)
    def _():
        for t in range(tiles):
            at = slice(t * key_tile, (t + 1) * key_tile)
            keys = k_ref[at, :]
            kext[at, :hd] = keys
            kext[at, hd:] = keys
            vext[at, :hd] = v_ref[at, :]
            vext[at, hd:] = jnp.ones((key_tile, hd), jnp.bfloat16)

    @pl.when(live != slots)
    def _():
        def prepare(step, carry):
            at = pl.ds(pl.multiple_of(step * key_tile, key_tile), key_tile)
            alive = step * key_tile + lax.broadcasted_iota(jnp.int32, (key_tile, hd), 0) < live
            keys = jnp.where(alive, k_ref[at, :].astype(jnp.float32), k_ref[0:1, :].astype(jnp.float32))
            keys = keys.astype(jnp.bfloat16)
            kext[at, :hd] = keys
            kext[at, hd:] = keys
            vext[at, :hd] = jnp.where(alive, v_ref[at, :].astype(jnp.float32), 0.0).astype(jnp.bfloat16)
            vext[at, hd:] = jnp.where(alive, 1.0, 0.0).astype(jnp.bfloat16)
            return carry

        lax.fori_loop(0, tiles, prepare, 0)

    for c, q_ref in enumerate(q_refs):
        for h in range(heads):
            rows = slice((c * heads + h) * tokens, (c * heads + h + 1) * tokens)
            x = q_ref[:, h * hd : (h + 1) * hd].astype(jnp.float32) * scale
            high = x.astype(jnp.bfloat16)
            qext[rows, :hd] = high
            qext[rows, hd:] = (x - high.astype(jnp.float32)).astype(jnp.bfloat16)

    low = jnp.full((row_block, LANES), MASKED, jnp.float32)

    def rows_of(b):
        if isinstance(b, int):
            return slice(b * row_block, (b + 1) * row_block)
        return pl.ds(pl.multiple_of(b * row_block, row_block), row_block)

    def score_tile(b, t, into, peak):
        s = nt_dot(qext[rows_of(b), :], kext[t * key_tile : (t + 1) * key_tile, :])
        into[t] = s
        for j in range(key_tile // LANES):
            peak = jnp.maximum(peak, s[:, j * LANES : (j + 1) * LANES])
        return peak

    def one_block(b, scores, peak, following, into):
        m = jnp.max(peak, axis=1, keepdims=True)
        peak = low
        acc = jnp.zeros((row_block, 2 * hd), jnp.float32)
        for t in range(tiles):
            if following is not None:
                peak = score_tile(following, t, into, peak)
            w = jnp.exp2(scores[t] - m).astype(jnp.bfloat16)
            acc = acc + jnp.dot(
                w, vext[t * key_tile : (t + 1) * key_tile, :], preferred_element_type=jnp.float32
            )
        total = acc[:, hd:]
        some = total > 0.0
        safe = jnp.where(some, total, 1.0)
        o = acc[:, :hd] / safe
        lse = jnp.where(some, m + jnp.log2(safe), MASKED)
        rows = rows_of(b)
        if not first:
            before = prev_lse_ref[rows, :]
            top = jnp.maximum(before, lse)
            w_before = jnp.exp2(before - top)
            w_now = jnp.exp2(lse - top)
            both = w_before + w_now
            o = (w_before * prev_o_ref[rows, :] + w_now * o) / both
            lse = top + jnp.log2(both)
        if not last:
            o_ref[rows, :] = o
            lse_ref[rows, :] = lse
            return peak
        out_ref = out_refs[b // per_chunk]
        for j in range(row_block // tokens):
            h = (b % per_chunk) * (row_block // tokens) + j
            part = slice(j * tokens, (j + 1) * tokens)
            lanes = slice(h * hd, (h + 1) * hd)
            out_ref[:tokens, lanes] = o[part].astype(jnp.bfloat16)
            flat = lse[part].T[:PART_ROWS, :]
            high = flat.astype(jnp.bfloat16).astype(jnp.float32)
            middle = (flat - high).astype(jnp.bfloat16).astype(jnp.float32)
            row = lax.broadcasted_iota(jnp.int32, flat.shape, 0)
            out_ref[tokens:, lanes] = jnp.where(
                row == 0, high, jnp.where(row == 1, middle, jnp.where(row == 2, flat - high - middle, 0.0))
            ).astype(jnp.bfloat16)
        return peak

    blocks = count * per_chunk
    peak = low
    for t in range(tiles):
        peak = score_tile(0, t, score_a, peak)
    looped = 0
    if not last and per_chunk == 2 and count > 1:
        looped = blocks - 2

        def pair(i, peak):
            peak = one_block(2 * i, score_a, peak, 2 * i + 1, score_b)
            return one_block(2 * i + 1, score_b, peak, 2 * i + 2, score_a)

        peak = lax.fori_loop(0, looped // 2, pair, peak)
    for b in range(looped, blocks):
        scores, into = (score_a, score_b) if b % 2 == 0 else (score_b, score_a)
        peak = one_block(b, scores, peak, b + 1 if b + 1 < blocks else None, into)


def attend(meta, places, queries, keys, values, slots, shard, state, state_block, last):
    count = len(queries)
    tokens, width = queries[0].shape
    whole = keys.shape[0] > slots
    hd = keys.shape[1] // 2 if whole else keys.shape[1]
    rows = tokens * (width // hd)
    row_block = min(MAX_BLOCK, rows)
    key_tile = min(MAX_TILE, slots)
    holders = meta.shape[0] // 2 - places
    first = state is None

    def fixed(shape):
        return pl.BlockSpec(shape, lambda i, meta_ref: (0, 0))

    def shard_at(column):
        if not whole:
            return pl.BlockSpec((slots, hd), lambda i, meta_ref: (0, 0))
        return pl.BlockSpec(
            (slots, hd), lambda i, meta_ref: (meta_ref[2 * places + holders + shard], column)
        )

    in_specs = [fixed((tokens, width))] * count + [shard_at(0), shard_at(1)]
    operands = [meta, *queries, keys, values]
    if not first:
        in_specs += [pl.BlockSpec((count * rows, hd), lambda i, meta_ref: (state_block, 0))] * 2
        operands += state
    if last:
        out_shape = [jax.ShapeDtypeStruct((tokens + PART_ROWS, width), jnp.bfloat16)] * count
        out_specs = [fixed((tokens + PART_ROWS, width))] * count
    else:
        out_shape = [jax.ShapeDtypeStruct((count * rows, hd), jnp.float32)] * 2
        out_specs = [fixed((count * rows, hd))] * 2
    return pl.pallas_call(
        functools.partial(attend_kernel, count, first, last, shard, places),
        grid_spec=pltpu.PrefetchScalarGridSpec(
            num_scalar_prefetch=1,
            grid=(1,),
            in_specs=in_specs,
            out_specs=out_specs,
            scratch_shapes=[
                pltpu.VMEM((count * rows, 2 * hd), jnp.bfloat16),
                pltpu.VMEM((slots, 2 * hd), jnp.bfloat16),
                pltpu.VMEM((slots, 2 * hd), jnp.bfloat16),
                pltpu.VMEM((slots // key_tile, row_block, key_tile), jnp.float32),
                pltpu.VMEM((slots // key_tile, row_block, key_tile), jnp.float32),
            ],
        ),
        out_shape=out_shape,
        compiler_params=pltpu.CompilerParams(vmem_limit_bytes=50 * 1024 * 1024),
        cost_estimate=pl.CostEstimate(
            flops=4 * count * rows * slots * hd,
            bytes_accessed=4 * slots * hd,
            transcendentals=count * rows * slots,
        ),
        name="attend_last" if last else "attend",
    )(*operands)


def combine_kernel(capacity, meta_ref, q_ref, k_ref, v_ref, *refs):
    *part_refs, out_ref, stacked = refs
    _, tokens, hd = k_ref.shape
    width = q_ref.shape[2]
    heads = width // hd
    scale = LOG2E / math.sqrt(hd)
    places = len(part_refs) * capacity
    for i, part_ref in enumerate(part_refs):
        for slot in range(capacity):
            r = meta_ref[i * capacity + slot]

            @pl.when(meta_ref[places + i * capacity + slot] > 0)
            def _(r=r, part_ref=part_ref, slot=slot):
                for h in range(heads):
                    stacked[h * tokens : (h + 1) * tokens, :] = q_ref[r, :, h * hd : (h + 1) * hd]
                s = nt_dot(stacked[...], k_ref[r]) * scale
                row = lax.broadcasted_iota(jnp.int32, s.shape, 0) % tokens
                seen = row >= lax.broadcasted_iota(jnp.int32, s.shape, 1)
                s = jnp.where(seen, s, MASKED)
                m = jnp.max(s, axis=1, keepdims=True)
                w = jnp.where(seen, jnp.exp2(s - m), 0.0)
                total = jnp.sum(w, axis=1, keepdims=True)
                o = jnp.dot(w.astype(jnp.bfloat16), v_ref[r], preferred_element_type=jnp.float32)
                base = part_ref.shape[0] - PART_ROWS
                for h in range(heads):
                    rows = slice(h * tokens, (h + 1) * tokens)
                    lanes = slice(h * hd, (h + 1) * hd)
                    far = part_ref[slot * tokens : (slot + 1) * tokens, lanes].astype(jnp.float32)
                    pieces = part_ref[base:, lanes].astype(jnp.float32)
                    flat = pieces[0:1] + pieces[1:2] + pieces[2:3]
                    lse = jnp.broadcast_to(flat, (hd, hd)).T[slot * tokens : (slot + 1) * tokens, :]
                    top = jnp.maximum(m[rows], lse)
                    own_scale = jnp.exp2(m[rows] - top)
                    far_scale = jnp.exp2(lse - top)
                    out_ref[r, :, lanes] = (
                        (own_scale * o[rows] + far_scale * far) / (own_scale * total[rows] + far_scale)
                    ).astype(jnp.bfloat16)


def combine(meta, capacity, q, keys, values, parts):
    responses, tokens, width = q.shape
    hd = keys.shape[-1]
    heads = width // hd
    return pl.pallas_call(
        functools.partial(combine_kernel, capacity),
        out_shape=jax.ShapeDtypeStruct(q.shape, jnp.bfloat16),
        in_specs=[pl.BlockSpec(memory_space=pltpu.SMEM)]
        + [pl.BlockSpec(memory_space=pltpu.VMEM)] * (3 + len(parts)),
        out_specs=pl.BlockSpec(memory_space=pltpu.VMEM),
        scratch_shapes=[pltpu.VMEM((heads * tokens, hd), jnp.bfloat16)],
        compiler_params=pltpu.CompilerParams(vmem_limit_bytes=24 * 1024 * 1024),
        cost_estimate=pl.CostEstimate(
            flops=4 * responses * heads * tokens * tokens * hd,
            bytes_accessed=8 * responses * tokens * width,
            transcendentals=responses * heads * tokens * tokens,
        ),
        name="combine",
    )(meta, q, keys, values, *parts)


INWARD = ((0, 2), (3, 1))
OUTWARD = ((1, 0), (2, 3))


def plane_hop(x, pairs):
    return lax.ppermute(x, "ctx", [(a * 2 + h, b * 2 + h) for a, b in pairs for h in range(2)])


def project(rows, other, blocks, plane, holder):
    group = lax.axis_index("kvh")
    groups = lax.axis_size("kvh")
    count = rows.shape[0]
    apart = plane ^ group
    even = apart & 1 == 0
    low = apart < 2
    block0, block1, block3, two_in, out_a, out_b = blocks
    half = out_a.shape[1]
    inner = (plane == 1) | (plane == 2)

    def swap_holders(x, keep):
        pairs = [
            ((p * 2 + h) * groups + k, (p * 2 + 1 - h) * groups + k)
            for p in range(groups)
            for h in range(2)
            for k in range(groups)
            if keep(p ^ k)
        ]
        return lax.ppermute(x, ("ctx", "kvh"), pairs)

    def to_group(x, flip, keep):
        pairs = [
            (c * groups + (k ^ flip), c * groups + k)
            for c in range(2 * groups)
            for k in range(groups)
            if keep(c // 2 ^ k)
        ]
        return lax.ppermute(x, ("ctx", "kvh"), pairs)

    def terms(x, block):
        return jnp.dot(x, block, preferred_element_type=jnp.float32).astype(jnp.bfloat16)

    def add(a, b):
        return (a.astype(jnp.float32) + b.astype(jnp.float32)).astype(jnp.bfloat16)

    def pair_sums(x):
        term0, term1, term3 = terms(x, block0), terms(x, block1), terms(x, block3)
        sent = jnp.concatenate([jnp.where(even, term1, term0), term3], axis=1)
        got = to_group(sent, 1, lambda i: True)
        width = term0.shape[1]
        return add(jnp.where(even, term0, term1), got[:, :width]), add(term3, got[:, width:])

    def chip_sums(near, far):
        got = to_group(jnp.where(low, far, near), 2, lambda i: i != 2)
        return add(jnp.where(low, near, far), got)

    mine_sums = pair_sums(rows)
    mine = chip_sums(*mine_sums)
    other, out_a, *mine_sums = lax.optimization_barrier((other, out_a, *mine_sums))
    their_sums = pair_sums(other)
    theirs = chip_sums(*their_sums)
    both = jnp.concatenate([rows, other], axis=0)

    def last_block(came_in, came_out, *ready):
        came_out = after(came_out, *ready)
        term = terms(both, jnp.where(inner, came_in, came_out))
        return add(term, to_group(term, 1, lambda i: i & 1 == 0))

    def last_sums(total):
        total = add(total, to_group(total, 2, lambda i: i == 2))
        return total[:count], swap_holders(total[count:], lambda i: i == 2)

    half_a = last_block(two_in[:, :half], out_a, *their_sums, mine)
    half_b = last_block(two_in[:, half:], out_b, half_a)
    half_b = after(half_b, theirs)
    back = swap_holders(theirs, lambda i: i != 2)
    mine_a, back_a = last_sums(half_a)
    mine_b, back_b = last_sums(half_b)
    mine = jnp.where(apart == 2, jnp.concatenate([mine_a, mine_b], axis=1), mine)
    back = jnp.where(apart == 2, jnp.concatenate([back_a, back_b], axis=1), back)
    return jnp.where(
        holder == 0,
        jnp.concatenate([mine, back], axis=1),
        jnp.concatenate([back, mine], axis=1),
    )


def local(
    queries, resp_keys, resp_values, prefix_keys, prefix_values, prefix_len, prompt_of, out_weight
):
    ctx_count = lax.axis_size("ctx")
    kvh_count = lax.axis_size("kvh")
    position = lax.axis_index("ctx")
    own_queries = queries[:, :, 0]
    own_keys = resp_keys[:, :, 0]
    own_values = resp_values[:, :, 0]
    resp_count, tokens_each, width = own_queries.shape
    slot_count = prefix_keys.shape[0]
    prompts = prefix_len.shape[0]
    holders = ctx_count // prompts
    my_prompt = position // holders
    my_holder = position % holders
    capacity = max(LANES // tokens_each, resp_count // prompts)
    places = prompts * capacity
    by_plane = kvh_count == prompts == 4 and holders == 2

    def cross(x, i):
        pairs = [(p * holders + h, (p ^ i) * holders + h) for p in range(prompts) for h in range(holders)]
        return lax.ppermute(x, "ctx", pairs)

    if by_plane:
        one, three = cross(out_weight, 1), cross(out_weight, 3)
        two_in = plane_hop(out_weight, INWARD)
    chunks, meta = pack(prompt_of, prefix_len, own_queries, capacity, holders, slot_count)
    chunks = chunks[:1] + [cross(x, i) for i, x in enumerate(chunks) if i > 0]
    near = prefix_keys[:, 0], prefix_values[:, 0]
    lines = [[p * holders + h for h in range(holders)] for p in range(prompts)]
    joined = jnp.concatenate(near, axis=1)
    joined = lax.all_gather(joined, "ctx", axis=0, tiled=True, axis_index_groups=lines)
    far = joined, joined
    away = chunks[:0:-1]

    state_home = state_away = None
    for shard in range(holders - 1):
        kv = near if shard == 0 else far
        state_home = attend(meta, places, chunks[:1], *kv, slot_count, shard, state_home, 0, False)
        state_home, away = lax.optimization_barrier((state_home, away))
        state_away = attend(meta, places, away, *kv, slot_count, shard, state_away, 0, False)
    shard = holders - 1
    done = [None] * prompts
    for where, members in enumerate([range(prompts - 1, 1, -1), [1]]):
        queries_now = [away[prompts - 1 - i] for i in members]
        block = 0 if where == 0 else prompts - 2
        results = attend(meta, places, queries_now, *far, slot_count, shard, state_away, block, True)
        for i, x in zip(members, results):
            done[i] = cross(x, i)
        if by_plane and where == 0:
            one, three, state_away = lax.optimization_barrier((one, three, state_away))
            half = out_weight.shape[1] // 2
            two_out = [plane_hop(x, OUTWARD) for x in (three[:, :half], three[:, half:])]
    if by_plane:
        two_in, state_home = lax.optimization_barrier((two_in, state_home))
    (done[0],) = attend(meta, places, chunks[:1], *far, slot_count, shard, state_home, 0, True)
    attended = combine(meta, capacity, own_queries, own_keys, own_values, done)
    rows = attended.reshape(resp_count * tokens_each, width)

    if by_plane:
        other = lax.ppermute(
            rows, "ctx", [(p * 2 + h, p * 2 + 1 - h) for p in range(prompts) for h in range(2)]
        )
        blocks = out_weight, one, three, two_in, *two_out
        projected = project(rows, other, blocks, my_prompt, my_holder)
    else:
        weights = lax.all_gather(out_weight, "ctx", axis=1, tiled=True)
        terms = jnp.dot(rows, weights, preferred_element_type=jnp.float32)
        projected = lax.psum_scatter(
            terms.astype(jnp.bfloat16), "kvh", scatter_dimension=1, tiled=True
        )
    return (attended[:, :, None, :], projected)


def solution(mesh):
    in_specs = (
        P("ctx", None, "kvh", None),
        P("ctx", None, "kvh", None),
        P("ctx", None, "kvh", None),
        P("ctx", "kvh", None),
        P("ctx", "kvh", None),
        P(),
        P(),
        P("kvh", "ctx"),
    )
    out_specs = (P("ctx", None, "kvh", None), P("ctx", "kvh"))
    return jax.shard_map(local, mesh=mesh, in_specs=in_specs, out_specs=out_specs, check_vma=False)
```

```python
import functools
import math

import jax
import jax.numpy as jnp
from jax import lax
from jax.experimental import pallas as pl
from jax.experimental.pallas import tpu as pltpu
from jax.sharding import PartitionSpec as P

MASKED = -1e30
LOG2E = math.log2(math.e)
LANES = 128
PART_ROWS = 16
MAX_TILE = 1024
MAX_BLOCK = 512


def nt_dot(a, b):
    return lax.dot_general(a, b, (((1,), (1,)), ((), ())), preferred_element_type=jnp.float32)


def after(x, *others):
    return lax.optimization_barrier((x, *others))[0]


def pack_kernel(capacity, holders, slots, prompt_ref, len_ref, q_ref, *refs):
    *chunk_refs, meta_ref = refs
    responses, tokens, _ = q_ref.shape
    position = lax.axis_index("ctx")
    mine, holder = position // holders, position % holders
    named = [prompt_ref[position * responses + r] for r in range(responses)]
    ranks = []
    for r in range(responses):
        rank = jnp.int32(0)
        for before in range(r):
            rank += (named[before] == named[r]).astype(jnp.int32)
        ranks.append(rank)
    places = len(chunk_refs) * capacity
    for i, chunk_ref in enumerate(chunk_refs):
        for slot in range(capacity):
            chosen, present = jnp.int32(0), jnp.int32(0)
            for r in range(responses):
                hit = ((named[r] == mine ^ i) & (ranks[r] == slot)).astype(jnp.int32)
                chosen += hit * r
                present += hit
            meta_ref[i * capacity + slot] = chosen
            meta_ref[places + i * capacity + slot] = present
            rows = slice(slot * tokens, (slot + 1) * tokens)
            chunk_ref[rows, :] = q_ref[chosen]

            @pl.when(present == 0)
            def _(chunk_ref=chunk_ref, rows=rows):
                chunk_ref[rows, :] = jnp.zeros_like(chunk_ref[rows, :])

    length = len_ref[mine]
    for j in range(holders):
        place = (holder + j) % holders
        meta_ref[2 * places + j] = jnp.clip(length - place * slots, 0, slots)
        meta_ref[2 * places + holders + j] = place


def pack(prompt_of, prefix_len, q, capacity, holders, slots):
    _, tokens, width = q.shape
    prompts = prefix_len.shape[0]
    smem = pl.BlockSpec(memory_space=pltpu.SMEM)
    vmem = pl.BlockSpec(memory_space=pltpu.VMEM)
    *chunks, meta = pl.pallas_call(
        functools.partial(pack_kernel, capacity, holders, slots),
        out_shape=[jax.ShapeDtypeStruct((capacity * tokens, width), q.dtype)] * prompts
        + [jax.ShapeDtypeStruct((2 * (prompts * capacity + holders),), jnp.int32)],
        in_specs=[smem, smem, vmem],
        out_specs=[vmem] * prompts + [smem],
        cost_estimate=pl.CostEstimate(flops=0, bytes_accessed=4 * q.size, transcendentals=0),
        name="pack",
    )(prompt_of, prefix_len, q)
    return chunks, meta


def attend_kernel(count, first, last, shard, places, meta_ref, *refs):
    q_refs, (k_ref, v_ref, *refs) = refs[:count], refs[count:]
    if not first:
        prev_o_ref, prev_lse_ref, *refs = refs
    if last:
        out_refs, refs = refs[:count], refs[count:]
    else:
        o_ref, lse_ref, *refs = refs
    qext, kext, vext, score_a, score_b = refs
    tokens = q_refs[0].shape[0]
    slots, hd = k_ref.shape
    heads = q_refs[0].shape[1] // hd
    scale = LOG2E / math.sqrt(hd)
    tiles, row_block, key_tile = score_a.shape
    per_chunk = heads * tokens // row_block
    live = meta_ref[2 * places + shard]

    @pl.when(live == slots)
    def _():
        for t in range(tiles):
            at = slice(t * key_tile, (t + 1) * key_tile)
            keys = k_ref[at, :]
            kext[at, :hd] = keys
            kext[at, hd:] = keys
            vext[at, :hd] = v_ref[at, :]
            vext[at, hd:] = jnp.ones((key_tile, hd), jnp.bfloat16)

    @pl.when(live != slots)
    def _():
        def prepare(step, carry):
            at = pl.ds(pl.multiple_of(step * key_tile, key_tile), key_tile)
            alive = step * key_tile + lax.broadcasted_iota(jnp.int32, (key_tile, hd), 0) < live
            keys = jnp.where(alive, k_ref[at, :].astype(jnp.float32), k_ref[0:1, :].astype(jnp.float32))
            keys = keys.astype(jnp.bfloat16)
            kext[at, :hd] = keys
            kext[at, hd:] = keys
            vext[at, :hd] = jnp.where(alive, v_ref[at, :].astype(jnp.float32), 0.0).astype(jnp.bfloat16)
            vext[at, hd:] = jnp.where(alive, 1.0, 0.0).astype(jnp.bfloat16)
            return carry

        lax.fori_loop(0, tiles, prepare, 0)

    for c, q_ref in enumerate(q_refs):
        for h in range(heads):
            rows = slice((c * heads + h) * tokens, (c * heads + h + 1) * tokens)
            x = q_ref[:, h * hd : (h + 1) * hd].astype(jnp.float32) * scale
            high = x.astype(jnp.bfloat16)
            qext[rows, :hd] = high
            qext[rows, hd:] = (x - high.astype(jnp.float32)).astype(jnp.bfloat16)

    low = jnp.full((row_block, LANES), MASKED, jnp.float32)

    def rows_of(b):
        if isinstance(b, int):
            return slice(b * row_block, (b + 1) * row_block)
        return pl.ds(pl.multiple_of(b * row_block, row_block), row_block)

    def score_tile(b, t, into, peak):
        s = nt_dot(qext[rows_of(b), :], kext[t * key_tile : (t + 1) * key_tile, :])
        into[t] = s
        for j in range(key_tile // LANES):
            peak = jnp.maximum(peak, s[:, j * LANES : (j + 1) * LANES])
        return peak

    def one_block(b, scores, peak, following, into):
        m = jnp.max(peak, axis=1, keepdims=True)
        peak = low
        acc = jnp.zeros((row_block, 2 * hd), jnp.float32)
        for t in range(tiles):
            if following is not None:
                peak = score_tile(following, t, into, peak)
            w = jnp.exp2(scores[t] - m).astype(jnp.bfloat16)
            acc = acc + jnp.dot(
                w, vext[t * key_tile : (t + 1) * key_tile, :], preferred_element_type=jnp.float32
            )
        total = acc[:, hd:]
        some = total > 0.0
        safe = jnp.where(some, total, 1.0)
        o = acc[:, :hd] / safe
        lse = jnp.where(some, m + jnp.log2(safe), MASKED)
        rows = rows_of(b)
        if not first:
            before = prev_lse_ref[rows, :]
            top = jnp.maximum(before, lse)
            w_before = jnp.exp2(before - top)
            w_now = jnp.exp2(lse - top)
            both = w_before + w_now
            o = (w_before * prev_o_ref[rows, :] + w_now * o) / both
            lse = top + jnp.log2(both)
        if not last:
            o_ref[rows, :] = o
            lse_ref[rows, :] = lse
            return peak
        out_ref = out_refs[b // per_chunk]
        for j in range(row_block // tokens):
            h = (b % per_chunk) * (row_block // tokens) + j
            part = slice(j * tokens, (j + 1) * tokens)
            lanes = slice(h * hd, (h + 1) * hd)
            out_ref[:tokens, lanes] = o[part].astype(jnp.bfloat16)
            flat = lse[part].T[:PART_ROWS, :]
            high = flat.astype(jnp.bfloat16).astype(jnp.float32)
            middle = (flat - high).astype(jnp.bfloat16).astype(jnp.float32)
            row = lax.broadcasted_iota(jnp.int32, flat.shape, 0)
            out_ref[tokens:, lanes] = jnp.where(
                row == 0, high, jnp.where(row == 1, middle, jnp.where(row == 2, flat - high - middle, 0.0))
            ).astype(jnp.bfloat16)
        return peak

    blocks = count * per_chunk
    peak = low
    for t in range(tiles):
        peak = score_tile(0, t, score_a, peak)
    looped = 0
    if not last and per_chunk == 2 and count > 1:
        looped = blocks - 2

        def pair(i, peak):
            peak = one_block(2 * i, score_a, peak, 2 * i + 1, score_b)
            return one_block(2 * i + 1, score_b, peak, 2 * i + 2, score_a)

        peak = lax.fori_loop(0, looped // 2, pair, peak)
    for b in range(looped, blocks):
        scores, into = (score_a, score_b) if b % 2 == 0 else (score_b, score_a)
        peak = one_block(b, scores, peak, b + 1 if b + 1 < blocks else None, into)


def attend(meta, places, queries, keys, values, slots, shard, state, state_block, last):
    count = len(queries)
    tokens, width = queries[0].shape
    whole = keys.shape[0] > slots
    hd = keys.shape[1] // 2 if whole else keys.shape[1]
    rows = tokens * (width // hd)
    row_block = min(MAX_BLOCK, rows)
    key_tile = min(MAX_TILE, slots)
    holders = meta.shape[0] // 2 - places
    first = state is None

    def fixed(shape):
        return pl.BlockSpec(shape, lambda i, meta_ref: (0, 0))

    def shard_at(column):
        if not whole:
            return pl.BlockSpec((slots, hd), lambda i, meta_ref: (0, 0))
        return pl.BlockSpec(
            (slots, hd), lambda i, meta_ref: (meta_ref[2 * places + holders + shard], column)
        )

    in_specs = [fixed((tokens, width))] * count + [shard_at(0), shard_at(1)]
    operands = [meta, *queries, keys, values]
    if not first:
        in_specs += [pl.BlockSpec((count * rows, hd), lambda i, meta_ref: (state_block, 0))] * 2
        operands += state
    if last:
        out_shape = [jax.ShapeDtypeStruct((tokens + PART_ROWS, width), jnp.bfloat16)] * count
        out_specs = [fixed((tokens + PART_ROWS, width))] * count
    else:
        out_shape = [jax.ShapeDtypeStruct((count * rows, hd), jnp.float32)] * 2
        out_specs = [fixed((count * rows, hd))] * 2
    return pl.pallas_call(
        functools.partial(attend_kernel, count, first, last, shard, places),
        grid_spec=pltpu.PrefetchScalarGridSpec(
            num_scalar_prefetch=1,
            grid=(1,),
            in_specs=in_specs,
            out_specs=out_specs,
            scratch_shapes=[
                pltpu.VMEM((count * rows, 2 * hd), jnp.bfloat16),
                pltpu.VMEM((slots, 2 * hd), jnp.bfloat16),
                pltpu.VMEM((slots, 2 * hd), jnp.bfloat16),
                pltpu.VMEM((slots // key_tile, row_block, key_tile), jnp.float32),
                pltpu.VMEM((slots // key_tile, row_block, key_tile), jnp.float32),
            ],
        ),
        out_shape=out_shape,
        compiler_params=pltpu.CompilerParams(vmem_limit_bytes=50 * 1024 * 1024),
        cost_estimate=pl.CostEstimate(
            flops=4 * count * rows * slots * hd,
            bytes_accessed=4 * slots * hd,
            transcendentals=count * rows * slots,
        ),
        name="attend_last" if last else "attend",
    )(*operands)


def combine_kernel(capacity, meta_ref, q_ref, k_ref, v_ref, *refs):
    *part_refs, out_ref, stacked = refs
    _, tokens, hd = k_ref.shape
    width = q_ref.shape[2]
    heads = width // hd
    scale = LOG2E / math.sqrt(hd)
    places = len(part_refs) * capacity
    for i, part_ref in enumerate(part_refs):
        for slot in range(capacity):
            r = meta_ref[i * capacity + slot]

            @pl.when(meta_ref[places + i * capacity + slot] > 0)
            def _(r=r, part_ref=part_ref, slot=slot):
                for h in range(heads):
                    stacked[h * tokens : (h + 1) * tokens, :] = q_ref[r, :, h * hd : (h + 1) * hd]
                s = nt_dot(stacked[...], k_ref[r]) * scale
                row = lax.broadcasted_iota(jnp.int32, s.shape, 0) % tokens
                seen = row >= lax.broadcasted_iota(jnp.int32, s.shape, 1)
                s = jnp.where(seen, s, MASKED)
                m = jnp.max(s, axis=1, keepdims=True)
                w = jnp.where(seen, jnp.exp2(s - m), 0.0)
                total = jnp.sum(w, axis=1, keepdims=True)
                o = jnp.dot(w.astype(jnp.bfloat16), v_ref[r], preferred_element_type=jnp.float32)
                base = part_ref.shape[0] - PART_ROWS
                for h in range(heads):
                    rows = slice(h * tokens, (h + 1) * tokens)
                    lanes = slice(h * hd, (h + 1) * hd)
                    far = part_ref[slot * tokens : (slot + 1) * tokens, lanes].astype(jnp.float32)
                    pieces = part_ref[base:, lanes].astype(jnp.float32)
                    flat = pieces[0:1] + pieces[1:2] + pieces[2:3]
                    lse = jnp.broadcast_to(flat, (hd, hd)).T[slot * tokens : (slot + 1) * tokens, :]
                    top = jnp.maximum(m[rows], lse)
                    own_scale = jnp.exp2(m[rows] - top)
                    far_scale = jnp.exp2(lse - top)
                    out_ref[r, :, lanes] = (
                        (own_scale * o[rows] + far_scale * far) / (own_scale * total[rows] + far_scale)
                    ).astype(jnp.bfloat16)


def combine(meta, capacity, q, keys, values, parts):
    responses, tokens, width = q.shape
    hd = keys.shape[-1]
    heads = width // hd
    return pl.pallas_call(
        functools.partial(combine_kernel, capacity),
        out_shape=jax.ShapeDtypeStruct(q.shape, jnp.bfloat16),
        in_specs=[pl.BlockSpec(memory_space=pltpu.SMEM)]
        + [pl.BlockSpec(memory_space=pltpu.VMEM)] * (3 + len(parts)),
        out_specs=pl.BlockSpec(memory_space=pltpu.VMEM),
        scratch_shapes=[pltpu.VMEM((heads * tokens, hd), jnp.bfloat16)],
        compiler_params=pltpu.CompilerParams(vmem_limit_bytes=24 * 1024 * 1024),
        cost_estimate=pl.CostEstimate(
            flops=4 * responses * heads * tokens * tokens * hd,
            bytes_accessed=8 * responses * tokens * width,
            transcendentals=responses * heads * tokens * tokens,
        ),
        name="combine",
    )(meta, q, keys, values, *parts)


def multiply_kernel(kept_first_ref, *refs):
    *row_refs, weight_ref, kept_ref, sent_ref, rows = refs
    count = row_refs[0].shape[0]

    @pl.when(pl.program_id(0) == 0)
    def _():
        for first, order in ((1, (0, 1, 2, 3)), (0, (2, 3, 0, 1))):

            @pl.when(kept_first_ref[0] == first)
            def _(order=order):
                for place, i in enumerate(order):
                    rows[place * count : (place + 1) * count, :] = row_refs[i][...]

    for place, ref in ((1, sent_ref), (0, kept_ref)):
        for part in range(2):
            at = slice(part * count, (part + 1) * count)
            x = rows[2 * place * count + part * count : 2 * place * count + (part + 1) * count, :]
            ref[at, :] = jnp.dot(x, weight_ref[0], preferred_element_type=jnp.float32).astype(ref.dtype)


def multiply(kept_first, row_parts, weights):
    count, depth = row_parts[0].shape
    blocks, _, width = weights.shape
    rows = pl.BlockSpec((count, depth), lambda j: (0, 0))
    out = pl.BlockSpec((2 * count, width), lambda j: (0, j))
    return pl.pallas_call(
        multiply_kernel,
        grid=(blocks,),
        out_shape=[jax.ShapeDtypeStruct((2 * count, blocks * width), jnp.bfloat16)] * 2,
        in_specs=[pl.BlockSpec(memory_space=pltpu.SMEM)]
        + [rows] * 4
        + [pl.BlockSpec((1, depth, width), lambda j: (j, 0, 0))],
        out_specs=[out] * 2,
        scratch_shapes=[pltpu.VMEM((4 * count, depth), jnp.bfloat16)],
        compiler_params=pltpu.CompilerParams(vmem_limit_bytes=32 * 1024 * 1024),
        cost_estimate=pl.CostEstimate(
            flops=8 * count * depth * blocks * width,
            bytes_accessed=2 * blocks * depth * width,
            transcendentals=0,
        ),
        name="multiply",
    )(kept_first.reshape(1), *row_parts, weights)


def project(rows, weights, plane, holder):
    group = lax.axis_index("kvh")
    chip = group // 2
    same = group % 2 == plane % 2
    parts = 2
    count = rows.shape[0] // parts
    width = weights.shape[2]

    def send(x, to, keep=lambda p, k: True):
        pairs = []
        for p in range(4):
            for h in range(2):
                for k in range(4):
                    if keep(p, k):
                        q, g, m = to(p, h, k)
                        pairs.append(((p * 2 + h) * 4 + k, (q * 2 + g) * 4 + m))
        return lax.ppermute(x, ("ctx", "kvh"), pairs)

    def fetch(x):
        return (
            x,
            send(x, lambda p, h, k: (p, 1 - h, k)),
            send(x, lambda p, h, k: (p ^ 1, h, k)),
            send(x, lambda p, h, k: (p ^ 1, 1 - h, k)),
        )

    def add(a, b):
        return (a.astype(jnp.float32) + b.astype(jnp.float32)).astype(jnp.bfloat16)

    def results(fetched):
        kept, sent = multiply(same.astype(jnp.int32), fetched, weights)
        total = add(kept, send(sent, lambda p, h, k: (p, h, k ^ 1)))
        low, high = total[:, :width], total[:, width:]
        away = send(jnp.where(chip == 0, high, low), lambda p, h, k: (p, h, k ^ 2))
        return add(jnp.where(chip == 0, low, high), away)

    def deliver(total):
        direct = send(
            total[:count], lambda p, h, k: (p ^ 1, h, k ^ 1), lambda p, k: k % 2 != p % 2
        )
        back = send(
            total[count:],
            lambda p, h, k: (p, 1 - h, k) if k % 2 == p % 2 else (p ^ 1, 1 - h, k ^ 1),
        )
        mine = jnp.where(same, total[:count], direct)
        return jnp.where(
            holder == 0,
            jnp.concatenate([mine, back], axis=1),
            jnp.concatenate([back, mine], axis=1),
        )

    fetched = [fetch(rows[i * count : (i + 1) * count]) for i in range(parts)]
    return jnp.concatenate([deliver(results(x)) for x in fetched], axis=0)


def local(
    queries, resp_keys, resp_values, prefix_keys, prefix_values, prefix_len, prompt_of, out_weight
):
    ctx_count = lax.axis_size("ctx")
    kvh_count = lax.axis_size("kvh")
    position = lax.axis_index("ctx")
    own_queries = queries[:, :, 0]
    own_keys = resp_keys[:, :, 0]
    own_values = resp_values[:, :, 0]
    resp_count, tokens_each, width = own_queries.shape
    slot_count = prefix_keys.shape[0]
    prompts = prefix_len.shape[0]
    holders = ctx_count // prompts
    my_prompt = position // holders
    my_holder = position % holders
    capacity = max(LANES // tokens_each, resp_count // prompts)
    places = prompts * capacity
    by_plane = kvh_count == prompts == 4 and holders == 2

    def cross(x, i):
        pairs = [(p * holders + h, (p ^ i) * holders + h) for p in range(prompts) for h in range(holders)]
        return lax.ppermute(x, "ctx", pairs)

    chunks, meta = pack(prompt_of, prefix_len, own_queries, capacity, holders, slot_count)
    chunks = chunks[:1] + [cross(x, i) for i, x in enumerate(chunks) if i > 0]
    near = prefix_keys[:, 0], prefix_values[:, 0]
    away = chunks[:0:-1]
    if by_plane:
        pairs = [[p * holders + h, (p + 2) * holders + h] for p in range(2) for h in range(holders)]
        weights = lax.all_gather(
            after(out_weight, *away), "ctx", axis=0, tiled=False, axis_index_groups=pairs
        )
        shards = [near, [after(x, away[-1]) for x in near]]
        shards[1] = [
            lax.ppermute(x, "ctx", [(c, c ^ 1) for c in range(ctx_count)]) for x in shards[1]
        ]
    else:
        lines = [[p * holders + h for h in range(holders)] for p in range(prompts)]
        joined = jnp.concatenate(near, axis=1)
        joined = lax.all_gather(joined, "ctx", axis=0, tiled=True, axis_index_groups=lines)
        shards = [near] + [(joined, joined)] * (holders - 1)

    state_home = state_away = None
    for shard in range(holders - 1):
        kv = shards[shard]
        state_home = attend(meta, places, chunks[:1], *kv, slot_count, shard, state_home, 0, False)
        state_home, away = lax.optimization_barrier((state_home, away))
        state_away = attend(meta, places, away, *kv, slot_count, shard, state_away, 0, False)
    shard = holders - 1
    far = shards[shard]
    done = [None] * prompts
    for where, members in enumerate([range(prompts - 1, 1, -1), [1]]):
        queries_now = [away[prompts - 1 - i] for i in members]
        block = 0 if where == 0 else prompts - 2
        results = attend(meta, places, queries_now, *far, slot_count, shard, state_away, block, True)
        for i, x in zip(members, results):
            done[i] = cross(x, i)
    (done[0],) = attend(meta, places, chunks[:1], *far, slot_count, shard, state_home, 0, True)
    attended = combine(meta, capacity, own_queries, own_keys, own_values, done)
    rows = attended.reshape(resp_count * tokens_each, width)

    if by_plane:
        projected = project(rows, weights, my_prompt, my_holder)
    else:
        weights = lax.all_gather(out_weight, "ctx", axis=1, tiled=True)
        terms = jnp.dot(rows, weights, preferred_element_type=jnp.float32)
        projected = lax.psum_scatter(
            terms.astype(jnp.bfloat16), "kvh", scatter_dimension=1, tiled=True
        )
    return (attended[:, :, None, :], projected)


def solution(mesh):
    in_specs = (
        P("ctx", None, "kvh", None),
        P("ctx", None, "kvh", None),
        P("ctx", None, "kvh", None),
        P("ctx", "kvh", None),
        P("ctx", "kvh", None),
        P(),
        P(),
        P("kvh", "ctx"),
    )
    out_specs = (P("ctx", None, "kvh", None), P("ctx", "kvh"))
    return jax.shard_map(local, mesh=mesh, in_specs=in_specs, out_specs=out_specs, check_vma=False)
```

```python
import functools
import math

import jax
import jax.numpy as jnp
from jax import lax
from jax.experimental import pallas as pl
from jax.experimental.pallas import tpu as pltpu
from jax.sharding import PartitionSpec as P

MASKED = -1e30
LOG2E = math.log2(math.e)
LANES = 128
PART_ROWS = 16
MAX_TILE = 512
MAX_BLOCK = 1024
VMEM = 60 * 1024 * 1024


def nt_dot(a, b):
    return lax.dot_general(a, b, (((1,), (1,)), ((), ())), preferred_element_type=jnp.float32)


def after(x, *others):
    return lax.optimization_barrier((x, *others))[0]


def pack_kernel(capacity, holders, slots, prompt_ref, len_ref, q_ref, *refs):
    *chunk_refs, meta_ref = refs
    responses, tokens, _ = q_ref.shape
    position = lax.axis_index("ctx")
    mine, holder = position // holders, position % holders
    named = [prompt_ref[position * responses + r] for r in range(responses)]
    ranks = []
    for r in range(responses):
        rank = jnp.int32(0)
        for before in range(r):
            rank += (named[before] == named[r]).astype(jnp.int32)
        ranks.append(rank)
    places = len(chunk_refs) * capacity
    for i, chunk_ref in enumerate(chunk_refs):
        for slot in range(capacity):
            chosen, present = jnp.int32(0), jnp.int32(0)
            for r in range(responses):
                hit = ((named[r] == mine ^ i) & (ranks[r] == slot)).astype(jnp.int32)
                chosen += hit * r
                present += hit
            meta_ref[i * capacity + slot] = chosen
            meta_ref[places + i * capacity + slot] = present
            rows = slice(slot * tokens, (slot + 1) * tokens)
            chunk_ref[rows, :] = q_ref[chosen]

            @pl.when(present == 0)
            def _(chunk_ref=chunk_ref, rows=rows):
                chunk_ref[rows, :] = jnp.zeros_like(chunk_ref[rows, :])

    length = len_ref[mine]
    for j in range(holders):
        place = (holder + j) % holders
        meta_ref[2 * places + j] = jnp.clip(length - place * slots, 0, slots)
        meta_ref[2 * places + holders + j] = place


def pack(prompt_of, prefix_len, q, capacity, holders, slots):
    _, tokens, width = q.shape
    prompts = prefix_len.shape[0]
    smem = pl.BlockSpec(memory_space=pltpu.SMEM)
    vmem = pl.BlockSpec(memory_space=pltpu.VMEM)
    *chunks, meta = pl.pallas_call(
        functools.partial(pack_kernel, capacity, holders, slots),
        out_shape=[jax.ShapeDtypeStruct((capacity * tokens, width), q.dtype)] * prompts
        + [jax.ShapeDtypeStruct((2 * (prompts * capacity + holders),), jnp.int32)],
        in_specs=[smem, smem, vmem],
        out_specs=[vmem] * prompts + [smem],
        compiler_params=pltpu.CompilerParams(vmem_limit_bytes=VMEM),
        cost_estimate=pl.CostEstimate(flops=0, bytes_accessed=4 * q.size, transcendentals=0),
        name="pack",
    )(prompt_of, prefix_len, q)
    return chunks, meta


def attend_kernel(count, first, last, shard, places, meta_ref, *refs):
    q_refs, (k_ref, v_ref, *refs) = refs[:count], refs[count:]
    if not first:
        prev_o_ref, prev_lse_ref, *refs = refs
    if last:
        out_refs, refs = refs[:count], refs[count:]
    else:
        o_ref, lse_ref, *refs = refs
    qext, kext, vext, score_a, score_b = refs
    tokens = q_refs[0].shape[0]
    slots, hd = k_ref.shape
    heads = q_refs[0].shape[1] // hd
    scale = LOG2E / math.sqrt(hd)
    tiles, row_block, key_tile = score_a.shape
    per_chunk = heads * tokens // row_block
    live = meta_ref[2 * places + shard]

    @pl.when(live == slots)
    def _():
        for t in range(tiles):
            at = slice(t * key_tile, (t + 1) * key_tile)
            keys = k_ref[at, :]
            kext[at, :hd] = keys
            kext[at, hd:] = keys
            vext[at, :hd] = v_ref[at, :]
            vext[at, hd:] = jnp.ones((key_tile, hd), jnp.bfloat16)

    @pl.when(live != slots)
    def _():
        def prepare(step, carry):
            at = pl.ds(pl.multiple_of(step * key_tile, key_tile), key_tile)
            alive = step * key_tile + lax.broadcasted_iota(jnp.int32, (key_tile, hd), 0) < live
            keys = jnp.where(alive, k_ref[at, :].astype(jnp.float32), k_ref[0:1, :].astype(jnp.float32))
            keys = keys.astype(jnp.bfloat16)
            kext[at, :hd] = keys
            kext[at, hd:] = keys
            vext[at, :hd] = jnp.where(alive, v_ref[at, :].astype(jnp.float32), 0.0).astype(jnp.bfloat16)
            vext[at, hd:] = jnp.where(alive, 1.0, 0.0).astype(jnp.bfloat16)
            return carry

        lax.fori_loop(0, tiles, prepare, 0)

    for c, q_ref in enumerate(q_refs):
        for h in range(heads):
            rows = slice((c * heads + h) * tokens, (c * heads + h + 1) * tokens)
            x = q_ref[:, h * hd : (h + 1) * hd].astype(jnp.float32) * scale
            high = x.astype(jnp.bfloat16)
            qext[rows, :hd] = high
            qext[rows, hd:] = (x - high.astype(jnp.float32)).astype(jnp.bfloat16)

    low = jnp.full((row_block, LANES), MASKED, jnp.float32)

    def rows_of(b):
        if isinstance(b, int):
            return slice(b * row_block, (b + 1) * row_block)
        return pl.ds(pl.multiple_of(b * row_block, row_block), row_block)

    def score_tile(b, t, into, peak):
        s = nt_dot(qext[rows_of(b), :], kext[t * key_tile : (t + 1) * key_tile, :])
        into[t] = s
        for j in range(key_tile // LANES):
            peak = jnp.maximum(peak, s[:, j * LANES : (j + 1) * LANES])
        return peak

    def one_block(b, scores, peak, following, into):
        m = jnp.max(peak, axis=1, keepdims=True)
        peak = low
        acc = jnp.zeros((row_block, 2 * hd), jnp.float32)
        for t in range(tiles):
            if following is not None:
                peak = score_tile(following, t, into, peak)
            w = jnp.exp2(scores[t] - m).astype(jnp.bfloat16)
            acc = acc + jnp.dot(
                w, vext[t * key_tile : (t + 1) * key_tile, :], preferred_element_type=jnp.float32
            )
        total = acc[:, hd:]
        some = total > 0.0
        safe = jnp.where(some, total, 1.0)
        o = acc[:, :hd] / safe
        lse = jnp.where(some, m + jnp.log2(safe), MASKED)
        rows = rows_of(b)
        if not first:
            before = prev_lse_ref[rows, :]
            top = jnp.maximum(before, lse)
            w_before = jnp.exp2(before - top)
            w_now = jnp.exp2(lse - top)
            both = w_before + w_now
            o = (w_before * prev_o_ref[rows, :] + w_now * o) / both
            lse = top + jnp.log2(both)
        if not last:
            o_ref[rows, :] = o
            lse_ref[rows, :] = lse
            return peak
        out_ref = out_refs[b // per_chunk]
        for j in range(row_block // tokens):
            h = (b % per_chunk) * (row_block // tokens) + j
            part = slice(j * tokens, (j + 1) * tokens)
            lanes = slice(h * hd, (h + 1) * hd)
            out_ref[:tokens, lanes] = o[part].astype(jnp.bfloat16)
            flat = lse[part].T[:PART_ROWS, :]
            high = flat.astype(jnp.bfloat16).astype(jnp.float32)
            middle = (flat - high).astype(jnp.bfloat16).astype(jnp.float32)
            row = lax.broadcasted_iota(jnp.int32, flat.shape, 0)
            out_ref[tokens:, lanes] = jnp.where(
                row == 0, high, jnp.where(row == 1, middle, jnp.where(row == 2, flat - high - middle, 0.0))
            ).astype(jnp.bfloat16)
        return peak

    blocks = count * per_chunk
    peak = low
    for t in range(tiles):
        peak = score_tile(0, t, score_a, peak)
    looped = 0
    if not last and per_chunk == 2 and count > 1:
        looped = blocks - 2

        def pair(i, peak):
            peak = one_block(2 * i, score_a, peak, 2 * i + 1, score_b)
            return one_block(2 * i + 1, score_b, peak, 2 * i + 2, score_a)

        peak = lax.fori_loop(0, looped // 2, pair, peak)
    for b in range(looped, blocks):
        scores, into = (score_a, score_b) if b % 2 == 0 else (score_b, score_a)
        peak = one_block(b, scores, peak, b + 1 if b + 1 < blocks else None, into)


def attend(meta, places, queries, keys, values, slots, shard, state, state_block, last):
    count = len(queries)
    tokens, width = queries[0].shape
    whole = keys.shape[0] > slots
    hd = keys.shape[1] // 2 if whole else keys.shape[1]
    rows = tokens * (width // hd)
    row_block = min(MAX_BLOCK, rows)
    key_tile = min(MAX_TILE, slots)
    holders = meta.shape[0] // 2 - places
    first = state is None

    def fixed(shape):
        return pl.BlockSpec(shape, lambda i, meta_ref: (0, 0))

    def shard_at(column):
        if not whole:
            return pl.BlockSpec((slots, hd), lambda i, meta_ref: (0, 0))
        return pl.BlockSpec(
            (slots, hd), lambda i, meta_ref: (meta_ref[2 * places + holders + shard], column)
        )

    in_specs = [fixed((tokens, width))] * count + [shard_at(0), shard_at(1)]
    operands = [meta, *queries, keys, values]
    if not first:
        in_specs += [pl.BlockSpec((count * rows, hd), lambda i, meta_ref: (state_block, 0))] * 2
        operands += state
    if last:
        out_shape = [jax.ShapeDtypeStruct((tokens + PART_ROWS, width), jnp.bfloat16)] * count
        out_specs = [fixed((tokens + PART_ROWS, width))] * count
    else:
        out_shape = [jax.ShapeDtypeStruct((count * rows, hd), jnp.float32)] * 2
        out_specs = [fixed((count * rows, hd))] * 2
    return pl.pallas_call(
        functools.partial(attend_kernel, count, first, last, shard, places),
        grid_spec=pltpu.PrefetchScalarGridSpec(
            num_scalar_prefetch=1,
            grid=(1,),
            in_specs=in_specs,
            out_specs=out_specs,
            scratch_shapes=[
                pltpu.VMEM((count * rows, 2 * hd), jnp.bfloat16),
                pltpu.VMEM((slots, 2 * hd), jnp.bfloat16),
                pltpu.VMEM((slots, 2 * hd), jnp.bfloat16),
                pltpu.VMEM((slots // key_tile, row_block, key_tile), jnp.float32),
                pltpu.VMEM((slots // key_tile, row_block, key_tile), jnp.float32),
            ],
        ),
        out_shape=out_shape,
        compiler_params=pltpu.CompilerParams(vmem_limit_bytes=VMEM),
        cost_estimate=pl.CostEstimate(
            flops=4 * count * rows * slots * hd,
            bytes_accessed=4 * slots * hd,
            transcendentals=count * rows * slots,
        ),
        name="attend_last" if last else "attend",
    )(*operands)


def combine_kernel(capacity, meta_ref, q_ref, k_ref, v_ref, *refs):
    *part_refs, out_ref, stacked = refs
    _, tokens, hd = k_ref.shape
    width = q_ref.shape[2]
    heads = width // hd
    scale = LOG2E / math.sqrt(hd)
    places = len(part_refs) * capacity
    for i, part_ref in enumerate(part_refs):
        for slot in range(capacity):
            r = meta_ref[i * capacity + slot]

            @pl.when(meta_ref[places + i * capacity + slot] > 0)
            def _(r=r, part_ref=part_ref, slot=slot):
                for h in range(heads):
                    stacked[h * tokens : (h + 1) * tokens, :] = q_ref[r, :, h * hd : (h + 1) * hd]
                s = nt_dot(stacked[...], k_ref[r]) * scale
                row = lax.broadcasted_iota(jnp.int32, s.shape, 0) % tokens
                seen = row >= lax.broadcasted_iota(jnp.int32, s.shape, 1)
                s = jnp.where(seen, s, MASKED)
                m = jnp.max(s, axis=1, keepdims=True)
                w = jnp.where(seen, jnp.exp2(s - m), 0.0)
                total = jnp.sum(w, axis=1, keepdims=True)
                o = jnp.dot(w.astype(jnp.bfloat16), v_ref[r], preferred_element_type=jnp.float32)
                base = part_ref.shape[0] - PART_ROWS
                for h in range(heads):
                    rows = slice(h * tokens, (h + 1) * tokens)
                    lanes = slice(h * hd, (h + 1) * hd)
                    far = part_ref[slot * tokens : (slot + 1) * tokens, lanes].astype(jnp.float32)
                    pieces = part_ref[base:, lanes].astype(jnp.float32)
                    flat = pieces[0:1] + pieces[1:2] + pieces[2:3]
                    lse = jnp.broadcast_to(flat, (hd, hd)).T[slot * tokens : (slot + 1) * tokens, :]
                    top = jnp.maximum(m[rows], lse)
                    own_scale = jnp.exp2(m[rows] - top)
                    far_scale = jnp.exp2(lse - top)
                    out_ref[r, :, lanes] = (
                        (own_scale * o[rows] + far_scale * far) / (own_scale * total[rows] + far_scale)
                    ).astype(jnp.bfloat16)


def combine(meta, capacity, q, keys, values, parts):
    responses, tokens, width = q.shape
    hd = keys.shape[-1]
    heads = width // hd
    return pl.pallas_call(
        functools.partial(combine_kernel, capacity),
        out_shape=jax.ShapeDtypeStruct(q.shape, jnp.bfloat16),
        in_specs=[pl.BlockSpec(memory_space=pltpu.SMEM)]
        + [pl.BlockSpec(memory_space=pltpu.VMEM)] * (3 + len(parts)),
        out_specs=pl.BlockSpec(memory_space=pltpu.VMEM),
        scratch_shapes=[pltpu.VMEM((heads * tokens, hd), jnp.bfloat16)],
        compiler_params=pltpu.CompilerParams(vmem_limit_bytes=VMEM),
        cost_estimate=pl.CostEstimate(
            flops=4 * responses * heads * tokens * tokens * hd,
            bytes_accessed=8 * responses * tokens * width,
            transcendentals=responses * heads * tokens * tokens,
        ),
        name="combine",
    )(meta, q, keys, values, *parts)


def multiply_kernel(kept_first_ref, *refs):
    *row_refs, weight_ref, kept_ref, sent_ref, rows = refs
    count = row_refs[0].shape[0]

    @pl.when(pl.program_id(0) == 0)
    def _():
        for first, order in ((1, (0, 1, 2, 3)), (0, (2, 3, 0, 1))):

            @pl.when(kept_first_ref[0] == first)
            def _(order=order):
                for place, i in enumerate(order):
                    rows[place * count : (place + 1) * count, :] = row_refs[i][...]

    for place, ref in ((1, sent_ref), (0, kept_ref)):
        for part in range(2):
            at = slice(part * count, (part + 1) * count)
            x = rows[2 * place * count + part * count : 2 * place * count + (part + 1) * count, :]
            ref[at, :] = jnp.dot(x, weight_ref[0], preferred_element_type=jnp.float32).astype(ref.dtype)


def multiply(kept_first, row_parts, weights):
    count, depth = row_parts[0].shape
    blocks, _, width = weights.shape
    rows = pl.BlockSpec((count, depth), lambda j: (0, 0))
    out = pl.BlockSpec((2 * count, width), lambda j: (0, j))
    return pl.pallas_call(
        multiply_kernel,
        grid=(blocks,),
        out_shape=[jax.ShapeDtypeStruct((2 * count, blocks * width), jnp.bfloat16)] * 2,
        in_specs=[pl.BlockSpec(memory_space=pltpu.SMEM)]
        + [rows] * 4
        + [pl.BlockSpec((1, depth, width), lambda j: (j, 0, 0))],
        out_specs=[out] * 2,
        scratch_shapes=[pltpu.VMEM((4 * count, depth), jnp.bfloat16)],
        compiler_params=pltpu.CompilerParams(vmem_limit_bytes=VMEM),
        cost_estimate=pl.CostEstimate(
            flops=8 * count * depth * blocks * width,
            bytes_accessed=2 * blocks * depth * width,
            transcendentals=0,
        ),
        name="multiply",
    )(kept_first.reshape(1), *row_parts, weights)


def project(rows, weights, plane, holder):
    group = lax.axis_index("kvh")
    chip = group // 2
    same = group % 2 == plane % 2
    parts = 2
    count = rows.shape[0] // parts
    width = weights.shape[2]

    def send(x, to, keep=lambda p, k: True):
        pairs = []
        for p in range(4):
            for h in range(2):
                for k in range(4):
                    if keep(p, k):
                        q, g, m = to(p, h, k)
                        pairs.append(((p * 2 + h) * 4 + k, (q * 2 + g) * 4 + m))
        return lax.ppermute(x, ("ctx", "kvh"), pairs)

    def fetch(x):
        return (
            x,
            send(x, lambda p, h, k: (p, 1 - h, k)),
            send(x, lambda p, h, k: (p ^ 1, h, k)),
            send(x, lambda p, h, k: (p ^ 1, 1 - h, k)),
        )

    def add(a, b):
        return (a.astype(jnp.float32) + b.astype(jnp.float32)).astype(jnp.bfloat16)

    def results(fetched):
        kept, sent = multiply(same.astype(jnp.int32), fetched, weights)
        total = add(kept, send(sent, lambda p, h, k: (p, h, k ^ 1)))
        low, high = total[:, :width], total[:, width:]
        away = send(jnp.where(chip == 0, high, low), lambda p, h, k: (p, h, k ^ 2))
        return add(jnp.where(chip == 0, low, high), away)

    def deliver(total):
        direct = send(
            total[:count], lambda p, h, k: (p ^ 1, h, k ^ 1), lambda p, k: k % 2 != p % 2
        )
        back = send(
            total[count:],
            lambda p, h, k: (p, 1 - h, k) if k % 2 == p % 2 else (p ^ 1, 1 - h, k ^ 1),
        )
        mine = jnp.where(same, total[:count], direct)
        return jnp.where(
            holder == 0,
            jnp.concatenate([mine, back], axis=1),
            jnp.concatenate([back, mine], axis=1),
        )

    fetched = [fetch(rows[i * count : (i + 1) * count]) for i in range(parts)]
    return jnp.concatenate([deliver(results(x)) for x in fetched], axis=0)


def local(
    queries, resp_keys, resp_values, prefix_keys, prefix_values, prefix_len, prompt_of, out_weight
):
    ctx_count = lax.axis_size("ctx")
    kvh_count = lax.axis_size("kvh")
    position = lax.axis_index("ctx")
    own_queries = queries[:, :, 0]
    own_keys = resp_keys[:, :, 0]
    own_values = resp_values[:, :, 0]
    resp_count, tokens_each, width = own_queries.shape
    slot_count = prefix_keys.shape[0]
    prompts = prefix_len.shape[0]
    holders = ctx_count // prompts
    my_prompt = position // holders
    my_holder = position % holders
    capacity = max(LANES // tokens_each, resp_count // prompts)
    places = prompts * capacity
    by_plane = kvh_count == prompts == 4 and holders == 2

    def cross(x, i):
        pairs = [(p * holders + h, (p ^ i) * holders + h) for p in range(prompts) for h in range(holders)]
        return lax.ppermute(x, "ctx", pairs)

    chunks, meta = pack(prompt_of, prefix_len, own_queries, capacity, holders, slot_count)
    chunks = chunks[:1] + [cross(x, i) for i, x in enumerate(chunks) if i > 0]
    near = prefix_keys[:, 0], prefix_values[:, 0]
    away = chunks[:0:-1]
    if by_plane:
        pairs = [[p * holders + h, (p + 2) * holders + h] for p in range(2) for h in range(holders)]
        weights = lax.all_gather(
            out_weight, "ctx", axis=0, tiled=False, axis_index_groups=pairs
        )
        shards = [near, near]
        shards[1] = [
            lax.ppermute(x, "ctx", [(c, c ^ 1) for c in range(ctx_count)]) for x in shards[1]
        ]
    else:
        lines = [[p * holders + h for h in range(holders)] for p in range(prompts)]
        joined = jnp.concatenate(near, axis=1)
        joined = lax.all_gather(joined, "ctx", axis=0, tiled=True, axis_index_groups=lines)
        shards = [near] + [(joined, joined)] * (holders - 1)

    state_home = state_away = None
    for shard in range(holders - 1):
        kv = shards[shard]
        state_home = attend(meta, places, chunks[:1], *kv, slot_count, shard, state_home, 0, False)
        state_home, away = lax.optimization_barrier((state_home, away))
        state_away = attend(meta, places, away, *kv, slot_count, shard, state_away, 0, False)
    shard = holders - 1
    far = shards[shard]
    done = [None] * prompts
    for where, members in enumerate([range(prompts - 1, 1, -1), [1]]):
        queries_now = [away[prompts - 1 - i] for i in members]
        block = 0 if where == 0 else prompts - 2
        results = attend(meta, places, queries_now, *far, slot_count, shard, state_away, block, True)
        for i, x in zip(members, results):
            done[i] = cross(x, i)
    (done[0],) = attend(meta, places, chunks[:1], *far, slot_count, shard, state_home, 0, True)
    attended = combine(meta, capacity, own_queries, own_keys, own_values, done)
    rows = attended.reshape(resp_count * tokens_each, width)

    if by_plane:
        projected = project(rows, weights, my_prompt, my_holder)
    else:
        weights = lax.all_gather(out_weight, "ctx", axis=1, tiled=True)
        terms = jnp.dot(rows, weights, preferred_element_type=jnp.float32)
        projected = lax.psum_scatter(
            terms.astype(jnp.bfloat16), "kvh", scatter_dimension=1, tiled=True
        )
    return (attended[:, :, None, :], projected)


def solution(mesh):
    in_specs = (
        P("ctx", None, "kvh", None),
        P("ctx", None, "kvh", None),
        P("ctx", None, "kvh", None),
        P("ctx", "kvh", None),
        P("ctx", "kvh", None),
        P(),
        P(),
        P("kvh", "ctx"),
    )
    out_specs = (P("ctx", None, "kvh", None), P("ctx", "kvh"))
    return jax.shard_map(local, mesh=mesh, in_specs=in_specs, out_specs=out_specs, check_vma=False)
```

```python
import functools
import math

import jax
import jax.numpy as jnp
from jax import lax
from jax.experimental import pallas as pl
from jax.experimental.pallas import tpu as pltpu
from jax.sharding import PartitionSpec as P

MASKED = -1e30
LOG2E = math.log2(math.e)
LANES = 128
PART_ROWS = 16
MAX_TILE = 1024
MAX_BLOCK = 256
VMEM = 60 * 1024 * 1024


def nt_dot(a, b):
    return lax.dot_general(a, b, (((1,), (1,)), ((), ())), preferred_element_type=jnp.float32)


def after(x, *others):
    return lax.optimization_barrier((x, *others))[0]


def pack_kernel(capacity, holders, slots, prompt_ref, len_ref, q_ref, *refs):
    *chunk_refs, meta_ref = refs
    responses, tokens, _ = q_ref.shape
    position = lax.axis_index("ctx")
    mine, holder = position // holders, position % holders
    named = [prompt_ref[position * responses + r] for r in range(responses)]
    ranks = []
    for r in range(responses):
        rank = jnp.int32(0)
        for before in range(r):
            rank += (named[before] == named[r]).astype(jnp.int32)
        ranks.append(rank)
    places = len(chunk_refs) * capacity
    for i, chunk_ref in enumerate(chunk_refs):
        for slot in range(capacity):
            chosen, present = jnp.int32(0), jnp.int32(0)
            for r in range(responses):
                hit = ((named[r] == mine ^ i) & (ranks[r] == slot)).astype(jnp.int32)
                chosen += hit * r
                present += hit
            meta_ref[i * capacity + slot] = chosen
            meta_ref[places + i * capacity + slot] = present
            rows = slice(slot * tokens, (slot + 1) * tokens)
            chunk_ref[rows, :] = q_ref[chosen]

            @pl.when(present == 0)
            def _(chunk_ref=chunk_ref, rows=rows):
                chunk_ref[rows, :] = jnp.zeros_like(chunk_ref[rows, :])

    length = len_ref[mine]
    for j in range(holders):
        place = (holder + j) % holders
        meta_ref[2 * places + j] = jnp.clip(length - place * slots, 0, slots)
        meta_ref[2 * places + holders + j] = place


def pack(prompt_of, prefix_len, q, capacity, holders, slots):
    _, tokens, width = q.shape
    prompts = prefix_len.shape[0]
    smem = pl.BlockSpec(memory_space=pltpu.SMEM)
    vmem = pl.BlockSpec(memory_space=pltpu.VMEM)
    *chunks, meta = pl.pallas_call(
        functools.partial(pack_kernel, capacity, holders, slots),
        out_shape=[jax.ShapeDtypeStruct((capacity * tokens, width), q.dtype)] * prompts
        + [jax.ShapeDtypeStruct((2 * (prompts * capacity + holders),), jnp.int32)],
        in_specs=[smem, smem, vmem],
        out_specs=[vmem] * prompts + [smem],
        compiler_params=pltpu.CompilerParams(vmem_limit_bytes=VMEM),
        cost_estimate=pl.CostEstimate(flops=0, bytes_accessed=4 * q.size, transcendentals=0),
        name="pack",
    )(prompt_of, prefix_len, q)
    return chunks, meta


def attend_kernel(count, first, last, shard, places, meta_ref, *refs):
    q_refs, (k_ref, v_ref, *refs) = refs[:count], refs[count:]
    if not first:
        prev_o_ref, prev_lse_ref, *refs = refs
    if last:
        out_refs, refs = refs[:count], refs[count:]
    else:
        o_ref, lse_ref, *refs = refs
    qext, kext, vext, score_a, score_b = refs
    tokens = q_refs[0].shape[0]
    slots, hd = k_ref.shape
    heads = q_refs[0].shape[1] // hd
    scale = LOG2E / math.sqrt(hd)
    tiles, row_block, key_tile = score_a.shape
    per_chunk = heads * tokens // row_block
    live = meta_ref[2 * places + shard]

    @pl.when(live == slots)
    def _():
        for t in range(tiles):
            at = slice(t * key_tile, (t + 1) * key_tile)
            keys = k_ref[at, :]
            kext[at, :hd] = keys
            kext[at, hd:] = keys
            vext[at, :hd] = v_ref[at, :]
            vext[at, hd:] = jnp.ones((key_tile, hd), jnp.bfloat16)

    @pl.when(live != slots)
    def _():
        def prepare(step, carry):
            at = pl.ds(pl.multiple_of(step * key_tile, key_tile), key_tile)
            alive = step * key_tile + lax.broadcasted_iota(jnp.int32, (key_tile, hd), 0) < live
            keys = jnp.where(alive, k_ref[at, :].astype(jnp.float32), k_ref[0:1, :].astype(jnp.float32))
            keys = keys.astype(jnp.bfloat16)
            kext[at, :hd] = keys
            kext[at, hd:] = keys
            vext[at, :hd] = jnp.where(alive, v_ref[at, :].astype(jnp.float32), 0.0).astype(jnp.bfloat16)
            vext[at, hd:] = jnp.where(alive, 1.0, 0.0).astype(jnp.bfloat16)
            return carry

        lax.fori_loop(0, tiles, prepare, 0)

    for c, q_ref in enumerate(q_refs):
        for h in range(heads):
            rows = slice((c * heads + h) * tokens, (c * heads + h + 1) * tokens)
            x = q_ref[:, h * hd : (h + 1) * hd].astype(jnp.float32) * scale
            high = x.astype(jnp.bfloat16)
            qext[rows, :hd] = high
            qext[rows, hd:] = (x - high.astype(jnp.float32)).astype(jnp.bfloat16)

    low = jnp.full((row_block, LANES), MASKED, jnp.float32)

    def rows_of(b):
        if isinstance(b, int):
            return slice(b * row_block, (b + 1) * row_block)
        return pl.ds(pl.multiple_of(b * row_block, row_block), row_block)

    def score_tile(b, t, into, peak):
        s = nt_dot(qext[rows_of(b), :], kext[t * key_tile : (t + 1) * key_tile, :])
        into[t] = s
        for j in range(key_tile // LANES):
            peak = jnp.maximum(peak, s[:, j * LANES : (j + 1) * LANES])
        return peak

    def one_block(b, scores, peak, following, into):
        m = jnp.max(peak, axis=1, keepdims=True)
        peak = low
        acc = jnp.zeros((row_block, 2 * hd), jnp.float32)
        for t in range(tiles):
            if following is not None:
                peak = score_tile(following, t, into, peak)
            w = jnp.exp2(scores[t] - m).astype(jnp.bfloat16)
            acc = acc + jnp.dot(
                w, vext[t * key_tile : (t + 1) * key_tile, :], preferred_element_type=jnp.float32
            )
        total = acc[:, hd:]
        some = total > 0.0
        safe = jnp.where(some, total, 1.0)
        o = acc[:, :hd] / safe
        lse = jnp.where(some, m + jnp.log2(safe), MASKED)
        rows = rows_of(b)
        if not first:
            before = prev_lse_ref[rows, :]
            top = jnp.maximum(before, lse)
            w_before = jnp.exp2(before - top)
            w_now = jnp.exp2(lse - top)
            both = w_before + w_now
            o = (w_before * prev_o_ref[rows, :] + w_now * o) / both
            lse = top + jnp.log2(both)
        if not last:
            o_ref[rows, :] = o
            lse_ref[rows, :] = lse
            return peak
        out_ref = out_refs[b // per_chunk]
        for j in range(row_block // tokens):
            h = (b % per_chunk) * (row_block // tokens) + j
            part = slice(j * tokens, (j + 1) * tokens)
            lanes = slice(h * hd, (h + 1) * hd)
            out_ref[:tokens, lanes] = o[part].astype(jnp.bfloat16)
            flat = lse[part].T[:PART_ROWS, :]
            high = flat.astype(jnp.bfloat16).astype(jnp.float32)
            middle = (flat - high).astype(jnp.bfloat16).astype(jnp.float32)
            row = lax.broadcasted_iota(jnp.int32, flat.shape, 0)
            out_ref[tokens:, lanes] = jnp.where(
                row == 0, high, jnp.where(row == 1, middle, jnp.where(row == 2, flat - high - middle, 0.0))
            ).astype(jnp.bfloat16)
        return peak

    blocks = count * per_chunk
    peak = low
    for t in range(tiles):
        peak = score_tile(0, t, score_a, peak)
    looped = 0
    if not last and per_chunk % 2 == 0 and count > 1:
        looped = blocks - 2

        def pair(i, peak):
            peak = one_block(2 * i, score_a, peak, 2 * i + 1, score_b)
            return one_block(2 * i + 1, score_b, peak, 2 * i + 2, score_a)

        peak = lax.fori_loop(0, looped // 2, pair, peak)
    for b in range(looped, blocks):
        scores, into = (score_a, score_b) if b % 2 == 0 else (score_b, score_a)
        peak = one_block(b, scores, peak, b + 1 if b + 1 < blocks else None, into)


def attend(meta, places, queries, keys, values, slots, shard, state, state_block, last):
    count = len(queries)
    tokens, width = queries[0].shape
    whole = keys.shape[0] > slots
    hd = keys.shape[1] // 2 if whole else keys.shape[1]
    rows = tokens * (width // hd)
    row_block = min(MAX_BLOCK, rows)
    key_tile = min(MAX_TILE, slots)
    holders = meta.shape[0] // 2 - places
    first = state is None

    def fixed(shape):
        return pl.BlockSpec(shape, lambda i, meta_ref: (0, 0))

    def shard_at(column):
        if not whole:
            return pl.BlockSpec((slots, hd), lambda i, meta_ref: (0, 0))
        return pl.BlockSpec(
            (slots, hd), lambda i, meta_ref: (meta_ref[2 * places + holders + shard], column)
        )

    in_specs = [fixed((tokens, width))] * count + [shard_at(0), shard_at(1)]
    operands = [meta, *queries, keys, values]
    if not first:
        in_specs += [pl.BlockSpec((count * rows, hd), lambda i, meta_ref: (state_block, 0))] * 2
        operands += state
    if last:
        out_shape = [jax.ShapeDtypeStruct((tokens + PART_ROWS, width), jnp.bfloat16)] * count
        out_specs = [fixed((tokens + PART_ROWS, width))] * count
    else:
        out_shape = [jax.ShapeDtypeStruct((count * rows, hd), jnp.float32)] * 2
        out_specs = [fixed((count * rows, hd))] * 2
    return pl.pallas_call(
        functools.partial(attend_kernel, count, first, last, shard, places),
        grid_spec=pltpu.PrefetchScalarGridSpec(
            num_scalar_prefetch=1,
            grid=(1,),
            in_specs=in_specs,
            out_specs=out_specs,
            scratch_shapes=[
                pltpu.VMEM((count * rows, 2 * hd), jnp.bfloat16),
                pltpu.VMEM((slots, 2 * hd), jnp.bfloat16),
                pltpu.VMEM((slots, 2 * hd), jnp.bfloat16),
                pltpu.VMEM((slots // key_tile, row_block, key_tile), jnp.float32),
                pltpu.VMEM((slots // key_tile, row_block, key_tile), jnp.float32),
            ],
        ),
        out_shape=out_shape,
        compiler_params=pltpu.CompilerParams(vmem_limit_bytes=VMEM),
        cost_estimate=pl.CostEstimate(
            flops=4 * rows * slots * hd if first and count == 1 else 0,
            bytes_accessed=0,
            transcendentals=0,
        ),
        name="attend_last" if last else "attend",
    )(*operands)


def combine_kernel(capacity, meta_ref, q_ref, k_ref, v_ref, *refs):
    *part_refs, out_ref, stacked = refs
    _, tokens, hd = k_ref.shape
    width = q_ref.shape[2]
    heads = width // hd
    scale = LOG2E / math.sqrt(hd)
    places = len(part_refs) * capacity
    for i, part_ref in enumerate(part_refs):
        for slot in range(capacity):
            r = meta_ref[i * capacity + slot]

            @pl.when(meta_ref[places + i * capacity + slot] > 0)
            def _(r=r, part_ref=part_ref, slot=slot):
                for h in range(heads):
                    stacked[h * tokens : (h + 1) * tokens, :] = q_ref[r, :, h * hd : (h + 1) * hd]
                s = nt_dot(stacked[...], k_ref[r]) * scale
                row = lax.broadcasted_iota(jnp.int32, s.shape, 0) % tokens
                seen = row >= lax.broadcasted_iota(jnp.int32, s.shape, 1)
                s = jnp.where(seen, s, MASKED)
                m = jnp.max(s, axis=1, keepdims=True)
                w = jnp.where(seen, jnp.exp2(s - m), 0.0)
                total = jnp.sum(w, axis=1, keepdims=True)
                o = jnp.dot(w.astype(jnp.bfloat16), v_ref[r], preferred_element_type=jnp.float32)
                base = part_ref.shape[0] - PART_ROWS
                for h in range(heads):
                    rows = slice(h * tokens, (h + 1) * tokens)
                    lanes = slice(h * hd, (h + 1) * hd)
                    far = part_ref[slot * tokens : (slot + 1) * tokens, lanes].astype(jnp.float32)
                    pieces = part_ref[base:, lanes].astype(jnp.float32)
                    flat = pieces[0:1] + pieces[1:2] + pieces[2:3]
                    lse = jnp.broadcast_to(flat, (hd, hd)).T[slot * tokens : (slot + 1) * tokens, :]
                    top = jnp.maximum(m[rows], lse)
                    own_scale = jnp.exp2(m[rows] - top)
                    far_scale = jnp.exp2(lse - top)
                    out_ref[r, :, lanes] = (
                        (own_scale * o[rows] + far_scale * far) / (own_scale * total[rows] + far_scale)
                    ).astype(jnp.bfloat16)


def combine(meta, capacity, q, keys, values, parts):
    responses, tokens, width = q.shape
    hd = keys.shape[-1]
    heads = width // hd
    return pl.pallas_call(
        functools.partial(combine_kernel, capacity),
        out_shape=jax.ShapeDtypeStruct(q.shape, jnp.bfloat16),
        in_specs=[pl.BlockSpec(memory_space=pltpu.SMEM)]
        + [pl.BlockSpec(memory_space=pltpu.VMEM)] * (3 + len(parts)),
        out_specs=pl.BlockSpec(memory_space=pltpu.VMEM),
        scratch_shapes=[pltpu.VMEM((heads * tokens, hd), jnp.bfloat16)],
        compiler_params=pltpu.CompilerParams(vmem_limit_bytes=VMEM),
        cost_estimate=pl.CostEstimate(flops=0, bytes_accessed=0, transcendentals=0),
        name="combine",
    )(meta, q, keys, values, *parts)


def multiply_kernel(kept_first_ref, *refs):
    *row_refs, weight_ref, kept_ref, sent_ref, rows = refs
    count = row_refs[0].shape[0]

    @pl.when(pl.program_id(0) == 0)
    def _():
        for first, order in ((1, (0, 1, 2, 3)), (0, (2, 3, 0, 1))):

            @pl.when(kept_first_ref[0] == first)
            def _(order=order):
                for place, i in enumerate(order):
                    rows[place * count : (place + 1) * count, :] = row_refs[i][...]

    for place, ref in ((1, sent_ref), (0, kept_ref)):
        for part in range(2):
            at = slice(part * count, (part + 1) * count)
            x = rows[2 * place * count + part * count : 2 * place * count + (part + 1) * count, :]
            ref[at, :] = jnp.dot(x, weight_ref[0], preferred_element_type=jnp.float32).astype(ref.dtype)


def multiply(kept_first, row_parts, weights, width, piece):
    count, depth = row_parts[0].shape
    blocks = weights.shape[0]
    rows = pl.BlockSpec((count, depth), lambda j: (0, 0))
    out = pl.BlockSpec((2 * count, width), lambda j: (0, j))
    return pl.pallas_call(
        multiply_kernel,
        grid=(blocks,),
        out_shape=[jax.ShapeDtypeStruct((2 * count, blocks * width), jnp.bfloat16)] * 2,
        in_specs=[pl.BlockSpec(memory_space=pltpu.SMEM)]
        + [rows] * 4
        + [pl.BlockSpec((1, depth, width), lambda j: (j, 0, piece))],
        out_specs=[out] * 2,
        scratch_shapes=[pltpu.VMEM((4 * count, depth), jnp.bfloat16)],
        compiler_params=pltpu.CompilerParams(vmem_limit_bytes=VMEM),
        cost_estimate=pl.CostEstimate(flops=0, bytes_accessed=0, transcendentals=0),
        name="multiply",
    )(kept_first.reshape(1), *row_parts, weights)


def arrange_kernel(pieces, flags_ref, *refs):
    *parts, out_ref = refs
    own, direct, back = parts[:pieces], parts[pieces : 2 * pieces], parts[2 * pieces :]
    count, width = back[0].shape
    for holder in range(2):

        @pl.when(flags_ref[1] == holder)
        def _(holder=holder):
            for i in range(pieces):
                here = slice((holder * pieces + i) * width, (holder * pieces + i + 1) * width)
                there = slice(((1 - holder) * pieces + i) * width, ((1 - holder) * pieces + i + 1) * width)
                out_ref[:, there] = back[i][...]

                @pl.when(flags_ref[0] != 0)
                def _(here=here, i=i):
                    out_ref[:, here] = own[i][:count, :]

                @pl.when(flags_ref[0] == 0)
                def _(here=here, i=i):
                    out_ref[:, here] = direct[i][...]


def arrange(same, holder, own, direct, back):
    count, width = back[0].shape
    pieces = len(back)
    vmem = pl.BlockSpec(memory_space=pltpu.VMEM)
    return pl.pallas_call(
        functools.partial(arrange_kernel, pieces),
        out_shape=jax.ShapeDtypeStruct((count, 2 * pieces * width), back[0].dtype),
        in_specs=[pl.BlockSpec(memory_space=pltpu.SMEM)] + [vmem] * (3 * pieces),
        out_specs=vmem,
        compiler_params=pltpu.CompilerParams(vmem_limit_bytes=VMEM),
        cost_estimate=pl.CostEstimate(flops=0, bytes_accessed=0, transcendentals=0),
        name="arrange",
    )(jnp.stack([same.astype(jnp.int32), holder.astype(jnp.int32)]), *own, *direct, *back)


def project(rows, weights, plane, holder):
    group = lax.axis_index("kvh")
    chip = group // 2
    same = group % 2 == plane % 2
    count = rows.shape[0]
    pieces = 4
    width = weights.shape[2] // pieces

    def send(x, to, keep=lambda p, k: True):
        pairs = []
        for p in range(4):
            for h in range(2):
                for k in range(4):
                    if keep(p, k):
                        q, g, m = to(p, h, k)
                        pairs.append(((p * 2 + h) * 4 + k, (q * 2 + g) * 4 + m))
        return lax.ppermute(x, ("ctx", "kvh"), pairs)

    def fetch(x):
        return (
            x,
            send(x, lambda p, h, k: (p, 1 - h, k)),
            send(x, lambda p, h, k: (p ^ 1, h, k)),
            send(x, lambda p, h, k: (p ^ 1, 1 - h, k)),
        )

    def add(a, b):
        return (a.astype(jnp.float32) + b.astype(jnp.float32)).astype(jnp.bfloat16)

    def chip_sums(fetched, piece):
        kept, sent = multiply(same.astype(jnp.int32), fetched, weights, width, piece)
        total = add(kept, send(sent, lambda p, h, k: (p, h, k ^ 1)))
        low, high = total[:, :width], total[:, width:]
        return jnp.where(chip == 0, low, high), jnp.where(chip == 0, high, low)

    def deliver(total):
        direct = send(
            total[:count], lambda p, h, k: (p ^ 1, h, k ^ 1), lambda p, k: k % 2 != p % 2
        )
        back = send(
            total[count:],
            lambda p, h, k: (p, 1 - h, k) if k % 2 == p % 2 else (p ^ 1, 1 - h, k ^ 1),
        )
        return total, direct, back

    fetched = fetch(rows)
    sums, delivered = [], []
    for piece in range(pieces):
        if piece >= 2:
            fetched = lax.optimization_barrier((fetched, sums[piece - 2]))[0]
        sums.append(chip_sums(fetched, piece))
    for kept, sent in sums:
        got = send(sent, lambda p, h, k: (p, h, k ^ 2))
        delivered.append(deliver(add(kept, got)))
    return arrange(same, holder, *zip(*delivered))


def local(
    queries, resp_keys, resp_values, prefix_keys, prefix_values, prefix_len, prompt_of, out_weight
):
    ctx_count = lax.axis_size("ctx")
    kvh_count = lax.axis_size("kvh")
    position = lax.axis_index("ctx")
    own_queries = queries[:, :, 0]
    own_keys = resp_keys[:, :, 0]
    own_values = resp_values[:, :, 0]
    resp_count, tokens_each, width = own_queries.shape
    slot_count = prefix_keys.shape[0]
    prompts = prefix_len.shape[0]
    holders = ctx_count // prompts
    my_prompt = position // holders
    my_holder = position % holders
    capacity = max(LANES // tokens_each, resp_count // prompts)
    places = prompts * capacity
    by_plane = kvh_count == prompts == 4 and holders == 2

    def cross(x, i):
        pairs = [(p * holders + h, (p ^ i) * holders + h) for p in range(prompts) for h in range(holders)]
        return lax.ppermute(x, "ctx", pairs)

    chunks, meta = pack(prompt_of, prefix_len, own_queries, capacity, holders, slot_count)
    chunks = chunks[:1] + [cross(x, i) for i, x in enumerate(chunks) if i > 0]
    near = prefix_keys[:, 0], prefix_values[:, 0]
    away = chunks[:0:-1]
    if by_plane:
        pairs = [[p * holders + h, (p + 2) * holders + h] for p in range(2) for h in range(holders)]
        weights = lax.all_gather(
            after(out_weight, *away), "ctx", axis=0, tiled=False, axis_index_groups=pairs
        )
        shards = [near, near]
        shards[1] = [
            lax.ppermute(x, "ctx", [(c, c ^ 1) for c in range(ctx_count)]) for x in shards[1]
        ]
    else:
        lines = [[p * holders + h for h in range(holders)] for p in range(prompts)]
        joined = jnp.concatenate(near, axis=1)
        joined = lax.all_gather(joined, "ctx", axis=0, tiled=True, axis_index_groups=lines)
        shards = [near] + [(joined, joined)] * (holders - 1)

    state_home = state_away = None
    for shard in range(holders - 1):
        kv = shards[shard]
        state_home = attend(meta, places, chunks[:1], *kv, slot_count, shard, state_home, 0, False)
        state_home, away = lax.optimization_barrier((state_home, away))
        state_away = attend(meta, places, away, *kv, slot_count, shard, state_away, 0, False)
    shard = holders - 1
    far = shards[shard]
    done = [None] * prompts
    for where, members in enumerate([range(prompts - 1, 1, -1), [1]]):
        queries_now = [away[prompts - 1 - i] for i in members]
        block = 0 if where == 0 else prompts - 2
        results = attend(meta, places, queries_now, *far, slot_count, shard, state_away, block, True)
        for i, x in zip(members, results):
            done[i] = cross(x, i)
    (done[0],) = attend(meta, places, chunks[:1], *far, slot_count, shard, state_home, 0, True)
    attended = combine(meta, capacity, own_queries, own_keys, own_values, done)
    rows = attended.reshape(resp_count * tokens_each, width)

    if by_plane:
        projected = project(rows, weights, my_prompt, my_holder)
    else:
        weights = lax.all_gather(out_weight, "ctx", axis=1, tiled=True)
        terms = jnp.dot(rows, weights, preferred_element_type=jnp.float32)
        projected = lax.psum_scatter(
            terms.astype(jnp.bfloat16), "kvh", scatter_dimension=1, tiled=True
        )
    return (attended[:, :, None, :], projected)


def solution(mesh):
    in_specs = (
        P("ctx", None, "kvh", None),
        P("ctx", None, "kvh", None),
        P("ctx", None, "kvh", None),
        P("ctx", "kvh", None),
        P("ctx", "kvh", None),
        P(),
        P(),
        P("kvh", "ctx"),
    )
    out_specs = (P("ctx", None, "kvh", None), P("ctx", "kvh"))
    return jax.shard_map(local, mesh=mesh, in_specs=in_specs, out_specs=out_specs, check_vma=False)
```

```python
import functools
import math

import jax
import jax.numpy as jnp
from jax import lax
from jax.experimental import pallas as pl
from jax.experimental.pallas import tpu as pltpu
from jax.sharding import PartitionSpec as P

MASKED = -1e30
LOG2E = math.log2(math.e)
LANES = 128
PART_ROWS = 16
MAX_TILE = 1024
MAX_BLOCK = 512
MIB = 1024 * 1024


def nt_dot(a, b):
    return lax.dot_general(a, b, (((1,), (1,)), ((), ())), preferred_element_type=jnp.float32)


def after(x, *others):
    return lax.optimization_barrier((x, *others))[0]


def pack_kernel(capacity, holders, slots, prompt_ref, len_ref, q_ref, *refs):
    *chunk_refs, meta_ref = refs
    responses, tokens, _ = q_ref.shape
    position = lax.axis_index("ctx")
    mine, holder = position // holders, position % holders
    named = [prompt_ref[position * responses + r] for r in range(responses)]
    ranks = []
    for r in range(responses):
        rank = jnp.int32(0)
        for before in range(r):
            rank += (named[before] == named[r]).astype(jnp.int32)
        ranks.append(rank)
    places = len(chunk_refs) * capacity
    for i, chunk_ref in enumerate(chunk_refs):
        for slot in range(capacity):
            chosen, present = jnp.int32(0), jnp.int32(0)
            for r in range(responses):
                hit = ((named[r] == mine ^ i) & (ranks[r] == slot)).astype(jnp.int32)
                chosen += hit * r
                present += hit
            meta_ref[i * capacity + slot] = chosen
            meta_ref[places + i * capacity + slot] = present
            rows = slice(slot * tokens, (slot + 1) * tokens)
            chunk_ref[rows, :] = q_ref[chosen]

            @pl.when(present == 0)
            def _(chunk_ref=chunk_ref, rows=rows):
                chunk_ref[rows, :] = jnp.zeros_like(chunk_ref[rows, :])

    length = len_ref[mine]
    for j in range(holders):
        place = (holder + j) % holders
        meta_ref[2 * places + j] = jnp.clip(length - place * slots, 0, slots)
        meta_ref[2 * places + holders + j] = place


def pack(prompt_of, prefix_len, q, capacity, holders, slots):
    _, tokens, width = q.shape
    prompts = prefix_len.shape[0]
    smem = pl.BlockSpec(memory_space=pltpu.SMEM)
    vmem = pl.BlockSpec(memory_space=pltpu.VMEM)
    *chunks, meta = pl.pallas_call(
        functools.partial(pack_kernel, capacity, holders, slots),
        out_shape=[jax.ShapeDtypeStruct((capacity * tokens, width), q.dtype)] * prompts
        + [jax.ShapeDtypeStruct((2 * (prompts * capacity + holders),), jnp.int32)],
        in_specs=[smem, smem, vmem],
        out_specs=[vmem] * prompts + [smem],
        compiler_params=pltpu.CompilerParams(vmem_limit_bytes=16 * MIB),
        cost_estimate=pl.CostEstimate(flops=0, bytes_accessed=4 * q.size, transcendentals=0),
        name="pack",
    )(prompt_of, prefix_len, q)
    return chunks, meta


def attend_kernel(count, first, last, shard, places, meta_ref, *refs):
    q_refs, (k_ref, v_ref, *refs) = refs[:count], refs[count:]
    if not first:
        prev_o_ref, prev_lse_ref, *refs = refs
    if last:
        out_refs, refs = refs[:count], refs[count:]
    else:
        o_ref, lse_ref, *refs = refs
    qext, kext, vext, score_a, score_b = refs
    tokens = q_refs[0].shape[0]
    slots, hd = k_ref.shape
    heads = q_refs[0].shape[1] // hd
    scale = LOG2E / math.sqrt(hd)
    tiles, row_block, key_tile = score_a.shape
    per_chunk = heads * tokens // row_block
    live = meta_ref[2 * places + shard]

    @pl.when(live == slots)
    def _():
        for t in range(tiles):
            at = slice(t * key_tile, (t + 1) * key_tile)
            keys = k_ref[at, :]
            kext[at, :hd] = keys
            kext[at, hd:] = keys
            vext[at, :hd] = v_ref[at, :]
            vext[at, hd:] = jnp.ones((key_tile, hd), jnp.bfloat16)

    @pl.when(live != slots)
    def _():
        def prepare(step, carry):
            at = pl.ds(pl.multiple_of(step * key_tile, key_tile), key_tile)
            alive = step * key_tile + lax.broadcasted_iota(jnp.int32, (key_tile, hd), 0) < live
            keys = jnp.where(alive, k_ref[at, :].astype(jnp.float32), k_ref[0:1, :].astype(jnp.float32))
            keys = keys.astype(jnp.bfloat16)
            kext[at, :hd] = keys
            kext[at, hd:] = keys
            vext[at, :hd] = jnp.where(alive, v_ref[at, :].astype(jnp.float32), 0.0).astype(jnp.bfloat16)
            vext[at, hd:] = jnp.where(alive, 1.0, 0.0).astype(jnp.bfloat16)
            return carry

        lax.fori_loop(0, tiles, prepare, 0)

    for c, q_ref in enumerate(q_refs):
        for h in range(heads):
            rows = slice((c * heads + h) * tokens, (c * heads + h + 1) * tokens)
            x = q_ref[:, h * hd : (h + 1) * hd].astype(jnp.float32) * scale
            high = x.astype(jnp.bfloat16)
            qext[rows, :hd] = high
            qext[rows, hd:] = (x - high.astype(jnp.float32)).astype(jnp.bfloat16)

    low = jnp.full((row_block, LANES), MASKED, jnp.float32)

    def rows_of(b):
        if isinstance(b, int):
            return slice(b * row_block, (b + 1) * row_block)
        return pl.ds(pl.multiple_of(b * row_block, row_block), row_block)

    def score_tile(b, t, into, peak):
        s = nt_dot(qext[rows_of(b), :], kext[t * key_tile : (t + 1) * key_tile, :])
        into[t] = s
        for j in range(key_tile // LANES):
            peak = jnp.maximum(peak, s[:, j * LANES : (j + 1) * LANES])
        return peak

    def one_block(b, scores, peak, following, into):
        m = jnp.max(peak, axis=1, keepdims=True)
        peak = low
        acc = jnp.zeros((row_block, 2 * hd), jnp.float32)
        for t in range(tiles):
            if following is not None:
                peak = score_tile(following, t, into, peak)
            w = jnp.exp2(scores[t] - m).astype(jnp.bfloat16)
            acc = acc + jnp.dot(
                w, vext[t * key_tile : (t + 1) * key_tile, :], preferred_element_type=jnp.float32
            )
        total = acc[:, hd:]
        some = total > 0.0
        safe = jnp.where(some, total, 1.0)
        o = acc[:, :hd] / safe
        lse = jnp.where(some, m + jnp.log2(safe), MASKED)
        rows = rows_of(b)
        if not first:
            before = prev_lse_ref[rows, :]
            top = jnp.maximum(before, lse)
            w_before = jnp.exp2(before - top)
            w_now = jnp.exp2(lse - top)
            both = w_before + w_now
            o = (w_before * prev_o_ref[rows, :] + w_now * o) / both
            lse = top + jnp.log2(both)
        if not last:
            o_ref[rows, :] = o
            lse_ref[rows, :] = lse
            return peak
        out_ref = out_refs[b // per_chunk]
        for j in range(row_block // tokens):
            h = (b % per_chunk) * (row_block // tokens) + j
            part = slice(j * tokens, (j + 1) * tokens)
            lanes = slice(h * hd, (h + 1) * hd)
            out_ref[:tokens, lanes] = o[part].astype(jnp.bfloat16)
            flat = lse[part].T[:PART_ROWS, :]
            high = flat.astype(jnp.bfloat16).astype(jnp.float32)
            middle = (flat - high).astype(jnp.bfloat16).astype(jnp.float32)
            row = lax.broadcasted_iota(jnp.int32, flat.shape, 0)
            out_ref[tokens:, lanes] = jnp.where(
                row == 0, high, jnp.where(row == 1, middle, jnp.where(row == 2, flat - high - middle, 0.0))
            ).astype(jnp.bfloat16)
        return peak

    blocks = count * per_chunk
    peak = low
    for t in range(tiles):
        peak = score_tile(0, t, score_a, peak)
    looped = 0
    if not last and per_chunk % 2 == 0 and count > 1:
        looped = blocks - 2

        def pair(i, peak):
            peak = one_block(2 * i, score_a, peak, 2 * i + 1, score_b)
            return one_block(2 * i + 1, score_b, peak, 2 * i + 2, score_a)

        peak = lax.fori_loop(0, looped // 2, pair, peak)
    for b in range(looped, blocks):
        scores, into = (score_a, score_b) if b % 2 == 0 else (score_b, score_a)
        peak = one_block(b, scores, peak, b + 1 if b + 1 < blocks else None, into)


def attend(meta, places, queries, keys, values, slots, shard, state, state_block, last):
    count = len(queries)
    tokens, width = queries[0].shape
    whole = keys.shape[0] > slots
    hd = keys.shape[1] // 2 if whole else keys.shape[1]
    rows = tokens * (width // hd)
    row_block = min(MAX_BLOCK, rows)
    key_tile = min(MAX_TILE, slots)
    holders = meta.shape[0] // 2 - places
    first = state is None

    def fixed(shape):
        return pl.BlockSpec(shape, lambda i, meta_ref: (0, 0))

    def shard_at(column):
        if not whole:
            return pl.BlockSpec((slots, hd), lambda i, meta_ref: (0, 0))
        return pl.BlockSpec(
            (slots, hd), lambda i, meta_ref: (meta_ref[2 * places + holders + shard], column)
        )

    in_specs = [fixed((tokens, width))] * count + [shard_at(0), shard_at(1)]
    operands = [meta, *queries, keys, values]
    if not first:
        in_specs += [pl.BlockSpec((count * rows, hd), lambda i, meta_ref: (state_block, 0))] * 2
        operands += state
    if last:
        out_shape = [jax.ShapeDtypeStruct((tokens + PART_ROWS, width), jnp.bfloat16)] * count
        out_specs = [fixed((tokens + PART_ROWS, width))] * count
    else:
        out_shape = [jax.ShapeDtypeStruct((count * rows, hd), jnp.float32)] * 2
        out_specs = [fixed((count * rows, hd))] * 2
    return pl.pallas_call(
        functools.partial(attend_kernel, count, first, last, shard, places),
        grid_spec=pltpu.PrefetchScalarGridSpec(
            num_scalar_prefetch=1,
            grid=(1,),
            in_specs=in_specs,
            out_specs=out_specs,
            scratch_shapes=[
                pltpu.VMEM((count * rows, 2 * hd), jnp.bfloat16),
                pltpu.VMEM((slots, 2 * hd), jnp.bfloat16),
                pltpu.VMEM((slots, 2 * hd), jnp.bfloat16),
                pltpu.VMEM((slots // key_tile, row_block, key_tile), jnp.float32),
                pltpu.VMEM((slots // key_tile, row_block, key_tile), jnp.float32),
            ],
        ),
        out_shape=out_shape,
        compiler_params=pltpu.CompilerParams(vmem_limit_bytes=40 * MIB),
        cost_estimate=pl.CostEstimate(
            flops=4 * count * rows * slots * hd if first else 0,
            bytes_accessed=0,
            transcendentals=0,
        ),
        name="attend_last" if last else "attend",
    )(*operands)


def combine_kernel(capacity, meta_ref, q_ref, k_ref, v_ref, *refs):
    *part_refs, out_ref, stacked = refs
    _, tokens, hd = k_ref.shape
    width = q_ref.shape[2]
    heads = width // hd
    scale = LOG2E / math.sqrt(hd)
    places = len(part_refs) * capacity
    for i, part_ref in enumerate(part_refs):
        for slot in range(capacity):
            r = meta_ref[i * capacity + slot]

            @pl.when(meta_ref[places + i * capacity + slot] > 0)
            def _(r=r, part_ref=part_ref, slot=slot):
                for h in range(heads):
                    stacked[h * tokens : (h + 1) * tokens, :] = q_ref[r, :, h * hd : (h + 1) * hd]
                s = nt_dot(stacked[...], k_ref[r]) * scale
                row = lax.broadcasted_iota(jnp.int32, s.shape, 0) % tokens
                seen = row >= lax.broadcasted_iota(jnp.int32, s.shape, 1)
                s = jnp.where(seen, s, MASKED)
                m = jnp.max(s, axis=1, keepdims=True)
                w = jnp.where(seen, jnp.exp2(s - m), 0.0)
                total = jnp.sum(w, axis=1, keepdims=True)
                o = jnp.dot(w.astype(jnp.bfloat16), v_ref[r], preferred_element_type=jnp.float32)
                base = part_ref.shape[0] - PART_ROWS
                for h in range(heads):
                    rows = slice(h * tokens, (h + 1) * tokens)
                    lanes = slice(h * hd, (h + 1) * hd)
                    far = part_ref[slot * tokens : (slot + 1) * tokens, lanes].astype(jnp.float32)
                    pieces = part_ref[base:, lanes].astype(jnp.float32)
                    flat = pieces[0:1] + pieces[1:2] + pieces[2:3]
                    lse = jnp.broadcast_to(flat, (hd, hd)).T[slot * tokens : (slot + 1) * tokens, :]
                    top = jnp.maximum(m[rows], lse)
                    own_scale = jnp.exp2(m[rows] - top)
                    far_scale = jnp.exp2(lse - top)
                    out_ref[r, :, lanes] = (
                        (own_scale * o[rows] + far_scale * far) / (own_scale * total[rows] + far_scale)
                    ).astype(jnp.bfloat16)


def combine(meta, capacity, q, keys, values, parts):
    responses, tokens, width = q.shape
    hd = keys.shape[-1]
    heads = width // hd
    return pl.pallas_call(
        functools.partial(combine_kernel, capacity),
        out_shape=jax.ShapeDtypeStruct(q.shape, jnp.bfloat16),
        in_specs=[pl.BlockSpec(memory_space=pltpu.SMEM)]
        + [pl.BlockSpec(memory_space=pltpu.VMEM)] * (3 + len(parts)),
        out_specs=pl.BlockSpec(memory_space=pltpu.VMEM),
        scratch_shapes=[pltpu.VMEM((heads * tokens, hd), jnp.bfloat16)],
        compiler_params=pltpu.CompilerParams(vmem_limit_bytes=24 * MIB),
        cost_estimate=pl.CostEstimate(flops=0, bytes_accessed=0, transcendentals=0),
        name="combine",
    )(meta, q, keys, values, *parts)


def multiply_kernel(kept_first_ref, *refs):
    *row_refs, weight_ref, kept_ref, sent_ref, rows = refs
    count = row_refs[0].shape[0]

    @pl.when(pl.program_id(0) == 0)
    def _():
        for first, order in ((1, (0, 1, 2, 3)), (0, (2, 3, 0, 1))):

            @pl.when(kept_first_ref[0] == first)
            def _(order=order):
                for place, i in enumerate(order):
                    rows[place * count : (place + 1) * count, :] = row_refs[i][...]

    for place, ref in ((1, sent_ref), (0, kept_ref)):
        for part in range(2):
            at = slice(part * count, (part + 1) * count)
            x = rows[2 * place * count + part * count : 2 * place * count + (part + 1) * count, :]
            ref[at, :] = jnp.dot(x, weight_ref[0], preferred_element_type=jnp.float32).astype(ref.dtype)


def multiply(kept_first, row_parts, weights, width, piece):
    count, depth = row_parts[0].shape
    blocks = weights.shape[0]
    rows = pl.BlockSpec((count, depth), lambda j: (0, 0))
    out = pl.BlockSpec((2 * count, width), lambda j: (0, j))
    return pl.pallas_call(
        multiply_kernel,
        grid=(blocks,),
        out_shape=[jax.ShapeDtypeStruct((2 * count, blocks * width), jnp.bfloat16)] * 2,
        in_specs=[pl.BlockSpec(memory_space=pltpu.SMEM)]
        + [rows] * 4
        + [pl.BlockSpec((1, depth, width), lambda j: (j, 0, piece))],
        out_specs=[out] * 2,
        scratch_shapes=[pltpu.VMEM((4 * count, depth), jnp.bfloat16)],
        compiler_params=pltpu.CompilerParams(vmem_limit_bytes=28 * MIB),
        cost_estimate=pl.CostEstimate(flops=0, bytes_accessed=0, transcendentals=0),
        name="multiply",
    )(kept_first.reshape(1), *row_parts, weights)


def arrange_kernel(pieces, flags_ref, *refs):
    *parts, out_ref = refs
    own, direct, back = parts[:pieces], parts[pieces : 2 * pieces], parts[2 * pieces :]
    count, width = back[0].shape
    for holder in range(2):

        @pl.when(flags_ref[1] == holder)
        def _(holder=holder):
            for i in range(pieces):
                here = slice((holder * pieces + i) * width, (holder * pieces + i + 1) * width)
                there = slice(((1 - holder) * pieces + i) * width, ((1 - holder) * pieces + i + 1) * width)
                out_ref[:, there] = back[i][...]

                @pl.when(flags_ref[0] != 0)
                def _(here=here, i=i):
                    out_ref[:, here] = own[i][:count, :]

                @pl.when(flags_ref[0] == 0)
                def _(here=here, i=i):
                    out_ref[:, here] = direct[i][...]


def arrange(same, holder, own, direct, back):
    count, width = back[0].shape
    pieces = len(back)
    vmem = pl.BlockSpec(memory_space=pltpu.VMEM)
    return pl.pallas_call(
        functools.partial(arrange_kernel, pieces),
        out_shape=jax.ShapeDtypeStruct((count, 2 * pieces * width), back[0].dtype),
        in_specs=[pl.BlockSpec(memory_space=pltpu.SMEM)] + [vmem] * (3 * pieces),
        out_specs=vmem,
        compiler_params=pltpu.CompilerParams(vmem_limit_bytes=16 * MIB),
        cost_estimate=pl.CostEstimate(flops=0, bytes_accessed=0, transcendentals=0),
        name="arrange",
    )(jnp.stack([same.astype(jnp.int32), holder.astype(jnp.int32)]), *own, *direct, *back)


def project(rows, weights, others, plane, holder):
    group = lax.axis_index("kvh")
    chip = group // 2
    same = group % 2 == plane % 2
    count = rows.shape[0]
    per_half = 2
    pieces = per_half * len(weights)
    width = weights[0].shape[1] // per_half
    upper = plane >= 2

    def send(x, to, keep=lambda p, k: True):
        pairs = []
        for p in range(4):
            for h in range(2):
                for k in range(4):
                    if keep(p, k):
                        q, g, m = to(p, h, k)
                        pairs.append(((p * 2 + h) * 4 + k, (q * 2 + g) * 4 + m))
        return lax.ppermute(x, ("ctx", "kvh"), pairs)

    def fetch(x):
        return (
            x,
            send(x, lambda p, h, k: (p, 1 - h, k)),
            send(x, lambda p, h, k: (p ^ 1, h, k)),
            send(x, lambda p, h, k: (p ^ 1, 1 - h, k)),
        )

    def add(a, b):
        return (a.astype(jnp.float32) + b.astype(jnp.float32)).astype(jnp.bfloat16)

    def chip_sums(fetched, columns, piece, *wanted):
        kept, sent = multiply(same.astype(jnp.int32), fetched, columns, width, piece)
        products.append(sent)
        got = after(send(sent, lambda p, h, k: (p, h, k ^ 1)), *wanted)
        total = add(kept, got)
        low, high = total[:, :width], total[:, width:]
        return jnp.where(chip == 0, low, high), jnp.where(chip == 0, high, low)

    def deliver(total):
        direct = send(
            total[:count], lambda p, h, k: (p ^ 1, h, k ^ 1), lambda p, k: k % 2 != p % 2
        )
        back = send(
            total[count:],
            lambda p, h, k: (p, 1 - h, k) if k % 2 == p % 2 else (p ^ 1, 1 - h, k ^ 1),
        )
        return total, direct, back

    fetched = fetch(rows)
    sums, delivered, products = [], [], []
    for own, other in zip(weights, others):
        if len(sums) >= 2:
            other = lax.optimization_barrier((other, sums[-2:]))[0]
        columns = jnp.stack([jnp.where(upper, other, own), jnp.where(upper, own, other)])
        for piece in range(per_half):
            wanted = () if sums else others[-1:]
            sums.append(chip_sums(fetched, columns, piece, *wanted))
    for kept, sent in sums:
        got = after(send(sent, lambda p, h, k: (p, h, k ^ 2)), *products)
        delivered.append(deliver(add(kept, got)))
    return arrange(same, holder, *zip(*delivered))


def local(
    queries, resp_keys, resp_values, prefix_keys, prefix_values, prefix_len, prompt_of, out_weight
):
    ctx_count = lax.axis_size("ctx")
    kvh_count = lax.axis_size("kvh")
    position = lax.axis_index("ctx")
    own_queries = queries[:, :, 0]
    own_keys = resp_keys[:, :, 0]
    own_values = resp_values[:, :, 0]
    resp_count, tokens_each, width = own_queries.shape
    slot_count = prefix_keys.shape[0]
    prompts = prefix_len.shape[0]
    holders = ctx_count // prompts
    my_prompt = position // holders
    my_holder = position % holders
    capacity = max(LANES // tokens_each, resp_count // prompts)
    places = prompts * capacity
    by_plane = kvh_count == prompts == 4 and holders == 2

    def cross(x, i):
        pairs = [(p * holders + h, (p ^ i) * holders + h) for p in range(prompts) for h in range(holders)]
        return lax.ppermute(x, "ctx", pairs)

    chunks, meta = pack(prompt_of, prefix_len, own_queries, capacity, holders, slot_count)
    chunks = chunks[:1] + [cross(x, i) for i, x in enumerate(chunks) if i > 0]
    near = prefix_keys[:, 0], prefix_values[:, 0]
    away = chunks[:0:-1]
    if by_plane:
        half = out_weight.shape[1] // 2
        weights = [out_weight[:, :half], out_weight[:, half:]]
        weights[0] = after(weights[0], *away)
        others = [cross(x, 2) for x in weights]
        shards = [near, near]
        shards[1] = [
            lax.ppermute(x, "ctx", [(c, c ^ 1) for c in range(ctx_count)]) for x in shards[1]
        ]
    else:
        lines = [[p * holders + h for h in range(holders)] for p in range(prompts)]
        joined = jnp.concatenate(near, axis=1)
        joined = lax.all_gather(joined, "ctx", axis=0, tiled=True, axis_index_groups=lines)
        shards = [near] + [(joined, joined)] * (holders - 1)

    state_home = state_away = None
    for shard in range(holders - 1):
        kv = shards[shard]
        state_home = attend(meta, places, chunks[:1], *kv, slot_count, shard, state_home, 0, False)
        state_home, away = lax.optimization_barrier((state_home, away))
        state_away = attend(meta, places, away, *kv, slot_count, shard, state_away, 0, False)
    shard = holders - 1
    far = shards[shard]
    done = [None] * prompts
    for where, members in enumerate([range(prompts - 1, 1, -1), [1]]):
        queries_now = [away[prompts - 1 - i] for i in members]
        block = 0 if where == 0 else prompts - 2
        results = attend(meta, places, queries_now, *far, slot_count, shard, state_away, block, True)
        for i, x in zip(members, results):
            done[i] = cross(x, i)
        if by_plane and where == 0:
            others[0], state_away = lax.optimization_barrier((others[0], state_away))
    (done[0],) = attend(meta, places, chunks[:1], *far, slot_count, shard, state_home, 0, True)
    attended = combine(meta, capacity, own_queries, own_keys, own_values, done)
    rows = attended.reshape(resp_count * tokens_each, width)

    if by_plane:
        projected = project(rows, weights, others, my_prompt, my_holder)
    else:
        weights = lax.all_gather(out_weight, "ctx", axis=1, tiled=True)
        terms = jnp.dot(rows, weights, preferred_element_type=jnp.float32)
        projected = lax.psum_scatter(
            terms.astype(jnp.bfloat16), "kvh", scatter_dimension=1, tiled=True
        )
    return (attended[:, :, None, :], projected)


def solution(mesh):
    in_specs = (
        P("ctx", None, "kvh", None),
        P("ctx", None, "kvh", None),
        P("ctx", None, "kvh", None),
        P("ctx", "kvh", None),
        P("ctx", "kvh", None),
        P(),
        P(),
        P("kvh", "ctx"),
    )
    out_specs = (P("ctx", None, "kvh", None), P("ctx", "kvh"))
    return jax.shard_map(local, mesh=mesh, in_specs=in_specs, out_specs=out_specs, check_vma=False)
```

```python
import functools
import math

import jax
import jax.numpy as jnp
from jax import lax
from jax.experimental import pallas as pl
from jax.experimental.pallas import tpu as pltpu
from jax.sharding import PartitionSpec as P

MASKED = -1e30
LOG2E = math.log2(math.e)
LANES = 128
PART_ROWS = 16
MAX_TILE = 1024
MAX_BLOCK = 512
MIB = 1024 * 1024


def nt_dot(a, b):
    return lax.dot_general(a, b, (((1,), (1,)), ((), ())), preferred_element_type=jnp.float32)


def after(x, *others):
    return lax.optimization_barrier((x, *others))[0]


def pack_kernel(capacity, holders, slots, prompt_ref, len_ref, q_ref, *refs):
    *chunk_refs, meta_ref = refs
    responses, tokens, _ = q_ref.shape
    position = lax.axis_index("ctx")
    mine, holder = position // holders, position % holders
    named = [prompt_ref[position * responses + r] for r in range(responses)]
    ranks = []
    for r in range(responses):
        rank = jnp.int32(0)
        for before in range(r):
            rank += (named[before] == named[r]).astype(jnp.int32)
        ranks.append(rank)
    places = len(chunk_refs) * capacity
    for i, chunk_ref in enumerate(chunk_refs):
        for slot in range(capacity):
            chosen, present = jnp.int32(0), jnp.int32(0)
            for r in range(responses):
                hit = ((named[r] == mine ^ i) & (ranks[r] == slot)).astype(jnp.int32)
                chosen += hit * r
                present += hit
            meta_ref[i * capacity + slot] = chosen
            meta_ref[places + i * capacity + slot] = present
            rows = slice(slot * tokens, (slot + 1) * tokens)
            chunk_ref[rows, :] = q_ref[chosen]

            @pl.when(present == 0)
            def _(chunk_ref=chunk_ref, rows=rows):
                chunk_ref[rows, :] = jnp.zeros_like(chunk_ref[rows, :])

    length = len_ref[mine]
    for j in range(holders):
        place = (holder + j) % holders
        meta_ref[2 * places + j] = jnp.clip(length - place * slots, 0, slots)
        meta_ref[2 * places + holders + j] = place


def pack(prompt_of, prefix_len, q, capacity, holders, slots):
    _, tokens, width = q.shape
    prompts = prefix_len.shape[0]
    smem = pl.BlockSpec(memory_space=pltpu.SMEM)
    vmem = pl.BlockSpec(memory_space=pltpu.VMEM)
    *chunks, meta = pl.pallas_call(
        functools.partial(pack_kernel, capacity, holders, slots),
        out_shape=[jax.ShapeDtypeStruct((capacity * tokens, width), q.dtype)] * prompts
        + [jax.ShapeDtypeStruct((2 * (prompts * capacity + holders),), jnp.int32)],
        in_specs=[smem, smem, vmem],
        out_specs=[vmem] * prompts + [smem],
        compiler_params=pltpu.CompilerParams(vmem_limit_bytes=16 * MIB),
        cost_estimate=pl.CostEstimate(flops=0, bytes_accessed=4 * q.size, transcendentals=0),
        name="pack",
    )(prompt_of, prefix_len, q)
    return chunks, meta


def attend_kernel(count, first, last, shard, places, meta_ref, *refs):
    q_refs, (k_ref, v_ref, *refs) = refs[:count], refs[count:]
    if not first:
        prev_o_ref, prev_lse_ref, *refs = refs
    if last:
        out_refs, refs = refs[:count], refs[count:]
    else:
        o_ref, lse_ref, *refs = refs
    qext, kext, vext, score_a, score_b = refs
    tokens = q_refs[0].shape[0]
    slots, hd = k_ref.shape
    heads = q_refs[0].shape[1] // hd
    scale = LOG2E / math.sqrt(hd)
    tiles, row_block, key_tile = score_a.shape
    per_chunk = heads * tokens // row_block
    live = meta_ref[2 * places + shard]

    @pl.when(live == slots)
    def _():
        for t in range(tiles):
            at = slice(t * key_tile, (t + 1) * key_tile)
            keys = k_ref[at, :]
            kext[at, :hd] = keys
            kext[at, hd:] = keys
            vext[at, :hd] = v_ref[at, :]
            vext[at, hd:] = jnp.ones((key_tile, hd), jnp.bfloat16)

    @pl.when(live != slots)
    def _():
        def prepare(step, carry):
            at = pl.ds(pl.multiple_of(step * key_tile, key_tile), key_tile)
            alive = step * key_tile + lax.broadcasted_iota(jnp.int32, (key_tile, hd), 0) < live
            keys = jnp.where(alive, k_ref[at, :].astype(jnp.float32), k_ref[0:1, :].astype(jnp.float32))
            keys = keys.astype(jnp.bfloat16)
            kext[at, :hd] = keys
            kext[at, hd:] = keys
            vext[at, :hd] = jnp.where(alive, v_ref[at, :].astype(jnp.float32), 0.0).astype(jnp.bfloat16)
            vext[at, hd:] = jnp.where(alive, 1.0, 0.0).astype(jnp.bfloat16)
            return carry

        lax.fori_loop(0, tiles, prepare, 0)

    for c, q_ref in enumerate(q_refs):
        for h in range(heads):
            rows = slice((c * heads + h) * tokens, (c * heads + h + 1) * tokens)
            x = q_ref[:, h * hd : (h + 1) * hd].astype(jnp.float32) * scale
            high = x.astype(jnp.bfloat16)
            qext[rows, :hd] = high
            qext[rows, hd:] = (x - high.astype(jnp.float32)).astype(jnp.bfloat16)

    low = jnp.full((row_block, LANES), MASKED, jnp.float32)

    def rows_of(b):
        if isinstance(b, int):
            return slice(b * row_block, (b + 1) * row_block)
        return pl.ds(pl.multiple_of(b * row_block, row_block), row_block)

    def score_tile(b, t, into, peak):
        s = nt_dot(qext[rows_of(b), :], kext[t * key_tile : (t + 1) * key_tile, :])
        into[t] = s
        for j in range(key_tile // LANES):
            peak = jnp.maximum(peak, s[:, j * LANES : (j + 1) * LANES])
        return peak

    def one_block(b, scores, peak, following, into):
        m = jnp.max(peak, axis=1, keepdims=True)
        peak = low
        acc = jnp.zeros((row_block, 2 * hd), jnp.float32)
        for t in range(tiles):
            if following is not None:
                peak = score_tile(following, t, into, peak)
            w = jnp.exp2(scores[t] - m).astype(jnp.bfloat16)
            acc = acc + jnp.dot(
                w, vext[t * key_tile : (t + 1) * key_tile, :], preferred_element_type=jnp.float32
            )
        total = acc[:, hd:]
        some = total > 0.0
        safe = jnp.where(some, total, 1.0)
        o = acc[:, :hd] / safe
        lse = jnp.where(some, m + jnp.log2(safe), MASKED)
        rows = rows_of(b)
        if not first:
            before = prev_lse_ref[rows, :]
            top = jnp.maximum(before, lse)
            w_before = jnp.exp2(before - top)
            w_now = jnp.exp2(lse - top)
            both = w_before + w_now
            o = (w_before * prev_o_ref[rows, :] + w_now * o) / both
            lse = top + jnp.log2(both)
        if not last:
            o_ref[rows, :] = o
            lse_ref[rows, :] = lse
            return peak
        out_ref = out_refs[b // per_chunk]
        for j in range(row_block // tokens):
            h = (b % per_chunk) * (row_block // tokens) + j
            part = slice(j * tokens, (j + 1) * tokens)
            lanes = slice(h * hd, (h + 1) * hd)
            out_ref[:tokens, lanes] = o[part].astype(jnp.bfloat16)
            flat = lse[part].T[:PART_ROWS, :]
            high = flat.astype(jnp.bfloat16).astype(jnp.float32)
            middle = (flat - high).astype(jnp.bfloat16).astype(jnp.float32)
            row = lax.broadcasted_iota(jnp.int32, flat.shape, 0)
            out_ref[tokens:, lanes] = jnp.where(
                row == 0, high, jnp.where(row == 1, middle, jnp.where(row == 2, flat - high - middle, 0.0))
            ).astype(jnp.bfloat16)
        return peak

    blocks = count * per_chunk
    peak = low
    for t in range(tiles):
        peak = score_tile(0, t, score_a, peak)
    looped = 0
    if not last and per_chunk % 2 == 0 and count > 1:
        looped = blocks - 2

        def pair(i, peak):
            peak = one_block(2 * i, score_a, peak, 2 * i + 1, score_b)
            return one_block(2 * i + 1, score_b, peak, 2 * i + 2, score_a)

        peak = lax.fori_loop(0, looped // 2, pair, peak)
    for b in range(looped, blocks):
        scores, into = (score_a, score_b) if b % 2 == 0 else (score_b, score_a)
        peak = one_block(b, scores, peak, b + 1 if b + 1 < blocks else None, into)


def attend(meta, places, queries, keys, values, slots, shard, state, state_block, last):
    count = len(queries)
    tokens, width = queries[0].shape
    whole = keys.shape[0] > slots
    hd = keys.shape[1] // 2 if whole else keys.shape[1]
    rows = tokens * (width // hd)
    row_block = min(MAX_BLOCK, rows)
    key_tile = min(MAX_TILE, slots)
    holders = meta.shape[0] // 2 - places
    first = state is None

    def fixed(shape):
        return pl.BlockSpec(shape, lambda i, meta_ref: (0, 0))

    def shard_at(column):
        if not whole:
            return pl.BlockSpec((slots, hd), lambda i, meta_ref: (0, 0))
        return pl.BlockSpec(
            (slots, hd), lambda i, meta_ref: (meta_ref[2 * places + holders + shard], column)
        )

    in_specs = [fixed((tokens, width))] * count + [shard_at(0), shard_at(1)]
    operands = [meta, *queries, keys, values]
    if not first:
        in_specs += [pl.BlockSpec((count * rows, hd), lambda i, meta_ref: (state_block, 0))] * 2
        operands += state
    if last:
        out_shape = [jax.ShapeDtypeStruct((tokens + PART_ROWS, width), jnp.bfloat16)] * count
        out_specs = [fixed((tokens + PART_ROWS, width))] * count
    else:
        out_shape = [jax.ShapeDtypeStruct((count * rows, hd), jnp.float32)] * 2
        out_specs = [fixed((count * rows, hd))] * 2
    return pl.pallas_call(
        functools.partial(attend_kernel, count, first, last, shard, places),
        grid_spec=pltpu.PrefetchScalarGridSpec(
            num_scalar_prefetch=1,
            grid=(1,),
            in_specs=in_specs,
            out_specs=out_specs,
            scratch_shapes=[
                pltpu.VMEM((count * rows, 2 * hd), jnp.bfloat16),
                pltpu.VMEM((slots, 2 * hd), jnp.bfloat16),
                pltpu.VMEM((slots, 2 * hd), jnp.bfloat16),
                pltpu.VMEM((slots // key_tile, row_block, key_tile), jnp.float32),
                pltpu.VMEM((slots // key_tile, row_block, key_tile), jnp.float32),
            ],
        ),
        out_shape=out_shape,
        compiler_params=pltpu.CompilerParams(vmem_limit_bytes=40 * MIB),
        cost_estimate=pl.CostEstimate(
            flops=4 * count * rows * slots * hd if first else 0,
            bytes_accessed=0,
            transcendentals=0,
        ),
        name="attend_last" if last else "attend",
    )(*operands)


def combine_kernel(capacity, meta_ref, q_ref, k_ref, v_ref, *refs):
    *part_refs, out_ref, stacked = refs
    _, tokens, hd = k_ref.shape
    width = q_ref.shape[2]
    heads = width // hd
    scale = LOG2E / math.sqrt(hd)
    places = len(part_refs) * capacity
    for i, part_ref in enumerate(part_refs):
        for slot in range(capacity):
            r = meta_ref[i * capacity + slot]

            @pl.when(meta_ref[places + i * capacity + slot] > 0)
            def _(r=r, part_ref=part_ref, slot=slot):
                for h in range(heads):
                    stacked[h * tokens : (h + 1) * tokens, :] = q_ref[r, :, h * hd : (h + 1) * hd]
                s = nt_dot(stacked[...], k_ref[r]) * scale
                row = lax.broadcasted_iota(jnp.int32, s.shape, 0) % tokens
                seen = row >= lax.broadcasted_iota(jnp.int32, s.shape, 1)
                s = jnp.where(seen, s, MASKED)
                m = jnp.max(s, axis=1, keepdims=True)
                w = jnp.where(seen, jnp.exp2(s - m), 0.0)
                total = jnp.sum(w, axis=1, keepdims=True)
                o = jnp.dot(w.astype(jnp.bfloat16), v_ref[r], preferred_element_type=jnp.float32)
                base = part_ref.shape[0] - PART_ROWS
                for h in range(heads):
                    rows = slice(h * tokens, (h + 1) * tokens)
                    lanes = slice(h * hd, (h + 1) * hd)
                    far = part_ref[slot * tokens : (slot + 1) * tokens, lanes].astype(jnp.float32)
                    pieces = part_ref[base:, lanes].astype(jnp.float32)
                    flat = pieces[0:1] + pieces[1:2] + pieces[2:3]
                    lse = jnp.broadcast_to(flat, (hd, hd)).T[slot * tokens : (slot + 1) * tokens, :]
                    top = jnp.maximum(m[rows], lse)
                    own_scale = jnp.exp2(m[rows] - top)
                    far_scale = jnp.exp2(lse - top)
                    out_ref[r, :, lanes] = (
                        (own_scale * o[rows] + far_scale * far) / (own_scale * total[rows] + far_scale)
                    ).astype(jnp.bfloat16)


def combine(meta, capacity, q, keys, values, parts):
    responses, tokens, width = q.shape
    hd = keys.shape[-1]
    heads = width // hd
    return pl.pallas_call(
        functools.partial(combine_kernel, capacity),
        out_shape=jax.ShapeDtypeStruct(q.shape, jnp.bfloat16),
        in_specs=[pl.BlockSpec(memory_space=pltpu.SMEM)]
        + [pl.BlockSpec(memory_space=pltpu.VMEM)] * (3 + len(parts)),
        out_specs=pl.BlockSpec(memory_space=pltpu.VMEM),
        scratch_shapes=[pltpu.VMEM((heads * tokens, hd), jnp.bfloat16)],
        compiler_params=pltpu.CompilerParams(vmem_limit_bytes=24 * MIB),
        cost_estimate=pl.CostEstimate(flops=0, bytes_accessed=0, transcendentals=0),
        name="combine",
    )(meta, q, keys, values, *parts)


def multiply_kernel(first_ref, second_ref, weight_ref, out_ref):
    count = first_ref.shape[0]
    for i, ref in enumerate((first_ref, second_ref)):
        out_ref[i * count : (i + 1) * count, :] = jnp.dot(
            ref[...], weight_ref[0], preferred_element_type=jnp.float32
        ).astype(out_ref.dtype)


def multiply(row_parts, weights):
    count, depth = row_parts[0].shape
    blocks, _, width = weights.shape
    return pl.pallas_call(
        multiply_kernel,
        grid=(blocks,),
        out_shape=jax.ShapeDtypeStruct((2 * count, blocks * width), jnp.bfloat16),
        in_specs=[pl.BlockSpec((count, depth), lambda j: (0, 0))] * 2
        + [pl.BlockSpec((1, depth, width), lambda j: (j, 0, 0))],
        out_specs=pl.BlockSpec((2 * count, width), lambda j: (0, j)),
        compiler_params=pltpu.CompilerParams(vmem_limit_bytes=24 * MIB),
        cost_estimate=pl.CostEstimate(flops=0, bytes_accessed=0, transcendentals=0),
        name="multiply",
    )(*row_parts, weights)


def arrange_kernel(halves, flags_ref, *refs):
    *parts, out_ref = refs
    own, own_back, direct, direct_back = (parts[i * halves : (i + 1) * halves] for i in range(4))
    count, width = direct[0].shape
    for holder in range(2):
        for same, sources in ((1, (own, own_back)), (0, (direct, direct_back))):

            @pl.when((flags_ref[1] == holder) & (flags_ref[0] == same))
            def _(holder=holder, sources=sources):
                for place, source in zip((holder, 1 - holder), sources):
                    for i in range(halves):
                        at = (place * halves + i) * width
                        out_ref[:, at : at + width] = source[i][:count, :]


def arrange(same, holder, *sources):
    count, width = sources[2][0].shape
    halves = len(sources[0])
    vmem = pl.BlockSpec(memory_space=pltpu.VMEM)
    return pl.pallas_call(
        functools.partial(arrange_kernel, halves),
        out_shape=jax.ShapeDtypeStruct((count, 2 * halves * width), jnp.bfloat16),
        in_specs=[pl.BlockSpec(memory_space=pltpu.SMEM)] + [vmem] * (4 * halves),
        out_specs=vmem,
        compiler_params=pltpu.CompilerParams(vmem_limit_bytes=16 * MIB),
        cost_estimate=pl.CostEstimate(flops=0, bytes_accessed=0, transcendentals=0),
        name="arrange",
    )(
        jnp.stack([same.astype(jnp.int32), holder.astype(jnp.int32)]),
        *(x for source in sources for x in source),
    )


def project(rows, weights, others, plane, holder):
    group = lax.axis_index("kvh")
    chip = group // 2
    same = group % 2 == plane % 2
    count = rows.shape[0]
    width = weights[0].shape[1]
    upper = plane >= 2

    def send(x, to, keep=lambda p, k: True):
        pairs = []
        for p in range(4):
            for h in range(2):
                for k in range(4):
                    if keep(p, k):
                        q, g, m = to(p, h, k)
                        pairs.append(((p * 2 + h) * 4 + k, (q * 2 + g) * 4 + m))
        return lax.ppermute(x, ("ctx", "kvh"), pairs)

    def add(a, b):
        return (a.astype(jnp.float32) + b.astype(jnp.float32)).astype(jnp.bfloat16)

    def summing(mine):
        return lambda p, k: (k % 2 == p % 2) == mine

    def core_sums(product, mine, *wanted):
        got = send(product, lambda p, h, k: (p, h, k ^ 1), lambda p, k: not summing(mine)(p, k))
        total = add(product, after(got, *wanted))
        low, high = total[:, :width], total[:, width:]
        return jnp.where(chip == 0, low, high), jnp.where(chip == 0, high, low)

    swapped = send(rows, lambda p, h, k: (p, 1 - h, k))
    away = (
        send(rows, lambda p, h, k: (p ^ 1, h, k)),
        send(rows, lambda p, h, k: (p ^ 1, 1 - h, k)),
    )
    columns = [
        jnp.stack([jnp.where(upper, other, own), jnp.where(upper, own, other)])
        for own, other in zip(weights, others)
    ]
    swapped, near = lax.optimization_barrier((swapped, away[0]))
    away = near, away[1]
    products = [multiply((rows, swapped), columns[0])]
    sums = [core_sums(products[0], True, others[1], away[1])]

    def x_sum(mine, sums, *wanted):
        kept, sent = sums
        got = send(sent, lambda p, h, k: (p, h, k ^ 2), summing(mine))
        return add(kept, after(got, *wanted))

    first_half, second_half = lax.optimization_barrier((columns, sums[0]))[0]
    sums.append(core_sums(multiply((rows, swapped), second_half), True))
    products.append(multiply(away, first_half))
    sums.append(core_sums(products[-1], False))
    totals = [x_sum(True, sums[0], products[-1])]
    second_half = after(second_half, totals[0], *sums[1])
    sums.append(core_sums(multiply(away, second_half), False))
    totals += [x_sum(mine, x) for mine, x in zip((True, False, False), sums[1:])]
    own, others_rows = totals[:2], totals[2:]
    own_back = [
        send(x[count:], lambda p, h, k: (p, 1 - h, k), summing(True)) for x in own
    ]
    direct, direct_back = (
        [
            send(
                x[i * count : (i + 1) * count],
                lambda p, h, k, i=i: (p ^ 1, h ^ i, k ^ 1),
                summing(False),
            )
            for x in others_rows
        ]
        for i in range(2)
    )
    return arrange(same, holder, own, own_back, direct, direct_back)


def local(
    queries, resp_keys, resp_values, prefix_keys, prefix_values, prefix_len, prompt_of, out_weight
):
    ctx_count = lax.axis_size("ctx")
    kvh_count = lax.axis_size("kvh")
    position = lax.axis_index("ctx")
    own_queries = queries[:, :, 0]
    own_keys = resp_keys[:, :, 0]
    own_values = resp_values[:, :, 0]
    resp_count, tokens_each, width = own_queries.shape
    slot_count = prefix_keys.shape[0]
    prompts = prefix_len.shape[0]
    holders = ctx_count // prompts
    my_prompt = position // holders
    my_holder = position % holders
    capacity = max(LANES // tokens_each, resp_count // prompts)
    places = prompts * capacity
    by_plane = kvh_count == prompts == 4 and holders == 2

    def cross(x, i):
        pairs = [(p * holders + h, (p ^ i) * holders + h) for p in range(prompts) for h in range(holders)]
        return lax.ppermute(x, "ctx", pairs)

    chunks, meta = pack(prompt_of, prefix_len, own_queries, capacity, holders, slot_count)
    chunks = chunks[:1] + [cross(x, i) for i, x in enumerate(chunks) if i > 0]
    near = prefix_keys[:, 0], prefix_values[:, 0]
    away = chunks[:0:-1]
    if by_plane:
        half = out_weight.shape[1] // 2
        weights = [out_weight[:, :half], out_weight[:, half:]]
        weights[0] = after(weights[0], *away)
        others = [cross(weights[0], 2)]
        shards = [near, near]
        shards[1] = [
            lax.ppermute(x, "ctx", [(c, c ^ 1) for c in range(ctx_count)]) for x in shards[1]
        ]
    else:
        lines = [[p * holders + h for h in range(holders)] for p in range(prompts)]
        joined = jnp.concatenate(near, axis=1)
        joined = lax.all_gather(joined, "ctx", axis=0, tiled=True, axis_index_groups=lines)
        shards = [near] + [(joined, joined)] * (holders - 1)

    state_home = state_away = None
    for shard in range(holders - 1):
        kv = shards[shard]
        state_home = attend(meta, places, chunks[:1], *kv, slot_count, shard, state_home, 0, False)
        state_home, away = lax.optimization_barrier((state_home, away))
        state_away = attend(meta, places, away, *kv, slot_count, shard, state_away, 0, False)
    shard = holders - 1
    far = shards[shard]
    done = [None] * prompts
    for where, members in enumerate([range(prompts - 1, 1, -1), [1]]):
        queries_now = [away[prompts - 1 - i] for i in members]
        block = 0 if where == 0 else prompts - 2
        results = attend(meta, places, queries_now, *far, slot_count, shard, state_away, block, True)
        for i, x in zip(members, results):
            done[i] = cross(x, i)
        if where == 0:
            state_away = lax.optimization_barrier((state_away, results[0]))[0]
    (done[0],) = attend(meta, places, chunks[:1], *far, slot_count, shard, state_home, 0, True)
    if by_plane:
        others[0], done[0] = lax.optimization_barrier((others[0], done[0]))
    attended = combine(meta, capacity, own_queries, own_keys, own_values, done)
    rows = attended.reshape(resp_count * tokens_each, width)

    if by_plane:
        others.append(cross(after(weights[1], rows), 2))
        projected = project(rows, weights, others, my_prompt, my_holder)
    else:
        weights = lax.all_gather(out_weight, "ctx", axis=1, tiled=True)
        terms = jnp.dot(rows, weights, preferred_element_type=jnp.float32)
        projected = lax.psum_scatter(
            terms.astype(jnp.bfloat16), "kvh", scatter_dimension=1, tiled=True
        )
    return (attended[:, :, None, :], projected)


def solution(mesh):
    in_specs = (
        P("ctx", None, "kvh", None),
        P("ctx", None, "kvh", None),
        P("ctx", None, "kvh", None),
        P("ctx", "kvh", None),
        P("ctx", "kvh", None),
        P(),
        P(),
        P("kvh", "ctx"),
    )
    out_specs = (P("ctx", None, "kvh", None), P("ctx", "kvh"))
    return jax.shard_map(local, mesh=mesh, in_specs=in_specs, out_specs=out_specs, check_vma=False)
```

```python
import functools
import math

import jax
import jax.numpy as jnp
from jax import lax
from jax.experimental import pallas as pl
from jax.experimental.pallas import tpu as pltpu
from jax.sharding import PartitionSpec as P

MASKED = -1e30
LOG2E = math.log2(math.e)
LANES = 128
PART_ROWS = 16
MAX_TILE = 1024
MAX_BLOCK = 512
MIB = 1024 * 1024


def nt_dot(a, b):
    return lax.dot_general(a, b, (((1,), (1,)), ((), ())), preferred_element_type=jnp.float32)


def after(x, *others):
    return lax.optimization_barrier((x, *others))[0]


def pack_kernel(capacity, holders, slots, prompt_ref, len_ref, q_ref, *refs):
    *chunk_refs, meta_ref = refs
    responses, tokens, _ = q_ref.shape
    position = lax.axis_index("ctx")
    mine, holder = position // holders, position % holders
    named = [prompt_ref[position * responses + r] for r in range(responses)]
    ranks = []
    for r in range(responses):
        rank = jnp.int32(0)
        for before in range(r):
            rank += (named[before] == named[r]).astype(jnp.int32)
        ranks.append(rank)
    places = len(chunk_refs) * capacity
    for i, chunk_ref in enumerate(chunk_refs):
        for slot in range(capacity):
            chosen, present = jnp.int32(0), jnp.int32(0)
            for r in range(responses):
                hit = ((named[r] == mine ^ i) & (ranks[r] == slot)).astype(jnp.int32)
                chosen += hit * r
                present += hit
            meta_ref[i * capacity + slot] = chosen
            meta_ref[places + i * capacity + slot] = present
            rows = slice(slot * tokens, (slot + 1) * tokens)
            chunk_ref[rows, :] = q_ref[chosen]

            @pl.when(present == 0)
            def _(chunk_ref=chunk_ref, rows=rows):
                chunk_ref[rows, :] = jnp.zeros_like(chunk_ref[rows, :])

    length = len_ref[mine]
    for j in range(holders):
        place = (holder + j) % holders
        meta_ref[2 * places + j] = jnp.clip(length - place * slots, 0, slots)
        meta_ref[2 * places + holders + j] = place


def pack(prompt_of, prefix_len, q, capacity, holders, slots):
    _, tokens, width = q.shape
    prompts = prefix_len.shape[0]
    smem = pl.BlockSpec(memory_space=pltpu.SMEM)
    vmem = pl.BlockSpec(memory_space=pltpu.VMEM)
    *chunks, meta = pl.pallas_call(
        functools.partial(pack_kernel, capacity, holders, slots),
        out_shape=[jax.ShapeDtypeStruct((capacity * tokens, width), q.dtype)] * prompts
        + [jax.ShapeDtypeStruct((2 * (prompts * capacity + holders),), jnp.int32)],
        in_specs=[smem, smem, vmem],
        out_specs=[vmem] * prompts + [smem],
        compiler_params=pltpu.CompilerParams(vmem_limit_bytes=16 * MIB),
        cost_estimate=pl.CostEstimate(flops=0, bytes_accessed=4 * q.size, transcendentals=0),
        name="pack",
    )(prompt_of, prefix_len, q)
    return chunks, meta


def attend_kernel(count, first, last, shard, places, meta_ref, *refs):
    q_refs, (k_ref, v_ref, *refs) = refs[:count], refs[count:]
    if not first:
        prev_o_ref, prev_lse_ref, *refs = refs
    if last:
        out_refs, refs = refs[:count], refs[count:]
    else:
        o_ref, lse_ref, *refs = refs
    qext, kext, vext, score_a, score_b = refs
    tokens = q_refs[0].shape[0]
    slots, hd = k_ref.shape
    heads = q_refs[0].shape[1] // hd
    scale = LOG2E / math.sqrt(hd)
    tiles, row_block, key_tile = score_a.shape
    per_chunk = heads * tokens // row_block
    live = meta_ref[2 * places + shard]

    @pl.when(live == slots)
    def _():
        for t in range(tiles):
            at = slice(t * key_tile, (t + 1) * key_tile)
            keys = k_ref[at, :]
            kext[at, :hd] = keys
            kext[at, hd:] = keys
            vext[at, :hd] = v_ref[at, :]
            vext[at, hd:] = jnp.ones((key_tile, hd), jnp.bfloat16)

    @pl.when(live != slots)
    def _():
        def prepare(step, carry):
            at = pl.ds(pl.multiple_of(step * key_tile, key_tile), key_tile)
            alive = step * key_tile + lax.broadcasted_iota(jnp.int32, (key_tile, hd), 0) < live
            keys = jnp.where(alive, k_ref[at, :].astype(jnp.float32), k_ref[0:1, :].astype(jnp.float32))
            keys = keys.astype(jnp.bfloat16)
            kext[at, :hd] = keys
            kext[at, hd:] = keys
            vext[at, :hd] = jnp.where(alive, v_ref[at, :].astype(jnp.float32), 0.0).astype(jnp.bfloat16)
            vext[at, hd:] = jnp.where(alive, 1.0, 0.0).astype(jnp.bfloat16)
            return carry

        lax.fori_loop(0, tiles, prepare, 0)

    for c, q_ref in enumerate(q_refs):
        for h in range(heads):
            rows = slice((c * heads + h) * tokens, (c * heads + h + 1) * tokens)
            x = q_ref[:, h * hd : (h + 1) * hd].astype(jnp.float32) * scale
            high = x.astype(jnp.bfloat16)
            qext[rows, :hd] = high
            qext[rows, hd:] = (x - high.astype(jnp.float32)).astype(jnp.bfloat16)

    low = jnp.full((row_block, LANES), MASKED, jnp.float32)

    def rows_of(b):
        if isinstance(b, int):
            return slice(b * row_block, (b + 1) * row_block)
        return pl.ds(pl.multiple_of(b * row_block, row_block), row_block)

    def score_tile(b, t, into, peak):
        s = nt_dot(qext[rows_of(b), :], kext[t * key_tile : (t + 1) * key_tile, :])
        into[t] = s
        for j in range(key_tile // LANES):
            peak = jnp.maximum(peak, s[:, j * LANES : (j + 1) * LANES])
        return peak

    def one_block(b, scores, peak, following, into):
        m = jnp.max(peak, axis=1, keepdims=True)
        peak = low
        acc = jnp.zeros((row_block, 2 * hd), jnp.float32)
        for t in range(tiles):
            if following is not None:
                peak = score_tile(following, t, into, peak)
            w = jnp.exp2(scores[t] - m).astype(jnp.bfloat16)
            acc = acc + jnp.dot(
                w, vext[t * key_tile : (t + 1) * key_tile, :], preferred_element_type=jnp.float32
            )
        total = acc[:, hd:]
        some = total > 0.0
        safe = jnp.where(some, total, 1.0)
        o = acc[:, :hd] / safe
        lse = jnp.where(some, m + jnp.log2(safe), MASKED)
        rows = rows_of(b)
        if not first:
            before = prev_lse_ref[rows, :]
            top = jnp.maximum(before, lse)
            w_before = jnp.exp2(before - top)
            w_now = jnp.exp2(lse - top)
            both = w_before + w_now
            o = (w_before * prev_o_ref[rows, :] + w_now * o) / both
            lse = top + jnp.log2(both)
        if not last:
            o_ref[rows, :] = o
            lse_ref[rows, :] = lse
            return peak
        out_ref = out_refs[b // per_chunk]
        for j in range(row_block // tokens):
            h = (b % per_chunk) * (row_block // tokens) + j
            part = slice(j * tokens, (j + 1) * tokens)
            lanes = slice(h * hd, (h + 1) * hd)
            out_ref[:tokens, lanes] = o[part].astype(jnp.bfloat16)
            flat = lse[part].T[:PART_ROWS, :]
            high = flat.astype(jnp.bfloat16).astype(jnp.float32)
            middle = (flat - high).astype(jnp.bfloat16).astype(jnp.float32)
            row = lax.broadcasted_iota(jnp.int32, flat.shape, 0)
            out_ref[tokens:, lanes] = jnp.where(
                row == 0, high, jnp.where(row == 1, middle, jnp.where(row == 2, flat - high - middle, 0.0))
            ).astype(jnp.bfloat16)
        return peak

    blocks = count * per_chunk
    peak = low
    for t in range(tiles):
        peak = score_tile(0, t, score_a, peak)
    looped = 0
    if not last and per_chunk % 2 == 0 and count > 1:
        looped = blocks - 2

        def pair(i, peak):
            peak = one_block(2 * i, score_a, peak, 2 * i + 1, score_b)
            return one_block(2 * i + 1, score_b, peak, 2 * i + 2, score_a)

        peak = lax.fori_loop(0, looped // 2, pair, peak)
    for b in range(looped, blocks):
        scores, into = (score_a, score_b) if b % 2 == 0 else (score_b, score_a)
        peak = one_block(b, scores, peak, b + 1 if b + 1 < blocks else None, into)


def attend(meta, places, queries, keys, values, slots, shard, state, state_block, last):
    count = len(queries)
    tokens, width = queries[0].shape
    whole = keys.shape[0] > slots
    hd = keys.shape[1] // 2 if whole else keys.shape[1]
    rows = tokens * (width // hd)
    row_block = min(MAX_BLOCK, rows)
    key_tile = min(MAX_TILE, slots)
    holders = meta.shape[0] // 2 - places
    first = state is None

    def fixed(shape):
        return pl.BlockSpec(shape, lambda i, meta_ref: (0, 0))

    def shard_at(column):
        if not whole:
            return pl.BlockSpec((slots, hd), lambda i, meta_ref: (0, 0))
        return pl.BlockSpec(
            (slots, hd), lambda i, meta_ref: (meta_ref[2 * places + holders + shard], column)
        )

    in_specs = [fixed((tokens, width))] * count + [shard_at(0), shard_at(1)]
    operands = [meta, *queries, keys, values]
    if not first:
        in_specs += [pl.BlockSpec((count * rows, hd), lambda i, meta_ref: (state_block, 0))] * 2
        operands += state
    if last:
        out_shape = [jax.ShapeDtypeStruct((tokens + PART_ROWS, width), jnp.bfloat16)] * count
        out_specs = [fixed((tokens + PART_ROWS, width))] * count
    else:
        out_shape = [jax.ShapeDtypeStruct((count * rows, hd), jnp.float32)] * 2
        out_specs = [fixed((count * rows, hd))] * 2
    return pl.pallas_call(
        functools.partial(attend_kernel, count, first, last, shard, places),
        grid_spec=pltpu.PrefetchScalarGridSpec(
            num_scalar_prefetch=1,
            grid=(1,),
            in_specs=in_specs,
            out_specs=out_specs,
            scratch_shapes=[
                pltpu.VMEM((count * rows, 2 * hd), jnp.bfloat16),
                pltpu.VMEM((slots, 2 * hd), jnp.bfloat16),
                pltpu.VMEM((slots, 2 * hd), jnp.bfloat16),
                pltpu.VMEM((slots // key_tile, row_block, key_tile), jnp.float32),
                pltpu.VMEM((slots // key_tile, row_block, key_tile), jnp.float32),
            ],
        ),
        out_shape=out_shape,
        compiler_params=pltpu.CompilerParams(vmem_limit_bytes=40 * MIB),
        cost_estimate=pl.CostEstimate(
            flops=4 * count * rows * slots * hd if first else 0,
            bytes_accessed=0,
            transcendentals=0,
        ),
        name="attend_last" if last else "attend",
    )(*operands)


def combine_kernel(capacity, meta_ref, q_ref, k_ref, v_ref, *refs):
    *part_refs, out_ref, stacked = refs
    _, tokens, hd = k_ref.shape
    width = q_ref.shape[2]
    heads = width // hd
    scale = LOG2E / math.sqrt(hd)
    places = len(part_refs) * capacity
    for i, part_ref in enumerate(part_refs):
        for slot in range(capacity):
            r = meta_ref[i * capacity + slot]

            @pl.when(meta_ref[places + i * capacity + slot] > 0)
            def _(r=r, part_ref=part_ref, slot=slot):
                for h in range(heads):
                    stacked[h * tokens : (h + 1) * tokens, :] = q_ref[r, :, h * hd : (h + 1) * hd]
                s = nt_dot(stacked[...], k_ref[r]) * scale
                row = lax.broadcasted_iota(jnp.int32, s.shape, 0) % tokens
                seen = row >= lax.broadcasted_iota(jnp.int32, s.shape, 1)
                s = jnp.where(seen, s, MASKED)
                m = jnp.max(s, axis=1, keepdims=True)
                w = jnp.where(seen, jnp.exp2(s - m), 0.0)
                total = jnp.sum(w, axis=1, keepdims=True)
                o = jnp.dot(w.astype(jnp.bfloat16), v_ref[r], preferred_element_type=jnp.float32)
                base = part_ref.shape[0] - PART_ROWS
                for h in range(heads):
                    rows = slice(h * tokens, (h + 1) * tokens)
                    lanes = slice(h * hd, (h + 1) * hd)
                    far = part_ref[slot * tokens : (slot + 1) * tokens, lanes].astype(jnp.float32)
                    pieces = part_ref[base:, lanes].astype(jnp.float32)
                    flat = pieces[0:1] + pieces[1:2] + pieces[2:3]
                    lse = jnp.broadcast_to(flat, (hd, hd)).T[slot * tokens : (slot + 1) * tokens, :]
                    top = jnp.maximum(m[rows], lse)
                    own_scale = jnp.exp2(m[rows] - top)
                    far_scale = jnp.exp2(lse - top)
                    out_ref[r, :, lanes] = (
                        (own_scale * o[rows] + far_scale * far) / (own_scale * total[rows] + far_scale)
                    ).astype(jnp.bfloat16)


def combine(meta, capacity, q, keys, values, parts):
    responses, tokens, width = q.shape
    hd = keys.shape[-1]
    heads = width // hd
    return pl.pallas_call(
        functools.partial(combine_kernel, capacity),
        out_shape=jax.ShapeDtypeStruct(q.shape, jnp.bfloat16),
        in_specs=[pl.BlockSpec(memory_space=pltpu.SMEM)]
        + [pl.BlockSpec(memory_space=pltpu.VMEM)] * (3 + len(parts)),
        out_specs=pl.BlockSpec(memory_space=pltpu.VMEM),
        scratch_shapes=[pltpu.VMEM((heads * tokens, hd), jnp.bfloat16)],
        compiler_params=pltpu.CompilerParams(vmem_limit_bytes=24 * MIB),
        cost_estimate=pl.CostEstimate(flops=0, bytes_accessed=0, transcendentals=0),
        name="combine",
    )(meta, q, keys, values, *parts)


def multiply_kernel(kept_first_ref, *refs):
    *row_refs, weight_ref, kept_ref, sent_ref, rows = refs
    count = row_refs[0].shape[0]

    @pl.when(pl.program_id(0) == 0)
    def _():
        for first, order in ((1, (0, 1, 2, 3)), (0, (2, 3, 0, 1))):

            @pl.when(kept_first_ref[0] == first)
            def _(order=order):
                for place, i in enumerate(order):
                    rows[place * count : (place + 1) * count, :] = row_refs[i][...]

    for place, ref in ((1, sent_ref), (0, kept_ref)):
        for part in range(2):
            at = slice(part * count, (part + 1) * count)
            x = rows[2 * place * count + part * count : 2 * place * count + (part + 1) * count, :]
            ref[at, :] = jnp.dot(x, weight_ref[0], preferred_element_type=jnp.float32).astype(ref.dtype)


def multiply(kept_first, row_parts, weights, width, piece):
    count, depth = row_parts[0].shape
    blocks = weights.shape[0]
    rows = pl.BlockSpec((count, depth), lambda j: (0, 0))
    out = pl.BlockSpec((2 * count, width), lambda j: (0, j))
    return pl.pallas_call(
        multiply_kernel,
        grid=(blocks,),
        out_shape=[jax.ShapeDtypeStruct((2 * count, blocks * width), jnp.bfloat16)] * 2,
        in_specs=[pl.BlockSpec(memory_space=pltpu.SMEM)]
        + [rows] * 4
        + [pl.BlockSpec((1, depth, width), lambda j: (j, 0, piece))],
        out_specs=[out] * 2,
        scratch_shapes=[pltpu.VMEM((4 * count, depth), jnp.bfloat16)],
        compiler_params=pltpu.CompilerParams(vmem_limit_bytes=28 * MIB),
        cost_estimate=pl.CostEstimate(flops=0, bytes_accessed=0, transcendentals=0),
        name="multiply",
    )(kept_first.reshape(1), *row_parts, weights)


def arrange_kernel(pieces, flags_ref, *refs):
    *parts, out_ref = refs
    own, direct, back = parts[:pieces], parts[pieces : 2 * pieces], parts[2 * pieces :]
    count, width = back[0].shape
    for holder in range(2):

        @pl.when(flags_ref[1] == holder)
        def _(holder=holder):
            for i in range(pieces):
                here = slice((holder * pieces + i) * width, (holder * pieces + i + 1) * width)
                there = slice(((1 - holder) * pieces + i) * width, ((1 - holder) * pieces + i + 1) * width)
                out_ref[:, there] = back[i][...]

                @pl.when(flags_ref[0] != 0)
                def _(here=here, i=i):
                    out_ref[:, here] = own[i][:count, :]

                @pl.when(flags_ref[0] == 0)
                def _(here=here, i=i):
                    out_ref[:, here] = direct[i][...]


def arrange(same, holder, own, direct, back):
    count, width = back[0].shape
    pieces = len(back)
    vmem = pl.BlockSpec(memory_space=pltpu.VMEM)
    return pl.pallas_call(
        functools.partial(arrange_kernel, pieces),
        out_shape=jax.ShapeDtypeStruct((count, 2 * pieces * width), back[0].dtype),
        in_specs=[pl.BlockSpec(memory_space=pltpu.SMEM)] + [vmem] * (3 * pieces),
        out_specs=vmem,
        compiler_params=pltpu.CompilerParams(vmem_limit_bytes=16 * MIB),
        cost_estimate=pl.CostEstimate(flops=0, bytes_accessed=0, transcendentals=0),
        name="arrange",
    )(jnp.stack([same.astype(jnp.int32), holder.astype(jnp.int32)]), *own, *direct, *back)


def project(rows, weights, others, plane, holder):
    group = lax.axis_index("kvh")
    chip = group // 2
    same = group % 2 == plane % 2
    count = rows.shape[0]
    per_half = 2
    width = weights[0].shape[1] // per_half
    upper = plane >= 2

    def send(x, to, keep=lambda p, k: True):
        pairs = []
        for p in range(4):
            for h in range(2):
                for k in range(4):
                    if keep(p, k):
                        q, g, m = to(p, h, k)
                        pairs.append(((p * 2 + h) * 4 + k, (q * 2 + g) * 4 + m))
        return lax.ppermute(x, ("ctx", "kvh"), pairs)

    def fetch(x):
        return (
            x,
            send(x, lambda p, h, k: (p, 1 - h, k)),
            send(x, lambda p, h, k: (p ^ 1, h, k)),
            send(x, lambda p, h, k: (p ^ 1, 1 - h, k)),
        )

    def add(a, b):
        return (a.astype(jnp.float32) + b.astype(jnp.float32)).astype(jnp.bfloat16)

    def chip_sums(product, *wanted):
        kept, sent = product
        got = after(send(sent, lambda p, h, k: (p, h, k ^ 1)), *wanted)
        total = add(kept, got)
        low, high = total[:, :width], total[:, width:]
        return jnp.where(chip == 0, low, high), jnp.where(chip == 0, high, low)

    def over_x(pairs):
        return [send(sent, lambda p, h, k: (p, h, k ^ 2)) for _, sent in pairs]

    def deliver(total):
        direct = send(
            total[:count], lambda p, h, k: (p ^ 1, h, k ^ 1), lambda p, k: k % 2 != p % 2
        )
        back = send(
            total[count:],
            lambda p, h, k: (p, 1 - h, k) if k % 2 == p % 2 else (p ^ 1, 1 - h, k ^ 1),
        )
        return total, direct, back

    fetched = fetch(rows)
    def half_products(half, other):
        own = weights[half]
        columns = jnp.stack([jnp.where(upper, other, own), jnp.where(upper, own, other)])
        flag = same.astype(jnp.int32)
        return [multiply(flag, fetched, columns, width, i) for i in range(per_half)]

    def finish(pairs, got):
        kept = jnp.concatenate([x for x, _ in pairs], axis=1)
        return deliver(add(kept, jnp.concatenate(got, axis=1)))

    products = half_products(0, others[0])
    sums = [chip_sums(products[0], others[1])] + [chip_sums(x) for x in products[1:]]
    products = half_products(1, after(others[1], *(x for pair in sums for x in pair)))
    got = [after(x, *(sent for _, sent in products)) for x in over_x(sums)]
    later = [chip_sums(x, got[0]) for x in products]
    delivered = [finish(sums, got), finish(later, over_x(later))]
    return arrange(same, holder, *zip(*delivered))


def local(
    queries, resp_keys, resp_values, prefix_keys, prefix_values, prefix_len, prompt_of, out_weight
):
    ctx_count = lax.axis_size("ctx")
    kvh_count = lax.axis_size("kvh")
    position = lax.axis_index("ctx")
    own_queries = queries[:, :, 0]
    own_keys = resp_keys[:, :, 0]
    own_values = resp_values[:, :, 0]
    resp_count, tokens_each, width = own_queries.shape
    slot_count = prefix_keys.shape[0]
    prompts = prefix_len.shape[0]
    holders = ctx_count // prompts
    my_prompt = position // holders
    my_holder = position % holders
    capacity = max(LANES // tokens_each, resp_count // prompts)
    places = prompts * capacity
    by_plane = kvh_count == prompts == 4 and holders == 2

    def cross(x, i):
        pairs = [(p * holders + h, (p ^ i) * holders + h) for p in range(prompts) for h in range(holders)]
        return lax.ppermute(x, "ctx", pairs)

    chunks, meta = pack(prompt_of, prefix_len, own_queries, capacity, holders, slot_count)
    chunks = chunks[:1] + [cross(x, i) for i, x in enumerate(chunks) if i > 0]
    near = prefix_keys[:, 0], prefix_values[:, 0]
    away = chunks[:0:-1]
    if by_plane:
        half = out_weight.shape[1] // 2
        weights = [out_weight[:, :half], out_weight[:, half:]]
        weights[0] = after(weights[0], *away)
        others = [cross(x, 2) for x in weights]
        shards = [near, near]
        shards[1] = [
            lax.ppermute(x, "ctx", [(c, c ^ 1) for c in range(ctx_count)]) for x in shards[1]
        ]
    else:
        lines = [[p * holders + h for h in range(holders)] for p in range(prompts)]
        joined = jnp.concatenate(near, axis=1)
        joined = lax.all_gather(joined, "ctx", axis=0, tiled=True, axis_index_groups=lines)
        shards = [near] + [(joined, joined)] * (holders - 1)

    state_home = state_away = None
    for shard in range(holders - 1):
        kv = shards[shard]
        state_home = attend(meta, places, chunks[:1], *kv, slot_count, shard, state_home, 0, False)
        state_home, away = lax.optimization_barrier((state_home, away))
        state_away = attend(meta, places, away, *kv, slot_count, shard, state_away, 0, False)
    shard = holders - 1
    far = shards[shard]
    done = [None] * prompts
    for where, members in enumerate([range(prompts - 1, 1, -1), [1]]):
        queries_now = [away[prompts - 1 - i] for i in members]
        block = 0 if where == 0 else prompts - 2
        results = attend(meta, places, queries_now, *far, slot_count, shard, state_away, block, True)
        for i, x in zip(members, results):
            done[i] = cross(x, i)
    (done[0],) = attend(meta, places, chunks[:1], *far, slot_count, shard, state_home, 0, True)
    if by_plane:
        others[0], done[0] = lax.optimization_barrier((others[0], done[0]))
    attended = combine(meta, capacity, own_queries, own_keys, own_values, done)
    rows = attended.reshape(resp_count * tokens_each, width)

    if by_plane:
        projected = project(rows, weights, others, my_prompt, my_holder)
    else:
        weights = lax.all_gather(out_weight, "ctx", axis=1, tiled=True)
        terms = jnp.dot(rows, weights, preferred_element_type=jnp.float32)
        projected = lax.psum_scatter(
            terms.astype(jnp.bfloat16), "kvh", scatter_dimension=1, tiled=True
        )
    return (attended[:, :, None, :], projected)


def solution(mesh):
    in_specs = (
        P("ctx", None, "kvh", None),
        P("ctx", None, "kvh", None),
        P("ctx", None, "kvh", None),
        P("ctx", "kvh", None),
        P("ctx", "kvh", None),
        P(),
        P(),
        P("kvh", "ctx"),
    )
    out_specs = (P("ctx", None, "kvh", None), P("ctx", "kvh"))
    return jax.shard_map(local, mesh=mesh, in_specs=in_specs, out_specs=out_specs, check_vma=False)
```

```python
import functools
import math

import jax
import jax.numpy as jnp
from jax import lax
from jax.experimental import pallas as pl
from jax.experimental.pallas import tpu as pltpu
from jax.sharding import PartitionSpec as P

MASKED = -1e30
LOG2E = math.log2(math.e)
LANES = 128
PART_ROWS = 16
MAX_TILE = 1024
MAX_BLOCK = 512
MIB = 1024 * 1024


def nt_dot(a, b):
    return lax.dot_general(a, b, (((1,), (1,)), ((), ())), preferred_element_type=jnp.float32)


def after(x, *others):
    return lax.optimization_barrier((x, *others))[0]


def pack_kernel(capacity, holders, slots, prompt_ref, len_ref, q_ref, *refs):
    *chunk_refs, meta_ref = refs
    responses, tokens, _ = q_ref.shape
    position = lax.axis_index("ctx")
    mine, holder = position // holders, position % holders
    named = [prompt_ref[position * responses + r] for r in range(responses)]
    ranks = []
    for r in range(responses):
        rank = jnp.int32(0)
        for before in range(r):
            rank += (named[before] == named[r]).astype(jnp.int32)
        ranks.append(rank)
    places = len(chunk_refs) * capacity
    for i, chunk_ref in enumerate(chunk_refs):
        for slot in range(capacity):
            chosen, present = jnp.int32(0), jnp.int32(0)
            for r in range(responses):
                hit = ((named[r] == mine ^ i) & (ranks[r] == slot)).astype(jnp.int32)
                chosen += hit * r
                present += hit
            meta_ref[i * capacity + slot] = chosen
            meta_ref[places + i * capacity + slot] = present
            rows = slice(slot * tokens, (slot + 1) * tokens)
            chunk_ref[rows, :] = q_ref[chosen]

            @pl.when(present == 0)
            def _(chunk_ref=chunk_ref, rows=rows):
                chunk_ref[rows, :] = jnp.zeros_like(chunk_ref[rows, :])

    length = len_ref[mine]
    for j in range(holders):
        place = (holder + j) % holders
        meta_ref[2 * places + j] = jnp.clip(length - place * slots, 0, slots)
        meta_ref[2 * places + holders + j] = place


def pack(prompt_of, prefix_len, q, capacity, holders, slots):
    _, tokens, width = q.shape
    prompts = prefix_len.shape[0]
    smem = pl.BlockSpec(memory_space=pltpu.SMEM)
    vmem = pl.BlockSpec(memory_space=pltpu.VMEM)
    *chunks, meta = pl.pallas_call(
        functools.partial(pack_kernel, capacity, holders, slots),
        out_shape=[jax.ShapeDtypeStruct((capacity * tokens, width), q.dtype)] * prompts
        + [jax.ShapeDtypeStruct((2 * (prompts * capacity + holders),), jnp.int32)],
        in_specs=[smem, smem, vmem],
        out_specs=[vmem] * prompts + [smem],
        compiler_params=pltpu.CompilerParams(vmem_limit_bytes=16 * MIB),
        cost_estimate=pl.CostEstimate(flops=0, bytes_accessed=4 * q.size, transcendentals=0),
        name="pack",
    )(prompt_of, prefix_len, q)
    return chunks, meta


def attend_kernel(count, first, last, shard, places, meta_ref, *refs):
    q_refs, (k_ref, v_ref, *refs) = refs[:count], refs[count:]
    if not first:
        prev_o_ref, prev_lse_ref, *refs = refs
    if last:
        out_refs, refs = refs[:count], refs[count:]
    else:
        o_ref, lse_ref, *refs = refs
    qext, kext, vext, score_a, score_b = refs
    tokens = q_refs[0].shape[0]
    slots, hd = k_ref.shape
    heads = q_refs[0].shape[1] // hd
    scale = LOG2E / math.sqrt(hd)
    tiles, row_block, key_tile = score_a.shape
    per_chunk = heads * tokens // row_block
    live = meta_ref[2 * places + shard]

    @pl.when(live == slots)
    def _():
        for t in range(tiles):
            at = slice(t * key_tile, (t + 1) * key_tile)
            keys = k_ref[at, :]
            kext[at, :hd] = keys
            kext[at, hd:] = keys
            vext[at, :hd] = v_ref[at, :]
            vext[at, hd:] = jnp.ones((key_tile, hd), jnp.bfloat16)

    @pl.when(live != slots)
    def _():
        def prepare(step, carry):
            at = pl.ds(pl.multiple_of(step * key_tile, key_tile), key_tile)
            alive = step * key_tile + lax.broadcasted_iota(jnp.int32, (key_tile, hd), 0) < live
            keys = jnp.where(alive, k_ref[at, :].astype(jnp.float32), k_ref[0:1, :].astype(jnp.float32))
            keys = keys.astype(jnp.bfloat16)
            kext[at, :hd] = keys
            kext[at, hd:] = keys
            vext[at, :hd] = jnp.where(alive, v_ref[at, :].astype(jnp.float32), 0.0).astype(jnp.bfloat16)
            vext[at, hd:] = jnp.where(alive, 1.0, 0.0).astype(jnp.bfloat16)
            return carry

        lax.fori_loop(0, tiles, prepare, 0)

    for c, q_ref in enumerate(q_refs):
        for h in range(heads):
            rows = slice((c * heads + h) * tokens, (c * heads + h + 1) * tokens)
            x = q_ref[:, h * hd : (h + 1) * hd].astype(jnp.float32) * scale
            high = x.astype(jnp.bfloat16)
            qext[rows, :hd] = high
            qext[rows, hd:] = (x - high.astype(jnp.float32)).astype(jnp.bfloat16)

    low = jnp.full((row_block, LANES), MASKED, jnp.float32)

    def rows_of(b):
        if isinstance(b, int):
            return slice(b * row_block, (b + 1) * row_block)
        return pl.ds(pl.multiple_of(b * row_block, row_block), row_block)

    def score_tile(b, t, into, peak):
        s = nt_dot(qext[rows_of(b), :], kext[t * key_tile : (t + 1) * key_tile, :])
        into[t] = s
        for j in range(key_tile // LANES):
            peak = jnp.maximum(peak, s[:, j * LANES : (j + 1) * LANES])
        return peak

    def one_block(b, scores, peak, following, into):
        m = jnp.max(peak, axis=1, keepdims=True)
        peak = low
        acc = jnp.zeros((row_block, 2 * hd), jnp.float32)
        for t in range(tiles):
            if following is not None:
                peak = score_tile(following, t, into, peak)
            w = jnp.exp2(scores[t] - m).astype(jnp.bfloat16)
            acc = acc + jnp.dot(
                w, vext[t * key_tile : (t + 1) * key_tile, :], preferred_element_type=jnp.float32
            )
        total = acc[:, hd:]
        some = total > 0.0
        safe = jnp.where(some, total, 1.0)
        o = acc[:, :hd] / safe
        lse = jnp.where(some, m + jnp.log2(safe), MASKED)
        rows = rows_of(b)
        if not first:
            before = prev_lse_ref[rows, :]
            top = jnp.maximum(before, lse)
            w_before = jnp.exp2(before - top)
            w_now = jnp.exp2(lse - top)
            both = w_before + w_now
            o = (w_before * prev_o_ref[rows, :] + w_now * o) / both
            lse = top + jnp.log2(both)
        if not last:
            o_ref[rows, :] = o
            lse_ref[rows, :] = lse
            return peak
        out_ref = out_refs[b // per_chunk]
        for j in range(row_block // tokens):
            h = (b % per_chunk) * (row_block // tokens) + j
            part = slice(j * tokens, (j + 1) * tokens)
            lanes = slice(h * hd, (h + 1) * hd)
            out_ref[:tokens, lanes] = o[part].astype(jnp.bfloat16)
            flat = lse[part].T[:PART_ROWS, :]
            high = flat.astype(jnp.bfloat16).astype(jnp.float32)
            middle = (flat - high).astype(jnp.bfloat16).astype(jnp.float32)
            row = lax.broadcasted_iota(jnp.int32, flat.shape, 0)
            out_ref[tokens:, lanes] = jnp.where(
                row == 0, high, jnp.where(row == 1, middle, jnp.where(row == 2, flat - high - middle, 0.0))
            ).astype(jnp.bfloat16)
        return peak

    blocks = count * per_chunk
    peak = low
    for t in range(tiles):
        peak = score_tile(0, t, score_a, peak)
    looped = 0
    if not last and per_chunk % 2 == 0 and count > 1:
        looped = blocks - 2

        def pair(i, peak):
            peak = one_block(2 * i, score_a, peak, 2 * i + 1, score_b)
            return one_block(2 * i + 1, score_b, peak, 2 * i + 2, score_a)

        peak = lax.fori_loop(0, looped // 2, pair, peak)
    for b in range(looped, blocks):
        scores, into = (score_a, score_b) if b % 2 == 0 else (score_b, score_a)
        peak = one_block(b, scores, peak, b + 1 if b + 1 < blocks else None, into)


def attend(meta, places, queries, keys, values, slots, shard, state, state_block, last):
    count = len(queries)
    tokens, width = queries[0].shape
    whole = keys.shape[0] > slots
    hd = keys.shape[1] // 2 if whole else keys.shape[1]
    rows = tokens * (width // hd)
    row_block = min(MAX_BLOCK, rows)
    key_tile = min(MAX_TILE, slots)
    holders = meta.shape[0] // 2 - places
    first = state is None

    def fixed(shape):
        return pl.BlockSpec(shape, lambda i, meta_ref: (0, 0))

    def shard_at(column):
        if not whole:
            return pl.BlockSpec((slots, hd), lambda i, meta_ref: (0, 0))
        return pl.BlockSpec(
            (slots, hd), lambda i, meta_ref: (meta_ref[2 * places + holders + shard], column)
        )

    in_specs = [fixed((tokens, width))] * count + [shard_at(0), shard_at(1)]
    operands = [meta, *queries, keys, values]
    if not first:
        in_specs += [pl.BlockSpec((count * rows, hd), lambda i, meta_ref: (state_block, 0))] * 2
        operands += state
    if last:
        out_shape = [jax.ShapeDtypeStruct((tokens + PART_ROWS, width), jnp.bfloat16)] * count
        out_specs = [fixed((tokens + PART_ROWS, width))] * count
    else:
        out_shape = [jax.ShapeDtypeStruct((count * rows, hd), jnp.float32)] * 2
        out_specs = [fixed((count * rows, hd))] * 2
    return pl.pallas_call(
        functools.partial(attend_kernel, count, first, last, shard, places),
        grid_spec=pltpu.PrefetchScalarGridSpec(
            num_scalar_prefetch=1,
            grid=(1,),
            in_specs=in_specs,
            out_specs=out_specs,
            scratch_shapes=[
                pltpu.VMEM((count * rows, 2 * hd), jnp.bfloat16),
                pltpu.VMEM((slots, 2 * hd), jnp.bfloat16),
                pltpu.VMEM((slots, 2 * hd), jnp.bfloat16),
                pltpu.VMEM((slots // key_tile, row_block, key_tile), jnp.float32),
                pltpu.VMEM((slots // key_tile, row_block, key_tile), jnp.float32),
            ],
        ),
        out_shape=out_shape,
        compiler_params=pltpu.CompilerParams(vmem_limit_bytes=40 * MIB),
        cost_estimate=pl.CostEstimate(
            flops=4 * count * rows * slots * hd if first else 0,
            bytes_accessed=0,
            transcendentals=0,
        ),
        name="attend_last" if last else "attend",
    )(*operands)


def combine_kernel(capacity, meta_ref, q_ref, k_ref, v_ref, *refs):
    *part_refs, out_ref, stacked = refs
    _, tokens, hd = k_ref.shape
    width = q_ref.shape[2]
    heads = width // hd
    scale = LOG2E / math.sqrt(hd)
    places = len(part_refs) * capacity
    for i, part_ref in enumerate(part_refs):
        for slot in range(capacity):
            r = meta_ref[i * capacity + slot]

            @pl.when(meta_ref[places + i * capacity + slot] > 0)
            def _(r=r, part_ref=part_ref, slot=slot):
                for h in range(heads):
                    stacked[h * tokens : (h + 1) * tokens, :] = q_ref[r, :, h * hd : (h + 1) * hd]
                s = nt_dot(stacked[...], k_ref[r]) * scale
                row = lax.broadcasted_iota(jnp.int32, s.shape, 0) % tokens
                seen = row >= lax.broadcasted_iota(jnp.int32, s.shape, 1)
                s = jnp.where(seen, s, MASKED)
                m = jnp.max(s, axis=1, keepdims=True)
                w = jnp.where(seen, jnp.exp2(s - m), 0.0)
                total = jnp.sum(w, axis=1, keepdims=True)
                o = jnp.dot(w.astype(jnp.bfloat16), v_ref[r], preferred_element_type=jnp.float32)
                base = part_ref.shape[0] - PART_ROWS
                for h in range(heads):
                    rows = slice(h * tokens, (h + 1) * tokens)
                    lanes = slice(h * hd, (h + 1) * hd)
                    far = part_ref[slot * tokens : (slot + 1) * tokens, lanes].astype(jnp.float32)
                    pieces = part_ref[base:, lanes].astype(jnp.float32)
                    flat = pieces[0:1] + pieces[1:2] + pieces[2:3]
                    lse = jnp.broadcast_to(flat, (hd, hd)).T[slot * tokens : (slot + 1) * tokens, :]
                    top = jnp.maximum(m[rows], lse)
                    own_scale = jnp.exp2(m[rows] - top)
                    far_scale = jnp.exp2(lse - top)
                    out_ref[r, :, lanes] = (
                        (own_scale * o[rows] + far_scale * far) / (own_scale * total[rows] + far_scale)
                    ).astype(jnp.bfloat16)


def combine(meta, capacity, q, keys, values, parts):
    responses, tokens, width = q.shape
    hd = keys.shape[-1]
    heads = width // hd
    return pl.pallas_call(
        functools.partial(combine_kernel, capacity),
        out_shape=jax.ShapeDtypeStruct(q.shape, jnp.bfloat16),
        in_specs=[pl.BlockSpec(memory_space=pltpu.SMEM)]
        + [pl.BlockSpec(memory_space=pltpu.VMEM)] * (3 + len(parts)),
        out_specs=pl.BlockSpec(memory_space=pltpu.VMEM),
        scratch_shapes=[pltpu.VMEM((heads * tokens, hd), jnp.bfloat16)],
        compiler_params=pltpu.CompilerParams(vmem_limit_bytes=24 * MIB),
        cost_estimate=pl.CostEstimate(flops=0, bytes_accessed=0, transcendentals=0),
        name="combine",
    )(meta, q, keys, values, *parts)


def multiply_kernel(kept_first_ref, *refs):
    *row_refs, weight_ref, kept_ref, sent_ref, rows = refs
    count = row_refs[0].shape[0]

    @pl.when(pl.program_id(0) == 0)
    def _():
        for first, order in ((1, (0, 1, 2, 3)), (0, (2, 3, 0, 1))):

            @pl.when(kept_first_ref[0] == first)
            def _(order=order):
                for place, i in enumerate(order):
                    rows[place * count : (place + 1) * count, :] = row_refs[i][...]

    for place, ref in ((1, sent_ref), (0, kept_ref)):
        for part in range(2):
            at = slice(part * count, (part + 1) * count)
            x = rows[2 * place * count + part * count : 2 * place * count + (part + 1) * count, :]
            ref[at, :] = jnp.dot(x, weight_ref[0], preferred_element_type=jnp.float32).astype(ref.dtype)


def multiply(kept_first, row_parts, weights, width, piece):
    count, depth = row_parts[0].shape
    blocks = weights.shape[0]
    rows = pl.BlockSpec((count, depth), lambda j: (0, 0))
    out = pl.BlockSpec((2 * count, width), lambda j: (0, j))
    return pl.pallas_call(
        multiply_kernel,
        grid=(blocks,),
        out_shape=[jax.ShapeDtypeStruct((2 * count, blocks * width), jnp.bfloat16)] * 2,
        in_specs=[pl.BlockSpec(memory_space=pltpu.SMEM)]
        + [rows] * 4
        + [pl.BlockSpec((1, depth, width), lambda j: (j, 0, piece))],
        out_specs=[out] * 2,
        scratch_shapes=[pltpu.VMEM((4 * count, depth), jnp.bfloat16)],
        compiler_params=pltpu.CompilerParams(vmem_limit_bytes=28 * MIB),
        cost_estimate=pl.CostEstimate(flops=0, bytes_accessed=0, transcendentals=0),
        name="multiply",
    )(kept_first.reshape(1), *row_parts, weights)


def arrange_kernel(pieces, flags_ref, *refs):
    *parts, out_ref = refs
    own, direct, back = parts[:pieces], parts[pieces : 2 * pieces], parts[2 * pieces :]
    count, width = back[0].shape
    for holder in range(2):

        @pl.when(flags_ref[1] == holder)
        def _(holder=holder):
            for i in range(pieces):
                here = slice((holder * pieces + i) * width, (holder * pieces + i + 1) * width)
                there = slice(((1 - holder) * pieces + i) * width, ((1 - holder) * pieces + i + 1) * width)
                out_ref[:, there] = back[i][...]

                @pl.when(flags_ref[0] != 0)
                def _(here=here, i=i):
                    out_ref[:, here] = own[i][:count, :]

                @pl.when(flags_ref[0] == 0)
                def _(here=here, i=i):
                    out_ref[:, here] = direct[i][...]


def arrange(same, holder, own, direct, back):
    count, width = back[0].shape
    pieces = len(back)
    vmem = pl.BlockSpec(memory_space=pltpu.VMEM)
    return pl.pallas_call(
        functools.partial(arrange_kernel, pieces),
        out_shape=jax.ShapeDtypeStruct((count, 2 * pieces * width), back[0].dtype),
        in_specs=[pl.BlockSpec(memory_space=pltpu.SMEM)] + [vmem] * (3 * pieces),
        out_specs=vmem,
        compiler_params=pltpu.CompilerParams(vmem_limit_bytes=16 * MIB),
        cost_estimate=pl.CostEstimate(flops=0, bytes_accessed=0, transcendentals=0),
        name="arrange",
    )(jnp.stack([same.astype(jnp.int32), holder.astype(jnp.int32)]), *own, *direct, *back)


def project(rows, weights, others, plane, holder):
    group = lax.axis_index("kvh")
    chip = group // 2
    same = group % 2 == plane % 2
    count = rows.shape[0]
    per_half = 2
    width = weights[0].shape[1] // per_half
    upper = plane >= 2

    def send(x, to, keep=lambda p, k: True):
        pairs = []
        for p in range(4):
            for h in range(2):
                for k in range(4):
                    if keep(p, k):
                        q, g, m = to(p, h, k)
                        pairs.append(((p * 2 + h) * 4 + k, (q * 2 + g) * 4 + m))
        return lax.ppermute(x, ("ctx", "kvh"), pairs)

    def fetch(x):
        near = send(x, lambda p, h, k: (p ^ 1, h, k))
        swapped = send(x, lambda p, h, k: (p, 1 - h, k))
        return x, swapped, near, send(near, lambda p, h, k: (p, 1 - h, k))

    def add(a, b):
        return (a.astype(jnp.float32) + b.astype(jnp.float32)).astype(jnp.bfloat16)

    def chip_sums(product, *wanted):
        kept, sent = product
        got = after(send(sent, lambda p, h, k: (p, h, k ^ 1)), *wanted)
        total = add(kept, got)
        low, high = total[:, :width], total[:, width:]
        return jnp.where(chip == 0, low, high), jnp.where(chip == 0, high, low)

    def over_x(pairs):
        return [send(sent, lambda p, h, k: (p, h, k ^ 2)) for _, sent in pairs]

    def deliver(total):
        direct = send(
            total[:count], lambda p, h, k: (p ^ 1, h, k ^ 1), lambda p, k: k % 2 != p % 2
        )
        back = send(
            total[count:],
            lambda p, h, k: (p, 1 - h, k) if k % 2 == p % 2 else (p ^ 1, 1 - h, k ^ 1),
        )
        return total, direct, back

    fetched = fetch(rows)
    def half_columns(half, other):
        own = weights[half]
        return jnp.stack([jnp.where(upper, other, own), jnp.where(upper, own, other)])

    def product(columns, piece):
        return multiply(same.astype(jnp.int32), fetched, columns, width, piece)

    def finish(pairs, got):
        kept = jnp.concatenate([x for x, _ in pairs], axis=1)
        return deliver(add(kept, jnp.concatenate(got, axis=1)))

    columns = half_columns(0, others[0])
    sums = [chip_sums(product(columns, 0), others[1])]
    for piece in range(1, per_half):
        sums.append(chip_sums(product(columns, piece)))
    columns = half_columns(1, after(others[1], *(x for pair in sums for x in pair)))
    products = [product(columns, i) for i in range(per_half)]
    got = [after(x, *(sent for _, sent in products)) for x in over_x(sums)]
    later = [chip_sums(x, got[0]) for x in products]
    delivered = [finish(sums, got), finish(later, over_x(later))]
    return arrange(same, holder, *zip(*delivered))


def local(
    queries, resp_keys, resp_values, prefix_keys, prefix_values, prefix_len, prompt_of, out_weight
):
    ctx_count = lax.axis_size("ctx")
    kvh_count = lax.axis_size("kvh")
    position = lax.axis_index("ctx")
    own_queries = queries[:, :, 0]
    own_keys = resp_keys[:, :, 0]
    own_values = resp_values[:, :, 0]
    resp_count, tokens_each, width = own_queries.shape
    slot_count = prefix_keys.shape[0]
    prompts = prefix_len.shape[0]
    holders = ctx_count // prompts
    my_prompt = position // holders
    my_holder = position % holders
    capacity = max(LANES // tokens_each, resp_count // prompts)
    places = prompts * capacity
    by_plane = kvh_count == prompts == 4 and holders == 2

    def cross(x, i):
        pairs = [(p * holders + h, (p ^ i) * holders + h) for p in range(prompts) for h in range(holders)]
        return lax.ppermute(x, "ctx", pairs)

    chunks, meta = pack(prompt_of, prefix_len, own_queries, capacity, holders, slot_count)
    chunks = chunks[:1] + [cross(x, i) for i, x in enumerate(chunks) if i > 0]
    near = prefix_keys[:, 0], prefix_values[:, 0]
    away = chunks[:0:-1]
    if by_plane:
        half = out_weight.shape[1] // 2
        weights = [out_weight[:, :half], out_weight[:, half:]]
        weights[0] = after(weights[0], *away)
        others = [cross(x, 2) for x in weights]
        shards = [near, near]
        shards[1] = [
            lax.ppermute(x, "ctx", [(c, c ^ 1) for c in range(ctx_count)]) for x in shards[1]
        ]
    else:
        lines = [[p * holders + h for h in range(holders)] for p in range(prompts)]
        joined = jnp.concatenate(near, axis=1)
        joined = lax.all_gather(joined, "ctx", axis=0, tiled=True, axis_index_groups=lines)
        shards = [near] + [(joined, joined)] * (holders - 1)

    state_home = state_away = None
    for shard in range(holders - 1):
        kv = shards[shard]
        state_home = attend(meta, places, chunks[:1], *kv, slot_count, shard, state_home, 0, False)
        state_home, away = lax.optimization_barrier((state_home, away))
        state_away = attend(meta, places, away, *kv, slot_count, shard, state_away, 0, False)
    shard = holders - 1
    far = shards[shard]
    done = [None] * prompts
    for where, members in enumerate([range(prompts - 1, 1, -1), [1]]):
        queries_now = [away[prompts - 1 - i] for i in members]
        block = 0 if where == 0 else prompts - 2
        results = attend(meta, places, queries_now, *far, slot_count, shard, state_away, block, True)
        for i, x in zip(members, results):
            done[i] = cross(x, i)
    (done[0],) = attend(meta, places, chunks[:1], *far, slot_count, shard, state_home, 0, True)
    if by_plane:
        others[0], done[0] = lax.optimization_barrier((others[0], done[0]))
    attended = combine(meta, capacity, own_queries, own_keys, own_values, done)
    rows = attended.reshape(resp_count * tokens_each, width)

    if by_plane:
        projected = project(rows, weights, others, my_prompt, my_holder)
    else:
        weights = lax.all_gather(out_weight, "ctx", axis=1, tiled=True)
        terms = jnp.dot(rows, weights, preferred_element_type=jnp.float32)
        projected = lax.psum_scatter(
            terms.astype(jnp.bfloat16), "kvh", scatter_dimension=1, tiled=True
        )
    return (attended[:, :, None, :], projected)


def solution(mesh):
    in_specs = (
        P("ctx", None, "kvh", None),
        P("ctx", None, "kvh", None),
        P("ctx", None, "kvh", None),
        P("ctx", "kvh", None),
        P("ctx", "kvh", None),
        P(),
        P(),
        P("kvh", "ctx"),
    )
    out_specs = (P("ctx", None, "kvh", None), P("ctx", "kvh"))
    return jax.shard_map(local, mesh=mesh, in_specs=in_specs, out_specs=out_specs, check_vma=False)
```

```python
import functools
import math

import jax
import jax.numpy as jnp
from jax import lax
from jax.experimental import pallas as pl
from jax.experimental.pallas import tpu as pltpu
from jax.sharding import PartitionSpec as P

MASKED = -1e30
LOG2E = math.log2(math.e)
LANES = 128
PART_ROWS = 16
MAX_TILE = 1024
MAX_BLOCK = 512
MIB = 1024 * 1024


def nt_dot(a, b):
    return lax.dot_general(a, b, (((1,), (1,)), ((), ())), preferred_element_type=jnp.float32)


def after(x, *others):
    return lax.optimization_barrier((x, *others))[0]


def pack_kernel(capacity, holders, slots, prompt_ref, len_ref, q_ref, *refs):
    *chunk_refs, meta_ref = refs
    responses, tokens, _ = q_ref.shape
    position = lax.axis_index("ctx")
    mine, holder = position // holders, position % holders
    named = [prompt_ref[position * responses + r] for r in range(responses)]
    ranks = []
    for r in range(responses):
        rank = jnp.int32(0)
        for before in range(r):
            rank += (named[before] == named[r]).astype(jnp.int32)
        ranks.append(rank)
    places = len(chunk_refs) * capacity
    for i, chunk_ref in enumerate(chunk_refs):
        for slot in range(capacity):
            chosen, present = jnp.int32(0), jnp.int32(0)
            for r in range(responses):
                hit = ((named[r] == mine ^ i) & (ranks[r] == slot)).astype(jnp.int32)
                chosen += hit * r
                present += hit
            meta_ref[i * capacity + slot] = chosen
            meta_ref[places + i * capacity + slot] = present
            rows = slice(slot * tokens, (slot + 1) * tokens)
            chunk_ref[rows, :] = q_ref[chosen]

            @pl.when(present == 0)
            def _(chunk_ref=chunk_ref, rows=rows):
                chunk_ref[rows, :] = jnp.zeros_like(chunk_ref[rows, :])

    length = len_ref[mine]
    for j in range(holders):
        place = (holder + j) % holders
        meta_ref[2 * places + j] = jnp.clip(length - place * slots, 0, slots)
        meta_ref[2 * places + holders + j] = place


def pack(prompt_of, prefix_len, q, capacity, holders, slots):
    _, tokens, width = q.shape
    prompts = prefix_len.shape[0]
    smem = pl.BlockSpec(memory_space=pltpu.SMEM)
    vmem = pl.BlockSpec(memory_space=pltpu.VMEM)
    *chunks, meta = pl.pallas_call(
        functools.partial(pack_kernel, capacity, holders, slots),
        out_shape=[jax.ShapeDtypeStruct((capacity * tokens, width), q.dtype)] * prompts
        + [jax.ShapeDtypeStruct((2 * (prompts * capacity + holders),), jnp.int32)],
        in_specs=[smem, smem, vmem],
        out_specs=[vmem] * prompts + [smem],
        compiler_params=pltpu.CompilerParams(vmem_limit_bytes=16 * MIB),
        cost_estimate=pl.CostEstimate(flops=0, bytes_accessed=4 * q.size, transcendentals=0),
        name="pack",
    )(prompt_of, prefix_len, q)
    return chunks, meta


def attend_kernel(count, first, last, shard, places, meta_ref, *refs):
    q_refs, (k_ref, v_ref, *refs) = refs[:count], refs[count:]
    if not first:
        prev_o_ref, prev_lse_ref, *refs = refs
    if last:
        out_refs, refs = refs[:count], refs[count:]
    else:
        o_ref, lse_ref, *refs = refs
    qext, kext, vext, score_a, score_b = refs
    tokens = q_refs[0].shape[0]
    slots, hd = k_ref.shape
    heads = q_refs[0].shape[1] // hd
    scale = LOG2E / math.sqrt(hd)
    tiles, row_block, key_tile = score_a.shape
    per_chunk = heads * tokens // row_block
    live = meta_ref[2 * places + shard]

    @pl.when(live == slots)
    def _():
        for t in range(tiles):
            at = slice(t * key_tile, (t + 1) * key_tile)
            keys = k_ref[at, :]
            kext[at, :hd] = keys
            kext[at, hd:] = keys
            vext[at, :hd] = v_ref[at, :]
            vext[at, hd:] = jnp.ones((key_tile, hd), jnp.bfloat16)

    @pl.when(live != slots)
    def _():
        def prepare(step, carry):
            at = pl.ds(pl.multiple_of(step * key_tile, key_tile), key_tile)
            alive = step * key_tile + lax.broadcasted_iota(jnp.int32, (key_tile, hd), 0) < live
            keys = jnp.where(alive, k_ref[at, :].astype(jnp.float32), k_ref[0:1, :].astype(jnp.float32))
            keys = keys.astype(jnp.bfloat16)
            kext[at, :hd] = keys
            kext[at, hd:] = keys
            vext[at, :hd] = jnp.where(alive, v_ref[at, :].astype(jnp.float32), 0.0).astype(jnp.bfloat16)
            vext[at, hd:] = jnp.where(alive, 1.0, 0.0).astype(jnp.bfloat16)
            return carry

        lax.fori_loop(0, tiles, prepare, 0)

    for c, q_ref in enumerate(q_refs):
        for h in range(heads):
            rows = slice((c * heads + h) * tokens, (c * heads + h + 1) * tokens)
            x = q_ref[:, h * hd : (h + 1) * hd].astype(jnp.float32) * scale
            high = x.astype(jnp.bfloat16)
            qext[rows, :hd] = high
            qext[rows, hd:] = (x - high.astype(jnp.float32)).astype(jnp.bfloat16)

    low = jnp.full((row_block, LANES), MASKED, jnp.float32)

    def rows_of(b):
        if isinstance(b, int):
            return slice(b * row_block, (b + 1) * row_block)
        return pl.ds(pl.multiple_of(b * row_block, row_block), row_block)

    def score_tile(b, t, into, peak):
        s = nt_dot(qext[rows_of(b), :], kext[t * key_tile : (t + 1) * key_tile, :])
        into[t] = s
        for j in range(key_tile // LANES):
            peak = jnp.maximum(peak, s[:, j * LANES : (j + 1) * LANES])
        return peak

    def one_block(b, scores, peak, following, into):
        m = jnp.max(peak, axis=1, keepdims=True)
        peak = low
        acc = jnp.zeros((row_block, 2 * hd), jnp.float32)
        for t in range(tiles):
            if following is not None:
                peak = score_tile(following, t, into, peak)
            w = jnp.exp2(scores[t] - m).astype(jnp.bfloat16)
            acc = acc + jnp.dot(
                w, vext[t * key_tile : (t + 1) * key_tile, :], preferred_element_type=jnp.float32
            )
        total = acc[:, hd:]
        some = total > 0.0
        safe = jnp.where(some, total, 1.0)
        o = acc[:, :hd] / safe
        lse = jnp.where(some, m + jnp.log2(safe), MASKED)
        rows = rows_of(b)
        if not first:
            before = prev_lse_ref[rows, :]
            top = jnp.maximum(before, lse)
            w_before = jnp.exp2(before - top)
            w_now = jnp.exp2(lse - top)
            both = w_before + w_now
            o = (w_before * prev_o_ref[rows, :] + w_now * o) / both
            lse = top + jnp.log2(both)
        if not last:
            o_ref[rows, :] = o
            lse_ref[rows, :] = lse
            return peak
        out_ref = out_refs[b // per_chunk]
        for j in range(row_block // tokens):
            h = (b % per_chunk) * (row_block // tokens) + j
            part = slice(j * tokens, (j + 1) * tokens)
            lanes = slice(h * hd, (h + 1) * hd)
            out_ref[:tokens, lanes] = o[part].astype(jnp.bfloat16)
            flat = lse[part].T[:PART_ROWS, :]
            high = flat.astype(jnp.bfloat16).astype(jnp.float32)
            middle = (flat - high).astype(jnp.bfloat16).astype(jnp.float32)
            row = lax.broadcasted_iota(jnp.int32, flat.shape, 0)
            out_ref[tokens:, lanes] = jnp.where(
                row == 0, high, jnp.where(row == 1, middle, jnp.where(row == 2, flat - high - middle, 0.0))
            ).astype(jnp.bfloat16)
        return peak

    blocks = count * per_chunk
    peak = low
    for t in range(tiles):
        peak = score_tile(0, t, score_a, peak)
    looped = 0
    if not last and per_chunk % 2 == 0 and count > 1:
        looped = blocks - 2

        def pair(i, peak):
            peak = one_block(2 * i, score_a, peak, 2 * i + 1, score_b)
            return one_block(2 * i + 1, score_b, peak, 2 * i + 2, score_a)

        peak = lax.fori_loop(0, looped // 2, pair, peak)
    for b in range(looped, blocks):
        scores, into = (score_a, score_b) if b % 2 == 0 else (score_b, score_a)
        peak = one_block(b, scores, peak, b + 1 if b + 1 < blocks else None, into)


def attend(meta, places, queries, keys, values, slots, shard, state, state_block, last):
    count = len(queries)
    tokens, width = queries[0].shape
    whole = keys.shape[0] > slots
    hd = keys.shape[1] // 2 if whole else keys.shape[1]
    rows = tokens * (width // hd)
    row_block = min(MAX_BLOCK, rows)
    key_tile = min(MAX_TILE, slots)
    holders = meta.shape[0] // 2 - places
    first = state is None

    def fixed(shape):
        return pl.BlockSpec(shape, lambda i, meta_ref: (0, 0))

    def shard_at(column):
        if not whole:
            return pl.BlockSpec((slots, hd), lambda i, meta_ref: (0, 0))
        return pl.BlockSpec(
            (slots, hd), lambda i, meta_ref: (meta_ref[2 * places + holders + shard], column)
        )

    in_specs = [fixed((tokens, width))] * count + [shard_at(0), shard_at(1)]
    operands = [meta, *queries, keys, values]
    if not first:
        in_specs += [pl.BlockSpec((count * rows, hd), lambda i, meta_ref: (state_block, 0))] * 2
        operands += state
    if last:
        out_shape = [jax.ShapeDtypeStruct((tokens + PART_ROWS, width), jnp.bfloat16)] * count
        out_specs = [fixed((tokens + PART_ROWS, width))] * count
    else:
        out_shape = [jax.ShapeDtypeStruct((count * rows, hd), jnp.float32)] * 2
        out_specs = [fixed((count * rows, hd))] * 2
    return pl.pallas_call(
        functools.partial(attend_kernel, count, first, last, shard, places),
        grid_spec=pltpu.PrefetchScalarGridSpec(
            num_scalar_prefetch=1,
            grid=(1,),
            in_specs=in_specs,
            out_specs=out_specs,
            scratch_shapes=[
                pltpu.VMEM((count * rows, 2 * hd), jnp.bfloat16),
                pltpu.VMEM((slots, 2 * hd), jnp.bfloat16),
                pltpu.VMEM((slots, 2 * hd), jnp.bfloat16),
                pltpu.VMEM((slots // key_tile, row_block, key_tile), jnp.float32),
                pltpu.VMEM((slots // key_tile, row_block, key_tile), jnp.float32),
            ],
        ),
        out_shape=out_shape,
        compiler_params=pltpu.CompilerParams(vmem_limit_bytes=40 * MIB),
        cost_estimate=pl.CostEstimate(
            flops=4 * count * rows * slots * hd if first else 0,
            bytes_accessed=0,
            transcendentals=0,
        ),
        name="attend_last" if last else "attend",
    )(*operands)


def combine_kernel(capacity, meta_ref, q_ref, k_ref, v_ref, *refs):
    *part_refs, out_ref, stacked = refs
    _, tokens, hd = k_ref.shape
    width = q_ref.shape[2]
    heads = width // hd
    scale = LOG2E / math.sqrt(hd)
    places = len(part_refs) * capacity
    for i, part_ref in enumerate(part_refs):
        for slot in range(capacity):
            r = meta_ref[i * capacity + slot]

            @pl.when(meta_ref[places + i * capacity + slot] > 0)
            def _(r=r, part_ref=part_ref, slot=slot):
                for h in range(heads):
                    stacked[h * tokens : (h + 1) * tokens, :] = q_ref[r, :, h * hd : (h + 1) * hd]
                s = nt_dot(stacked[...], k_ref[r]) * scale
                row = lax.broadcasted_iota(jnp.int32, s.shape, 0) % tokens
                seen = row >= lax.broadcasted_iota(jnp.int32, s.shape, 1)
                s = jnp.where(seen, s, MASKED)
                m = jnp.max(s, axis=1, keepdims=True)
                w = jnp.where(seen, jnp.exp2(s - m), 0.0)
                total = jnp.sum(w, axis=1, keepdims=True)
                o = jnp.dot(w.astype(jnp.bfloat16), v_ref[r], preferred_element_type=jnp.float32)
                base = part_ref.shape[0] - PART_ROWS
                for h in range(heads):
                    rows = slice(h * tokens, (h + 1) * tokens)
                    lanes = slice(h * hd, (h + 1) * hd)
                    far = part_ref[slot * tokens : (slot + 1) * tokens, lanes].astype(jnp.float32)
                    pieces = part_ref[base:, lanes].astype(jnp.float32)
                    flat = pieces[0:1] + pieces[1:2] + pieces[2:3]
                    lse = jnp.broadcast_to(flat, (hd, hd)).T[slot * tokens : (slot + 1) * tokens, :]
                    top = jnp.maximum(m[rows], lse)
                    own_scale = jnp.exp2(m[rows] - top)
                    far_scale = jnp.exp2(lse - top)
                    out_ref[r, :, lanes] = (
                        (own_scale * o[rows] + far_scale * far) / (own_scale * total[rows] + far_scale)
                    ).astype(jnp.bfloat16)


def combine(meta, capacity, q, keys, values, parts):
    responses, tokens, width = q.shape
    hd = keys.shape[-1]
    heads = width // hd
    return pl.pallas_call(
        functools.partial(combine_kernel, capacity),
        out_shape=jax.ShapeDtypeStruct(q.shape, jnp.bfloat16),
        in_specs=[pl.BlockSpec(memory_space=pltpu.SMEM)]
        + [pl.BlockSpec(memory_space=pltpu.VMEM)] * (3 + len(parts)),
        out_specs=pl.BlockSpec(memory_space=pltpu.VMEM),
        scratch_shapes=[pltpu.VMEM((heads * tokens, hd), jnp.bfloat16)],
        compiler_params=pltpu.CompilerParams(vmem_limit_bytes=24 * MIB),
        cost_estimate=pl.CostEstimate(flops=0, bytes_accessed=0, transcendentals=0),
        name="combine",
    )(meta, q, keys, values, *parts)


def multiply_kernel(kept_first_ref, *refs):
    *row_refs, weight_ref, kept_ref, sent_ref, rows = refs
    count = row_refs[0].shape[0]

    @pl.when(pl.program_id(0) == 0)
    def _():
        for first, order in ((1, (0, 1, 2, 3)), (0, (2, 3, 0, 1))):

            @pl.when(kept_first_ref[0] == first)
            def _(order=order):
                for place, i in enumerate(order):
                    rows[place * count : (place + 1) * count, :] = row_refs[i][...]

    for place, ref in ((1, sent_ref), (0, kept_ref)):
        for part in range(2):
            at = slice(part * count, (part + 1) * count)
            x = rows[2 * place * count + part * count : 2 * place * count + (part + 1) * count, :]
            ref[at, :] = jnp.dot(x, weight_ref[0], preferred_element_type=jnp.float32).astype(ref.dtype)


def multiply(kept_first, row_parts, weights, width, piece):
    count, depth = row_parts[0].shape
    blocks = weights.shape[0]
    rows = pl.BlockSpec((count, depth), lambda j: (0, 0))
    out = pl.BlockSpec((2 * count, width), lambda j: (0, j))
    return pl.pallas_call(
        multiply_kernel,
        grid=(blocks,),
        out_shape=[jax.ShapeDtypeStruct((2 * count, blocks * width), jnp.bfloat16)] * 2,
        in_specs=[pl.BlockSpec(memory_space=pltpu.SMEM)]
        + [rows] * 4
        + [pl.BlockSpec((1, depth, width), lambda j: (j, 0, piece))],
        out_specs=[out] * 2,
        scratch_shapes=[pltpu.VMEM((4 * count, depth), jnp.bfloat16)],
        compiler_params=pltpu.CompilerParams(vmem_limit_bytes=28 * MIB),
        cost_estimate=pl.CostEstimate(flops=0, bytes_accessed=0, transcendentals=0),
        name="multiply",
    )(kept_first.reshape(1), *row_parts, weights)


def arrange_kernel(pieces, flags_ref, *refs):
    *parts, out_ref = refs
    own, direct, back = parts[:pieces], parts[pieces : 2 * pieces], parts[2 * pieces :]
    count, width = back[0].shape
    for holder in range(2):

        @pl.when(flags_ref[1] == holder)
        def _(holder=holder):
            for i in range(pieces):
                here = slice((holder * pieces + i) * width, (holder * pieces + i + 1) * width)
                there = slice(((1 - holder) * pieces + i) * width, ((1 - holder) * pieces + i + 1) * width)
                out_ref[:, there] = back[i][...]

                @pl.when(flags_ref[0] != 0)
                def _(here=here, i=i):
                    out_ref[:, here] = own[i][:count, :]

                @pl.when(flags_ref[0] == 0)
                def _(here=here, i=i):
                    out_ref[:, here] = direct[i][...]


def arrange(same, holder, own, direct, back):
    count, width = back[0].shape
    pieces = len(back)
    vmem = pl.BlockSpec(memory_space=pltpu.VMEM)
    return pl.pallas_call(
        functools.partial(arrange_kernel, pieces),
        out_shape=jax.ShapeDtypeStruct((count, 2 * pieces * width), back[0].dtype),
        in_specs=[pl.BlockSpec(memory_space=pltpu.SMEM)] + [vmem] * (3 * pieces),
        out_specs=vmem,
        compiler_params=pltpu.CompilerParams(vmem_limit_bytes=16 * MIB),
        cost_estimate=pl.CostEstimate(flops=0, bytes_accessed=0, transcendentals=0),
        name="arrange",
    )(jnp.stack([same.astype(jnp.int32), holder.astype(jnp.int32)]), *own, *direct, *back)


def project(rows, weights, others, plane, holder):
    group = lax.axis_index("kvh")
    chip = group // 2
    same = group % 2 == plane % 2
    count = rows.shape[0]
    per_half = 2
    width = weights[0].shape[1] // per_half
    upper = plane >= 2

    def send(x, to, keep=lambda p, k: True):
        pairs = []
        for p in range(4):
            for h in range(2):
                for k in range(4):
                    if keep(p, k):
                        q, g, m = to(p, h, k)
                        pairs.append(((p * 2 + h) * 4 + k, (q * 2 + g) * 4 + m))
        return lax.ppermute(x, ("ctx", "kvh"), pairs)

    def fetch(x):
        near = send(x, lambda p, h, k: (p ^ 1, h, k))
        swapped = send(x, lambda p, h, k: (p, 1 - h, k))
        return x, swapped, near, send(near, lambda p, h, k: (p, 1 - h, k))

    def add(a, b):
        return (a.astype(jnp.float32) + b.astype(jnp.float32)).astype(jnp.bfloat16)

    def chip_sums(product, *wanted):
        kept, sent = product
        got = after(send(sent, lambda p, h, k: (p, h, k ^ 1)), *wanted)
        total = add(kept, got)
        low, high = total[:, :width], total[:, width:]
        return jnp.where(chip == 0, low, high), jnp.where(chip == 0, high, low)

    def over_x(pairs):
        return [send(sent, lambda p, h, k: (p, h, k ^ 2)) for _, sent in pairs]

    def deliver(total):
        direct = send(
            total[:count], lambda p, h, k: (p ^ 1, h, k ^ 1), lambda p, k: k % 2 != p % 2
        )
        back = send(
            total[count:],
            lambda p, h, k: (p, 1 - h, k) if k % 2 == p % 2 else (p ^ 1, 1 - h, k ^ 1),
        )
        return total, direct, back

    fetched = fetch(rows)
    def half_columns(half, other):
        own = weights[half]
        return jnp.stack([jnp.where(upper, other, own), jnp.where(upper, own, other)])

    def product(columns, piece):
        return multiply(same.astype(jnp.int32), fetched, columns, width, piece)

    def finish(pairs, got):
        kept = jnp.concatenate([x for x, _ in pairs], axis=1)
        return deliver(add(kept, jnp.concatenate(got, axis=1)))

    columns = half_columns(0, others[0])
    sums = [chip_sums(product(columns, 0))]
    for piece in range(1, per_half):
        sums.append(chip_sums(product(columns, piece), others[1]))
    got = over_x(sums)
    columns = half_columns(1, after(others[1], got[0], *(x for pair in sums for x in pair)))
    products = [product(columns, i) for i in range(per_half)]
    got[1:] = [after(x, *(sent for _, sent in products)) for x in got[1:]]
    later = [chip_sums(x, got[0]) for x in products]
    delivered = [finish(sums, got), finish(later, over_x(later))]
    return arrange(same, holder, *zip(*delivered))


def local(
    queries, resp_keys, resp_values, prefix_keys, prefix_values, prefix_len, prompt_of, out_weight
):
    ctx_count = lax.axis_size("ctx")
    kvh_count = lax.axis_size("kvh")
    position = lax.axis_index("ctx")
    own_queries = queries[:, :, 0]
    own_keys = resp_keys[:, :, 0]
    own_values = resp_values[:, :, 0]
    resp_count, tokens_each, width = own_queries.shape
    slot_count = prefix_keys.shape[0]
    prompts = prefix_len.shape[0]
    holders = ctx_count // prompts
    my_prompt = position // holders
    my_holder = position % holders
    capacity = max(LANES // tokens_each, resp_count // prompts)
    places = prompts * capacity
    by_plane = kvh_count == prompts == 4 and holders == 2

    def cross(x, i):
        pairs = [(p * holders + h, (p ^ i) * holders + h) for p in range(prompts) for h in range(holders)]
        return lax.ppermute(x, "ctx", pairs)

    chunks, meta = pack(prompt_of, prefix_len, own_queries, capacity, holders, slot_count)
    chunks = chunks[:1] + [cross(x, i) for i, x in enumerate(chunks) if i > 0]
    near = prefix_keys[:, 0], prefix_values[:, 0]
    away = chunks[:0:-1]
    if by_plane:
        half = out_weight.shape[1] // 2
        weights = [out_weight[:, :half], out_weight[:, half:]]
        weights[0] = after(weights[0], *away)
        others = [cross(x, 2) for x in weights]
        shards = [near, near]
        shards[1] = [
            lax.ppermute(x, "ctx", [(c, c ^ 1) for c in range(ctx_count)]) for x in shards[1]
        ]
    else:
        lines = [[p * holders + h for h in range(holders)] for p in range(prompts)]
        joined = jnp.concatenate(near, axis=1)
        joined = lax.all_gather(joined, "ctx", axis=0, tiled=True, axis_index_groups=lines)
        shards = [near] + [(joined, joined)] * (holders - 1)

    state_home = state_away = None
    for shard in range(holders - 1):
        kv = shards[shard]
        state_home = attend(meta, places, chunks[:1], *kv, slot_count, shard, state_home, 0, False)
        state_home, away = lax.optimization_barrier((state_home, away))
        state_away = attend(meta, places, away, *kv, slot_count, shard, state_away, 0, False)
    shard = holders - 1
    far = shards[shard]
    done = [None] * prompts
    for where, members in enumerate([range(prompts - 1, 1, -1), [1]]):
        queries_now = [away[prompts - 1 - i] for i in members]
        block = 0 if where == 0 else prompts - 2
        results = attend(meta, places, queries_now, *far, slot_count, shard, state_away, block, True)
        for i, x in zip(members, results):
            done[i] = cross(x, i)
    (done[0],) = attend(meta, places, chunks[:1], *far, slot_count, shard, state_home, 0, True)
    if by_plane:
        others[0], done[0] = lax.optimization_barrier((others[0], done[0]))
    attended = combine(meta, capacity, own_queries, own_keys, own_values, done)
    rows = attended.reshape(resp_count * tokens_each, width)

    if by_plane:
        projected = project(rows, weights, others, my_prompt, my_holder)
    else:
        weights = lax.all_gather(out_weight, "ctx", axis=1, tiled=True)
        terms = jnp.dot(rows, weights, preferred_element_type=jnp.float32)
        projected = lax.psum_scatter(
            terms.astype(jnp.bfloat16), "kvh", scatter_dimension=1, tiled=True
        )
    return (attended[:, :, None, :], projected)


def solution(mesh):
    in_specs = (
        P("ctx", None, "kvh", None),
        P("ctx", None, "kvh", None),
        P("ctx", None, "kvh", None),
        P("ctx", "kvh", None),
        P("ctx", "kvh", None),
        P(),
        P(),
        P("kvh", "ctx"),
    )
    out_specs = (P("ctx", None, "kvh", None), P("ctx", "kvh"))
    return jax.shard_map(local, mesh=mesh, in_specs=in_specs, out_specs=out_specs, check_vma=False)
```
